32 devices in a mesh: groups: 2 (over x), wide: 16 (over z, y, core).
Axes of the slice: x: 2, y: 2, z: 4, core: 2. Of those that a mesh axis runs over, the one named last changes fastest.
Arguments:
- key_mant: bfloat16 [32768, 128], P(('groups', 'wide')), parts along dimension 0, may hold values from -8 to 8
- scale_exp: int32 [1024], P(('groups', 'wide')), parts along dimension 0, may hold values from -1 to 1
- values: bfloat16 [32768, 128], P(('groups', 'wide')), parts along dimension 0, may hold values from -6 to 6
- queries: bfloat16 [2048, 128], P('groups'), parts along dimension 0, may hold values from -8 to 8
- compact_index: int32 [1024], P('groups'), parts along dimension 0, may hold values from 0 to 15615, as said below
- shard_lengths: int32 [32], P('groups'), parts along dimension 0, may hold values from 256 to 1024, as said below
Outputs:
- key_weights: float32 [1024], P('groups'), parts along dimension 0
- compact_values: float32 [1024, 128], P('groups'), parts along dimension 0
The draws below stay inside these ranges and needn't reach their ends.
There are 2 independent parts, one for each index of `groups`. The reference program is written for one: setup_inputs(seed, part) draws one part's arguments, and reference() takes and returns one part's arrays. A program takes and returns all parts, laid end to end along the dimension named above; each array names one. Nothing has to cross between parts.
Inputs may be any that keep to these rules, and one draw needn't show every extreme that they name: `compact_index`: distinct; each lies among the first 256 positions of its shard of 1024 tokens. `shard_lengths`: some shard is full in every draw.
All inputs are finite; a program needn't handle non-finite values. Where the reference program divides by a largest or mean magnitude, that divisor is 1e-20 or more.
Results may differ from the reference program's by a relative error of at most 0.0003.
Values may be sent and summed in bfloat16 or wider, within the bound.
No kernel may reach another device: no remote copies, remote signals or barrier semaphores. Data moves between devices by JAX's collectives and lax.ppermute only.
A program may use at most 256 MiB of HBM per device.

```python
import jax
import jax.numpy as jnp
from jax import lax

DH = 128
NQ = 1024
CTX_DEV = 1024
M = 512
QB = 32
NNLS_STEPS = 8
NS_ITERS = 9
TOKENS = 16384
SHARDS = 16


def exponent_table(key):
    return jax.random.randint(jax.random.fold_in(key, 11), (TOKENS // QB,), -1, 2).astype(jnp.int32)


def compact_positions(key):
    index_key = jax.random.fold_in(key, 14)
    quarter = CTX_DEV // 4
    pool_size = SHARDS * quarter
    middle = jax.random.permutation(index_key, pool_size - 2)[:M - 2].astype(jnp.int32) + 1
    chosen = jnp.concatenate([jnp.zeros((1,), jnp.int32), middle, jnp.full((1,), pool_size - 1, jnp.int32)])
    return (chosen // quarter * CTX_DEV + chosen % quarter).astype(jnp.int32)


def cluster_directions(key):
    signs = jax.random.randint(jax.random.fold_in(key, 16), (4, DH), 0, 2)
    return (2 * signs - 1).astype(jnp.float32)


def center_scale():
    return (3.5 * DH ** (-0.5)) ** 0.5


def token_clusters(key):
    split_keys = jax.random.split(jax.random.fold_in(key, 17), 3)
    slot = jax.random.randint(split_keys[0], (TOKENS,), 0, 16)
    live_table = jnp.array([0, 0, 0, 0, 0, 0, 0, 0, 1, 1, 1, 1, 1, 2, 2, 2], jnp.int32)
    compact_table = jnp.array([0, 1, 1, 1, 2, 2, 2, 2, 2, 3, 3, 3, 3, 3, 3, 3], jnp.int32)
    live_order = jax.random.permutation(split_keys[1], 4).astype(jnp.int32)
    compact_order = jax.random.permutation(split_keys[2], 4).astype(jnp.int32)
    live_cluster = jnp.take(live_order, jnp.take(live_table, slot))
    compact_cluster = jnp.take(compact_order, jnp.take(compact_table, slot))
    chosen = compact_positions(key)
    is_compact = jnp.zeros((TOKENS,), jnp.int32).at[chosen].set(1)
    return jnp.where(is_compact == 1, compact_cluster, live_cluster)


def draw_scale_exp(key, part):
    return exponent_table(key)


def draw_key_mant(key, part):
    directions = cluster_directions(key)
    clusters = token_clusters(key)
    noise_key = jax.random.fold_in(key, 12)
    gain_key = jax.random.fold_in(key, 19)
    gains = jnp.exp(jax.random.uniform(gain_key, (TOKENS,), jnp.float32, jnp.log(0.4), jnp.log(1.4)))
    centers = center_scale() * jnp.take(directions, clusters, axis=0)
    noise = jnp.clip(jax.random.normal(noise_key, (TOKENS, DH), jnp.float32), -5.0, 5.0)
    sampled = centers + gains[:, None] * noise
    return sampled.astype(jnp.bfloat16)


def draw_queries(key, part):
    directions = cluster_directions(key)
    noise_key = jax.random.fold_in(key, 13)
    cluster_key = jax.random.fold_in(key, 18)
    clusters = jax.random.randint(cluster_key, (NQ,), 0, 4)
    centers = center_scale() * jnp.take(directions, clusters, axis=0)
    sampled = centers + 0.5 * jnp.clip(jax.random.normal(noise_key, (NQ, DH), jnp.float32), -6.0, 6.0)
    return sampled.astype(jnp.bfloat16)


def draw_compact_index(key, part):
    return compact_positions(key)


def draw_shard_lengths(key, part):
    split_keys = jax.random.split(jax.random.fold_in(key, 15), 5)
    base_len = jax.random.randint(split_keys[0], (SHARDS,), CTX_DEV // 4, CTX_DEV // 4 + CTX_DEV // 8 + 1)
    long_len = jax.random.randint(split_keys[1], (SHARDS,), CTX_DEV // 2, CTX_DEV + 1)
    chosen = jax.random.randint(split_keys[2], (SHARDS,), 0, 8) == 0
    lengths = jnp.where(chosen, long_len, base_len)
    full_shard = jax.random.randint(split_keys[3], (), 0, SHARDS)
    short_shard = (full_shard + 1 + jax.random.randint(split_keys[4], (), 0, SHARDS - 1)) % SHARDS
    shard_pos = jnp.arange(SHARDS, dtype=jnp.int32)
    lengths = jnp.where(shard_pos == full_shard, CTX_DEV, lengths)
    lengths = jnp.where(shard_pos == short_shard, CTX_DEV // 4, lengths)
    return lengths.astype(jnp.int32)


def shard_levels(key, dims, cuts, least, largest):
    def one(dim, parts):
        heights = jax.random.uniform(jax.random.fold_in(jax.random.fold_in(key, 6), dim), (parts,), jnp.float32, least / len(cuts), largest / len(cuts))
        return jnp.repeat(jnp.exp(heights), dims[dim] // parts).reshape((-1,) + (1,) * (len(dims) - dim - 1))

    factor_of = one(*cuts[0])
    for cut in cuts[1:]:
        factor_of = factor_of * one(*cut)
    return factor_of


def bell_draw(own_key, shape, spread, bound, shards=(), kind=jnp.bfloat16):
    drawn = spread * jax.random.normal(own_key, shape, jnp.float32)
    if shards:
        drawn = drawn * shard_levels(own_key, shape, shards, -0.22, 0.18)
    return jnp.clip(drawn, -bound, bound).astype(kind)


def setup_inputs(seed: int = 0, part: int = 0) -> dict:
    seeds = jax.random.split(jax.random.key(seed), 7)
    part_keys = jax.random.split(jax.random.fold_in(seeds[6], part), 7)
    return {
        "key_mant": draw_key_mant(jax.random.fold_in(jax.random.fold_in(seeds[6], part), 71), part),
        "scale_exp": draw_scale_exp(jax.random.fold_in(jax.random.fold_in(seeds[6], part), 71), part),
        "values": bell_draw(part_keys[2], (TOKENS, DH), 1.0, 6.0, ((0, 16),)),
        "queries": draw_queries(jax.random.fold_in(jax.random.fold_in(seeds[6], part), 71), part),
        "compact_index": draw_compact_index(jax.random.fold_in(jax.random.fold_in(seeds[6], part), 71), part),
        "shard_lengths": draw_shard_lengths(jax.random.fold_in(jax.random.fold_in(seeds[6], part), 71), part),
    }


ridge_weight = 4.0
nnls_ridge = 0.1
floor_value = -1e30


def dequantize(key_mant, scale_exp):
    factor = jnp.repeat(jnp.exp2(scale_exp.astype(jnp.float32)), QB)
    return (key_mant.astype(jnp.float32) * factor[:, None]).astype(jnp.bfloat16)


def reference(key_mant, scale_exp, values, queries, compact_index, shard_lengths):
    highest = lax.Precision.HIGHEST
    score_scale = DH ** -0.5
    keys = dequantize(key_mant, scale_exp)
    shard_count = TOKENS // CTX_DEV
    key_blocks = keys.reshape(shard_count, CTX_DEV, DH)
    value_blocks = values.reshape(shard_count, CTX_DEV, DH)
    positions = jnp.arange(CTX_DEV, dtype=jnp.int32)

    def block_scores(key_block, length):
        scores = lax.dot_general(queries, key_block, (((1,), (1,)), ((), ())), preferred_element_type=jnp.float32) * score_scale
        return scores, positions < length

    def max_step(state, inputs_pair):
        key_block, length = inputs_pair
        scores, live_mask = block_scores(key_block, length)
        return jnp.maximum(state, jnp.max(jnp.where(live_mask[None, :], scores, floor_value), axis=1)), None

    row_max, unused = lax.scan(max_step, jnp.full((NQ,), floor_value, jnp.float32), (key_blocks, shard_lengths))

    def sum_step(state, inputs_triple):
        row_mass, numerator = state
        key_block, value_block, length = inputs_triple
        scores, live_mask = block_scores(key_block, length)
        attn = jnp.where(live_mask[None, :], jnp.exp(scores - row_max[:, None]), 0.0)
        row_mass = row_mass + jnp.sum(attn, axis=1)
        numerator = numerator + jnp.dot(attn.astype(jnp.bfloat16), value_block, preferred_element_type=jnp.float32)
        return (row_mass, numerator), None

    initial = (jnp.zeros((NQ,), jnp.float32), jnp.zeros((NQ, DH), jnp.float32))
    (row_mass, numerator), unused = lax.scan(sum_step, initial, (key_blocks, value_blocks, shard_lengths))
    outputs = numerator / row_mass[:, None]

    compact_keys = keys[compact_index]
    prior_values = values[compact_index].astype(jnp.float32)
    features = jnp.exp(lax.dot_general(queries, compact_keys, (((1,), (1,)), ((), ())), preferred_element_type=jnp.float32) * score_scale - row_max[:, None])
    live_total = jnp.sum(shard_lengths).astype(jnp.float32)
    target = row_mass * (M / live_total)
    frobenius = jnp.sum(features * features)
    damping = nnls_ridge * (frobenius / M + 1e-6)
    stepsize = 1.0 / (frobenius + damping)
    key_weights = jnp.ones((M,), jnp.float32)
    for number in range(NNLS_STEPS):
        residual = jnp.dot(features, key_weights, precision=highest) - target
        gradient = jnp.dot(features.T, residual, precision=highest) + damping * key_weights
        key_weights = jnp.maximum(key_weights - stepsize * gradient, 0.0)

    attend = features * key_weights[None, :] / target[:, None]
    attend_gram = jnp.dot(attend.T, attend, precision=highest)
    attend_out = jnp.dot(attend.T, outputs, precision=highest)
    ridge = ridge_weight * (jnp.trace(attend_gram) / M + 1e-6)
    identity = jnp.eye(M, dtype=jnp.float32)
    system = attend_gram + ridge * identity
    right_side = attend_out + ridge * prior_values
    inverse = identity / jnp.max(jnp.sum(jnp.abs(system), axis=1))
    for number in range(NS_ITERS):
        inverse = 2.0 * inverse - jnp.dot(jnp.dot(inverse, system, precision=highest), inverse, precision=highest)
    compact_values = jnp.dot(inverse, right_side, precision=highest)
    return key_weights, compact_values
```

```python
import jax
import jax.numpy as jnp
from jax import lax
from jax.experimental import pallas as pl
from jax.experimental.pallas import tpu as pltpu
from jax.sharding import PartitionSpec as P

DH = 128
NQ = 1024
M = 512
QB = 32
SELECT_FROM = 256
NNLS_STEPS = 8
NS_ITERS = 9
STAT_ROWS = 8

ridge_weight = 4.0
nnls_ridge = 0.1
floor_value = -1e30
EXP2_SCALE = DH ** (-0.5) * 1.4426950408889634

f32 = jnp.float32
bf16 = jnp.bfloat16
NN = (((1,), (0,)), ((), ()))
NT = (((1,), (1,)), ((), ()))
TN = (((0,), (0,)), ((), ()))


def params():
    return pltpu.CompilerParams(vmem_limit_bytes=48 * 1024 * 1024)


def vmem(count):
    return [pl.BlockSpec(memory_space=pltpu.VMEM)] * count


def smem(count):
    return [pl.BlockSpec(memory_space=pltpu.SMEM)] * count


def mm(left, right, dims):
    return lax.dot_general(left, right, dims, preferred_element_type=f32)


def split(x):
    high = x.astype(bf16)
    return high, (x - high.astype(f32)).astype(bf16)


def mm3(left, right, dims):
    return mm(left[0], right[0], dims) + (mm(left[0], right[1], dims) + mm(left[1], right[0], dims))


def stat_tile(row_max, row_mass):
    row = lax.broadcasted_iota(jnp.int32, (STAT_ROWS, row_max.shape[1]), 0)
    return jnp.where(row == 0, row_max, jnp.where(row == 1, row_mass, 0.0))


def attention_kernel(
    len_ref, exp_ref, index_ref, mant_ref, value_ref, query_ref,
    send_ref, keep_ref, send_rows_ref, keep_rows_ref, key_ref,
):
    ctx = mant_ref.shape[0]
    me = lax.axis_index("wide")
    core = lax.rem(me, 2)
    own_len = len_ref[me]
    for b in range(ctx // QB):
        exponent = exp_ref[b]
        factor = jnp.where(exponent > 0, 2.0, jnp.where(exponent < 0, 0.5, 1.0)).astype(f32)
        rows = pl.ds(b * QB, QB)
        key_ref[rows, :] = (mant_ref[rows, :].astype(f32) * factor).astype(bf16)
    half_m = M // 2
    position = lax.broadcasted_iota(jnp.int32, (SELECT_FROM, half_m), 0)
    for half, out in ((1 - core, send_rows_ref), (core, keep_rows_ref)):
        columns = pl.ds(pl.multiple_of(half * half_m, half_m), half_m)
        wanted = index_ref[:, columns] - me * ctx
        chosen = jnp.where(position == wanted, 1.0, 0.0).astype(bf16)
        out[:, :DH] = mm(chosen, key_ref[:SELECT_FROM, :], TN).astype(bf16)
        out[:, DH:] = mm(chosen, value_ref[:SELECT_FROM, :], TN).astype(bf16)
    chunk = 256
    half_q = NQ // 2
    dead = lax.broadcasted_iota(jnp.int32, (ctx, chunk), 0) >= own_len
    for half, out in ((1 - core, send_ref), (core, keep_ref)):
        for c in range(half_q // chunk):
            begin = pl.multiple_of(half * half_q + c * chunk, chunk)
            scores = mm(key_ref[...], query_ref[pl.ds(begin, chunk), :], NT)
            scores = jnp.where(dead, floor_value, scores)
            row_max = jnp.max(scores, axis=0, keepdims=True)
            attn = jnp.exp2((scores - row_max) * EXP2_SCALE)
            row_mass = jnp.sum(attn, axis=0, keepdims=True)
            out[:DH, pl.ds(c * chunk, chunk)] = mm(value_ref[...], attn.astype(bf16), TN)
            out[DH:, pl.ds(c * chunk, chunk)] = stat_tile(row_max, row_mass)


def joined(first, second):
    max_first, max_second = first[DH : DH + 1], second[DH : DH + 1]
    joint = jnp.maximum(max_first, max_second)
    scale_first = jnp.exp2((max_first - joint) * EXP2_SCALE)
    scale_second = jnp.exp2((max_second - joint) * EXP2_SCALE)
    mass = first[DH + 1 : DH + 2] * scale_first + second[DH + 1 : DH + 2] * scale_second
    return first[:DH] * scale_first + second[:DH] * scale_second, stat_tile(joint, mass)


def halve_kernel(first_ref, second_ref, first_rows_ref, second_rows_ref,
                 send_ref, keep_ref, send_rows_ref, keep_rows_ref):
    me = lax.axis_index("wide")
    bit = lax.rem(lax.div(me, 2), 2)
    width = send_ref.shape[1]
    height = send_rows_ref.shape[0]
    for half, out, out_rows in ((1 - bit, send_ref, send_rows_ref), (bit, keep_ref, keep_rows_ref)):
        columns = pl.ds(pl.multiple_of(half * width, width), width)
        numer, stats = joined(first_ref[:, columns], second_ref[:, columns])
        out[:DH, :] = numer
        out[DH:, :] = stats
        rows = pl.ds(pl.multiple_of(half * height, height), height)
        out_rows[...] = first_rows_ref[rows, :] + second_rows_ref[rows, :]


def join_kernel(first_ref, second_ref, first_rows_ref, second_rows_ref, out_ref, out_rows_ref):
    numer, stats = joined(first_ref[...], second_ref[...])
    out_ref[:DH, :] = numer
    out_ref[DH:, :] = stats
    out_rows_ref[...] = first_rows_ref[...] + second_rows_ref[...]


def refit_kernel(
    len_ref, query_ref, part0, part1, part2, part3, rows0, rows1, rows2, rows3,
    weight_out, value_out,
    key_ref, prior_ref, feat_hi, feat_lo, scaled_hi, scaled_lo, out_hi, out_lo,
    gram_hi, gram_lo, power_ref, refit_ref,
):
    me = lax.axis_index("wide")
    core = lax.rem(me, 2)
    bit = lax.rem(lax.div(me, 2), 2)
    total = len_ref[0]
    for i in range(1, len_ref.shape[0]):
        total = total + len_ref[i]
    live_total = jnp.full((1, 1), total, jnp.int32).astype(f32)
    places = ((core, bit), (core, 1 - bit), (1 - core, bit), (1 - core, 1 - bit))
    parts = (part0, part1, part2, part3)
    quarter = NQ // 4
    quarter_m = M // 4
    for (hi_bit, lo_bit), rows_ref in zip(places, (rows0, rows1, rows2, rows3)):
        rows = pl.ds(pl.multiple_of((hi_bit * 2 + lo_bit) * quarter_m, quarter_m), quarter_m)
        key_ref[rows, :] = rows_ref[:, :DH]
        prior_ref[rows, :] = rows_ref[:, DH:].astype(f32)
    frobenius = jnp.zeros((1, 1), f32)
    linear = jnp.zeros((16, M), f32)
    for p, ((hi_bit, lo_bit), part) in enumerate(zip(places, parts)):
        begin = pl.multiple_of((hi_bit * 2 + lo_bit) * quarter, quarter)
        columns = pl.ds(p * quarter, quarter)
        row_max, row_mass = part[DH : DH + 1, :], part[DH + 1 : DH + 2, :]
        scores = mm(key_ref[...], query_ref[pl.ds(begin, quarter), :], NT)
        features = jnp.exp2((scores - row_max) * EXP2_SCALE)
        target = row_mass * (M / live_total)
        high, low = split(features)
        feat_hi[:, columns] = high
        feat_lo[:, columns] = low
        frobenius = frobenius + jnp.sum(
            jnp.sum(features * features, axis=0, keepdims=True), axis=1, keepdims=True
        )
        target_pair = split(jnp.broadcast_to(target, (16, quarter)))
        linear = linear + mm3(target_pair, (high, low), NT)
        high, low = split(features * (1.0 / target))
        scaled_hi[:, columns] = high
        scaled_lo[:, columns] = low
        high, low = split(part[:DH, :] / row_mass)
        out_hi[:, columns] = high
        out_lo[:, columns] = low
    feat = (feat_hi[...], feat_lo[...])
    high, low = split(mm3(feat, feat, NT))
    gram_hi[...] = high
    gram_lo[...] = low
    damping = nnls_ridge * (frobenius / M + 1e-6)
    stepsize = 1.0 / (frobenius + damping)

    def nnls_step(number, weights):
        gradient = mm3(split(weights), (gram_hi[...], gram_lo[...]), NN) - linear + damping * weights
        return jnp.maximum(weights - stepsize * gradient, 0.0)

    weights = lax.fori_loop(0, NNLS_STEPS, nnls_step, jnp.ones((16, M), f32))
    weight_row = weights[:1]
    weight_out[...] = weight_row
    weight_column = jnp.broadcast_to(weight_row, (DH, M)).T
    scaled = (scaled_hi[...], scaled_lo[...])
    gram = mm3(scaled, scaled, NT) * weight_row
    gram = gram * jnp.concatenate([weight_column] * (M // DH), axis=1)
    diagonal = lax.broadcasted_iota(jnp.int32, (M, M), 0) == lax.broadcasted_iota(
        jnp.int32, (M, M), 1
    )
    trace = jnp.sum(
        jnp.sum(jnp.where(diagonal, gram, 0.0), axis=0, keepdims=True), axis=1, keepdims=True
    )
    ridge = ridge_weight * (trace / M + 1e-6)
    system = gram + jnp.where(diagonal, ridge, 0.0)
    right_side = weight_column * mm3(scaled, (out_hi[...], out_lo[...]), NT)
    right_side = right_side + ridge * prior_ref[...]
    bound = jnp.max(jnp.sum(jnp.abs(system), axis=0, keepdims=True), axis=1, keepdims=True)
    power_ref[...] = system / bound
    refit_ref[...] = right_side / bound

    def newton_step(number, carry):
        power = power_ref[...]
        refit = refit_ref[...]
        pair = split(power)
        refit_ref[...] = 2.0 * refit - mm3(pair, split(refit), NN)
        power_ref[...] = 2.0 * power - mm3(pair, pair, NN)
        return carry

    lax.fori_loop(0, NS_ITERS - 1, newton_step, 0)
    refit = refit_ref[...]
    value_out[...] = 2.0 * refit - mm3(split(power_ref[...]), split(refit), NN)


def shape(rows, columns, dtype):
    return jax.ShapeDtypeStruct((rows, columns), dtype)


def per_device(key_mant, scale_exp, values, queries, compact_index, shard_lengths):
    wide_count = lax.axis_size("wide")
    ctx = key_mant.shape[0]
    rows_num = DH + STAT_ROWS

    def exchanged(arrays, mask):
        pairs = [(i, i ^ mask) for i in range(wide_count)]
        return tuple(lax.ppermute(array, "wide", pairs) for array in arrays)

    send, keep, send_rows, keep_rows = pl.pallas_call(
        attention_kernel,
        out_shape=(shape(rows_num, NQ // 2, f32),) * 2 + (shape(M // 2, 2 * DH, bf16),) * 2,
        in_specs=smem(2) + vmem(4),
        out_specs=tuple(vmem(4)),
        scratch_shapes=[pltpu.VMEM((ctx, DH), bf16)],
        compiler_params=params(),
    )(shard_lengths, scale_exp, compact_index.reshape(1, M), key_mant, values, queries)
    got, got_rows = exchanged((send, send_rows), 1)
    send, keep, send_rows, keep_rows = pl.pallas_call(
        halve_kernel,
        out_shape=(shape(rows_num, NQ // 4, f32),) * 2 + (shape(M // 4, 2 * DH, bf16),) * 2,
        in_specs=vmem(4),
        out_specs=tuple(vmem(4)),
        compiler_params=params(),
    )(keep, got, keep_rows, got_rows)
    got, got_rows = exchanged((send, send_rows), 2)
    mask = 4
    while True:
        keep, keep_rows = pl.pallas_call(
            join_kernel,
            out_shape=(shape(rows_num, NQ // 4, f32), shape(M // 4, 2 * DH, bf16)),
            in_specs=vmem(4),
            out_specs=tuple(vmem(2)),
            compiler_params=params(),
        )(keep, got, keep_rows, got_rows)
        if mask >= wide_count:
            break
        got, got_rows = exchanged((keep, keep_rows), mask)
        mask *= 2
    side, side_rows = exchanged((keep, keep_rows), 2)
    core, core_rows, both, both_rows = exchanged((keep, keep_rows, side, side_rows), 1)
    weights, compact_values = pl.pallas_call(
        refit_kernel,
        out_shape=(shape(1, M, f32), shape(M, DH, f32)),
        in_specs=smem(1) + vmem(9),
        out_specs=tuple(vmem(2)),
        scratch_shapes=[
            pltpu.VMEM((M, DH), bf16),
            pltpu.VMEM((M, DH), f32),
            pltpu.VMEM((M, NQ), bf16),
            pltpu.VMEM((M, NQ), bf16),
            pltpu.VMEM((M, NQ), bf16),
            pltpu.VMEM((M, NQ), bf16),
            pltpu.VMEM((DH, NQ), bf16),
            pltpu.VMEM((DH, NQ), bf16),
            pltpu.VMEM((M, M), bf16),
            pltpu.VMEM((M, M), bf16),
            pltpu.VMEM((M, M), f32),
            pltpu.VMEM((M, DH), f32),
        ],
        compiler_params=params(),
    )(shard_lengths, queries, keep, side, core, both, keep_rows, side_rows, core_rows, both_rows)
    return weights.reshape(M), compact_values


def solution(mesh):
    placed = (
        P(("groups", "wide"), None),
        P(("groups", "wide")),
        P(("groups", "wide"), None),
        P("groups", None),
        P("groups"),
        P("groups"),
    )
    return jax.shard_map(
        per_device,
        mesh=mesh,
        in_specs=placed,
        out_specs=(P("groups"), P("groups", None)),
        check_vma=False,
    )
```

```python
import jax
import jax.numpy as jnp
from jax import lax
from jax.experimental import pallas as pl
from jax.experimental.pallas import tpu as pltpu
from jax.sharding import PartitionSpec as P

DH = 128
NQ = 1024
M = 512
QB = 32
SELECT_FROM = 256
NNLS_STEPS = 8
NS_ITERS = 9
CHUNKS = 4
CHUNK = NQ // CHUNKS
QUARTER_M = M // CHUNKS
SUM_ROWS = 2 * DH + QUARTER_M // 2

ridge_weight = 4.0
nnls_ridge = 0.1
floor_value = -1e30
EXP2_SCALE = DH ** (-0.5) * 1.4426950408889634

f32 = jnp.float32
bf16 = jnp.bfloat16
NN = (((1,), (0,)), ((), ()))
NT = (((1,), (1,)), ((), ()))
TN = (((0,), (0,)), ((), ()))


def mm(left, right, dims):
    return lax.dot_general(left, right, dims, preferred_element_type=f32)


def split(x):
    high = x.astype(bf16)
    return high, (x - high.astype(f32)).astype(bf16)


def mm3(left, right, dims):
    return mm(left[0], right[0], dims) + (mm(left[0], right[1], dims) + mm(left[1], right[0], dims))


def total_of(x):
    return jnp.sum(jnp.sum(x, axis=0, keepdims=True), axis=1, keepdims=True)


def place(number, size):
    return pl.ds(pl.multiple_of(number * size, size), size)


def bits():
    me = lax.axis_index("wide")
    return me, lax.rem(me, 2), lax.rem(lax.div(me, 2), 2)


def put_sums(out_ref, columns, sums):
    high, low = split(sums)
    out_ref[:DH, columns] = high
    out_ref[DH : 2 * DH, columns] = low


def get_sums(ref, columns):
    return ref[:DH, columns].astype(f32) + ref[DH : 2 * DH, columns].astype(f32)


def attention_kernel(
    len_hbm, exp_hbm, index_hbm, mant_hbm, value_hbm, query_hbm,
    stat_ref, send_key_ref, keep_key_ref, send_ref, keep_ref,
    len_ref, exp_ref, index_ref, mant_ref, value_ref, query_ref, key_ref, sems,
):
    copies = [
        pltpu.make_async_copy(source, target, sems.at[i])
        for i, (source, target) in enumerate(
            (
                (exp_hbm, exp_ref),
                (mant_hbm, mant_ref),
                (query_hbm, query_ref),
                (len_hbm, len_ref),
                (index_hbm, index_ref),
                (value_hbm, value_ref),
            )
        )
    ]
    for copy in copies:
        copy.start()
    ctx = mant_ref.shape[0]
    me, core, bit = bits()
    for copy in copies:
        copy.wait()
    own_len = len_ref[me]
    for b in range(ctx // QB):
        exponent = exp_ref[b]
        factor = jnp.where(exponent > 0, 2.0, jnp.where(exponent < 0, 0.5, 1.0)).astype(f32)
        rows = pl.ds(b * QB, QB)
        key_ref[rows, :] = (mant_ref[rows, :].astype(f32) * factor).astype(bf16)
    half_m = M // 2
    position = lax.broadcasted_iota(jnp.int32, (SELECT_FROM, half_m), 0)
    for half, key_out, out in ((1 - core, send_key_ref, send_ref), (core, keep_key_ref, keep_ref)):
        wanted = index_ref[:, place(half, half_m)] - me * ctx
        chosen = jnp.where(position == wanted, 1.0, 0.0).astype(bf16)
        key_out[...] = mm(chosen, key_ref[:SELECT_FROM, :], TN).astype(bf16)
        prior = mm(value_ref[:SELECT_FROM, :], chosen, TN).astype(bf16)
        for piece in range(2):
            for part in range(2):
                begin = piece * CHUNK + part * QUARTER_M
                out[2 * DH :, begin : begin + QUARTER_M] = prior[
                    part * (DH // 2) : (part + 1) * (DH // 2), piece * QUARTER_M : (piece + 1) * QUARTER_M
                ]
    dead = lax.broadcasted_iota(jnp.int32, (ctx, CHUNK), 0) >= own_len
    for half, out in ((1 - core, send_ref), (core, keep_ref)):
        for c in range(2):
            number = half * 2 + c
            scores = mm(key_ref[...], query_ref[place(number, CHUNK), :], NT)
            scores = jnp.where(dead, floor_value, scores)
            row_max = jnp.max(scores, axis=0, keepdims=True)
            attn = jnp.exp2((scores - row_max) * EXP2_SCALE)
            stat_ref[pl.ds(number, 1), :] = row_max
            stat_ref[pl.ds(CHUNKS + number, 1), :] = jnp.sum(attn, axis=0, keepdims=True)
            sums = mm(value_ref[...], attn.astype(bf16), TN)
            put_sums(out, pl.ds(c * CHUNK, CHUNK), sums)


def joined_stats(first_ref, second_ref, out_ref, scale_ref):
    max_first, max_second = first_ref[:CHUNKS, :], second_ref[:CHUNKS, :]
    joint = jnp.maximum(max_first, max_second)
    scale_first = jnp.exp2((max_first - joint) * EXP2_SCALE)
    scale_second = jnp.exp2((max_second - joint) * EXP2_SCALE)
    out_ref[:CHUNKS, :] = joint
    out_ref[CHUNKS:, :] = first_ref[CHUNKS:, :] * scale_first + second_ref[CHUNKS:, :] * scale_second
    scale_ref[...] = scale_first


def core_kernel(stat_a, stat_b, key_a, key_b, send_in, keep_in,
                stat_out, key_out, send_out, keep_out, scale_ref):
    me, core, bit = bits()
    joined_stats(stat_a, stat_b, stat_out, scale_ref)
    key_out[...] = key_a[...] + key_b[...]
    for half, source, out in ((1 - core, send_in, send_out), (core, keep_in, keep_out)):
        for c in range(2):
            columns = pl.ds(c * CHUNK, CHUNK)
            factor = scale_ref[pl.ds(half * 2 + c, 1), :]
            put_sums(out, columns, get_sums(source, columns) * factor)
        out[2 * DH :, :] = source[2 * DH :, :]


def halve_kernel(stat_a, stat_b, key_a, key_b, sum_a, sum_b,
                 stat_out, key_out, send_out, keep_out, scale_ref):
    me, core, bit = bits()
    joined_stats(stat_a, stat_b, stat_out, scale_ref)
    key_out[...] = key_a[...] + key_b[...]
    everything = pl.ds(0, CHUNK)
    for half, out in ((1 - bit, send_out), (bit, keep_out)):
        columns = place(half, CHUNK)
        factor = scale_ref[pl.ds(core * 2 + half, 1), :]
        put_sums(out, everything, (get_sums(sum_a, columns) + get_sums(sum_b, columns)) * factor)
        out[2 * DH :, :] = sum_a[2 * DH :, columns] + sum_b[2 * DH :, columns]


def join_kernel(stat_a, stat_b, key_a, key_b, sum_a, sum_b, stat_out, key_out, sum_out, scale_ref):
    me, core, bit = bits()
    joined_stats(stat_a, stat_b, stat_out, scale_ref)
    key_out[...] = key_a[...] + key_b[...]
    everything = pl.ds(0, CHUNK)
    factor = scale_ref[pl.ds(core * 2 + bit, 1), :]
    put_sums(sum_out, everything, (get_sums(sum_a, everything) + get_sums(sum_b, everything)) * factor)
    sum_out[2 * DH :, :] = sum_a[2 * DH :, :] + sum_b[2 * DH :, :]


def outputs_kernel(stat_ref, sum_a, sum_b, after_ref, out_ref):
    me, core, bit = bits()
    everything = pl.ds(0, CHUNK)
    row_mass = stat_ref[pl.ds(CHUNKS + core * 2 + bit, 1), :]
    put_sums(out_ref, everything, (get_sums(sum_a, everything) + get_sums(sum_b, everything)) / row_mass)
    out_ref[2 * DH :, :] = sum_a[2 * DH :, :] + sum_b[2 * DH :, :]


def feature_kernel(
    len_ref, query_ref, stat_ref, own_key_ref, other_key_ref,
    gram_hi, gram_lo, linear_ref, norm_ref, scaled_hi, scaled_lo,
    key_ref, feat_hi, feat_lo,
):
    me, core, bit = bits()
    total = len_ref[0]
    for i in range(1, len_ref.shape[0]):
        total = total + len_ref[i]
    live_total = jnp.full((1, 1), total, jnp.int32).astype(f32)
    key_ref[place(core, M // 2), :] = own_key_ref[...]
    key_ref[place(1 - core, M // 2), :] = other_key_ref[...]
    frobenius = jnp.zeros((1, 1), f32)
    linear = jnp.zeros((16, M), f32)
    for c in range(CHUNKS):
        columns = pl.ds(c * CHUNK, CHUNK)
        row_max, row_mass = stat_ref[c : c + 1, :], stat_ref[CHUNKS + c : CHUNKS + c + 1, :]
        scores = mm(key_ref[...], query_ref[columns, :], NT)
        features = jnp.exp2((scores - row_max) * EXP2_SCALE)
        target = row_mass * (M / live_total)
        high, low = split(features)
        feat_hi[:, columns] = high
        feat_lo[:, columns] = low
        frobenius = frobenius + total_of(features * features)
        linear = linear + mm3(split(jnp.broadcast_to(target, (16, CHUNK))), (high, low), NT)
        high, low = split(features * (1.0 / target))
        scaled_hi[:, columns] = high
        scaled_lo[:, columns] = low
    feat = (feat_hi[...], feat_lo[...])
    high, low = split(mm3(feat, feat, NT))
    gram_hi[...] = high
    gram_lo[...] = low
    linear_ref[...] = linear
    norm_ref[...] = jnp.broadcast_to(frobenius, norm_ref.shape)


def weight_kernel(
    gram_hi, gram_lo, linear_ref, norm_ref, scaled_hi, scaled_lo,
    weight_out, factor_out, power_out, attend_ref,
):
    linear = linear_ref[...]
    frobenius = norm_ref[:1, :1]
    damping = nnls_ridge * (frobenius / M + 1e-6)
    stepsize = 1.0 / (frobenius + damping)
    weights = jnp.ones((16, M), f32)
    for number in range(NNLS_STEPS):
        gradient = mm3(split(weights), (gram_hi[...], gram_lo[...]), NN) - linear + damping * weights
        weights = jnp.maximum(weights - stepsize * gradient, 0.0)
        if number % 2 == 0 and number // 2 < CHUNKS:
            columns = pl.ds(number // 2 * CHUNK, CHUNK)
            scaled = (scaled_hi[:, columns], scaled_lo[:, columns])
            part = mm3(scaled, scaled, NT)
            attend_ref[...] = part if number == 0 else attend_ref[...] + part
    weight_row = weights[:1]
    weight_out[...] = weight_row
    weight_column = jnp.broadcast_to(weight_row, (DH, M)).T
    gram = attend_ref[...] * weight_row
    gram = gram * jnp.concatenate([weight_column] * (M // DH), axis=1)
    diagonal = lax.broadcasted_iota(jnp.int32, (M, M), 0) == lax.broadcasted_iota(
        jnp.int32, (M, M), 1
    )
    ridge = ridge_weight * (total_of(jnp.where(diagonal, gram, 0.0)) / M + 1e-6)
    system = gram + jnp.where(diagonal, ridge, 0.0)
    bound = jnp.max(jnp.sum(jnp.abs(system), axis=0, keepdims=True), axis=1, keepdims=True)
    row = lax.broadcasted_iota(jnp.int32, factor_out.shape, 0)
    factor_out[...] = jnp.where(row == 0, ridge, bound)
    power_out[...] = system * (1.0 / bound)


def forward_kernel(sum_ref, after_ref, out_ref):
    out_ref[...] = sum_ref[...]


def refit_kernel(
    power_in, weight_ref, factor_ref, scaled_hi, scaled_lo, part0, part1, part2, part3,
    value_out, both_ref, left_ref, right_ref, prior_ref,
):
    me, core, bit = bits()
    places = ((core, bit), (core, 1 - bit), (1 - core, bit), (1 - core, 1 - bit))
    product = jnp.zeros((DH, M), f32)
    for (hi_bit, lo_bit), part in zip(places, (part0, part1, part2, part3)):
        number = hi_bit * 2 + lo_bit
        columns = place(number, CHUNK)
        lanes = place(number, QUARTER_M)
        prior_ref[: DH // 2, lanes] = part[2 * DH :, :QUARTER_M].astype(f32)
        prior_ref[DH // 2 :, lanes] = part[2 * DH :, QUARTER_M:].astype(f32)
        high = mm(part[: 2 * DH, :], scaled_hi[:, columns], NT)
        product = product + (high[:DH] + high[DH:] + mm(part[:DH, :], scaled_lo[:, columns], NT))
    ridge, bound = factor_ref[0:1, :1], factor_ref[1:2, :1]
    both_ref[:M, :] = power_in[...]
    both_ref[M:, :] = (weight_ref[...] * product + ridge * prior_ref[...]) * (1.0 / bound)

    def newton_step(number, carry):
        both = both_ref[...]
        high, low = split(both)
        both_ref[...] = 2.0 * both - mm3((high, low), (high[:M], low[:M]), NN)
        return carry

    lax.fori_loop(0, NS_ITERS - 1, newton_step, 0)
    refit = both_ref[M:, :]
    refit = 2.0 * refit - mm3(split(refit), split(both_ref[:M, :]), NN)
    value_out[...] = refit.T


def shape(rows, columns, dtype):
    return jax.ShapeDtypeStruct((rows, columns), dtype)


def call(kernel, outs, arrays, scalars=0, scratch=(), in_specs=None, flops=None, limit=48):
    return pl.pallas_call(
        kernel,
        out_shape=tuple(outs),
        in_specs=in_specs
        or [pl.BlockSpec(memory_space=pltpu.SMEM)] * scalars
        + [pl.BlockSpec(memory_space=pltpu.VMEM)] * (len(arrays) - scalars),
        out_specs=tuple([pl.BlockSpec(memory_space=pltpu.VMEM)] * len(outs)),
        scratch_shapes=list(scratch),
        compiler_params=pltpu.CompilerParams(vmem_limit_bytes=limit * 1024 * 1024),
        cost_estimate=None
        if flops is None
        else pl.CostEstimate(flops=flops, bytes_accessed=1024, transcendentals=0),
    )(*arrays)


def per_device(key_mant, scale_exp, values, queries, compact_index, shard_lengths):
    wide_count = lax.axis_size("wide")
    ctx = key_mant.shape[0]

    def exchanged(array, mask):
        return lax.ppermute(array, "wide", [(i, i ^ mask) for i in range(wide_count)])

    stat_shape = shape(2 * CHUNKS, CHUNK, f32)
    key_shape = shape(M // 2, DH, bf16)
    half_sum = shape(SUM_ROWS, 2 * CHUNK, bf16)
    quarter_sum = shape(SUM_ROWS, CHUNK, bf16)
    factors = [pltpu.VMEM((CHUNKS, CHUNK), f32)]

    stats, send_keys, keys, send, keep = call(
        attention_kernel,
        (stat_shape, key_shape, key_shape, half_sum, half_sum),
        (shard_lengths, scale_exp, compact_index.reshape(1, M), key_mant, values, queries),
        in_specs=[pl.BlockSpec(memory_space=pltpu.HBM)] * 6,
        flops=10**9,
        limit=48,
        scratch=[
            pltpu.SMEM(shard_lengths.shape, jnp.int32),
            pltpu.SMEM(scale_exp.shape, jnp.int32),
            pltpu.VMEM((1, M), jnp.int32),
            pltpu.VMEM((ctx, DH), bf16),
            pltpu.VMEM((ctx, DH), bf16),
            pltpu.VMEM((NQ, DH), bf16),
            pltpu.VMEM((ctx, DH), bf16),
            pltpu.SemaphoreType.DMA((6,)),
        ],
    )
    stats, keys, send, keep = call(
        core_kernel,
        (stat_shape, key_shape, half_sum, half_sum),
        (stats, exchanged(stats, 1), keys, exchanged(send_keys, 1), send, keep),
        scratch=factors,
    )
    stats, keys, send, keep = call(
        halve_kernel,
        (stat_shape, key_shape, quarter_sum, quarter_sum),
        (stats, exchanged(stats, 2), keys, exchanged(keys, 2), keep, exchanged(send, 1)),
        scratch=factors,
    )
    sums, got = keep, exchanged(send, 2)
    mask = 4
    while mask < wide_count:
        stats, keys, sums = call(
            join_kernel,
            (stat_shape, key_shape, quarter_sum),
            (stats, exchanged(stats, mask), keys, exchanged(keys, mask), sums, got),
            scratch=factors,
        )
        got = exchanged(sums, mask)
        mask *= 2
    gram_hi, gram_lo, linear, norm, scaled_hi, scaled_lo = call(
        feature_kernel,
        (shape(M, M, bf16),) * 2 + (shape(16, M, f32), shape(8, DH, f32)) + (shape(M, NQ, bf16),) * 2,
        (shard_lengths, queries, stats, keys, exchanged(keys, 1)),
        scalars=1,
        flops=4 * 10**9,
        scratch=[pltpu.VMEM((M, DH), bf16), pltpu.VMEM((M, NQ), bf16), pltpu.VMEM((M, NQ), bf16)],
    )
    (outputs,) = call(outputs_kernel, (quarter_sum,), (stats, sums, got, norm))
    side = exchanged(outputs, 2)
    core = exchanged(outputs, 1)
    weights, factor, power = call(
        weight_kernel,
        (shape(1, M, f32), shape(8, DH, f32), shape(M, M, f32)),
        (gram_hi, gram_lo, linear, norm, scaled_hi, scaled_lo),
        flops=5 * 10**9,
        scratch=[pltpu.VMEM((M, M), f32)],
    )
    (side,) = call(forward_kernel, (quarter_sum,), (side, factor))
    (compact_values,) = call(
        refit_kernel,
        (shape(M, DH, f32),),
        (power, weights, factor, scaled_hi, scaled_lo, outputs, side, core, exchanged(side, 1)),
        scratch=[
            pltpu.VMEM((M + DH, M), f32),
            pltpu.VMEM((M + DH, 3 * M), bf16),
            pltpu.VMEM((3 * M, M), bf16),
            pltpu.VMEM((DH, M), f32),
        ],
    )
    return weights.reshape(M), compact_values


def solution(mesh):
    placed = (
        P(("groups", "wide"), None),
        P(("groups", "wide")),
        P(("groups", "wide"), None),
        P("groups", None),
        P("groups"),
        P("groups"),
    )
    return jax.shard_map(
        per_device,
        mesh=mesh,
        in_specs=placed,
        out_specs=(P("groups"), P("groups", None)),
        check_vma=False,
    )
```

```python
import jax
import jax.numpy as jnp
from jax import lax
from jax.experimental import pallas as pl
from jax.experimental.pallas import tpu as pltpu
from jax.sharding import PartitionSpec as P

DH = 128
NQ = 1024
M = 512
QB = 32
SELECT_FROM = 256
NNLS_STEPS = 8
NS_ITERS = 9
CHUNKS = 4
CHUNK = NQ // CHUNKS
QUARTER_M = M // CHUNKS
SUM_ROWS = DH + QUARTER_M // 2

ridge_weight = 4.0
nnls_ridge = 0.1
floor_value = -1e30
EXP2_SCALE = DH ** (-0.5) * 1.4426950408889634

f32 = jnp.float32
bf16 = jnp.bfloat16
NN = (((1,), (0,)), ((), ()))
NT = (((1,), (1,)), ((), ()))
TN = (((0,), (0,)), ((), ()))


def mm(left, right, dims):
    return lax.dot_general(left, right, dims, preferred_element_type=f32)


def split(x):
    high = x.astype(bf16)
    return high, (x - high.astype(f32)).astype(bf16)


def mm3(left, right, dims):
    return mm(left[0], right[0], dims) + (mm(left[0], right[1], dims) + mm(left[1], right[0], dims))


def total_of(x):
    return jnp.sum(jnp.sum(x, axis=0, keepdims=True), axis=1, keepdims=True)


def place(number, size):
    return pl.ds(pl.multiple_of(number * size, size), size)


def bits():
    me = lax.axis_index("wide")
    return me, lax.rem(me, 2), lax.rem(lax.div(me, 2), 2)


def put_sums(out_ref, columns, sums):
    out_ref[:DH, columns] = sums.astype(bf16)


def get_sums(ref, columns):
    return ref[:DH, columns].astype(f32)


def attention_kernel(
    len_hbm, exp_hbm, index_hbm, mant_hbm, value_hbm, query_hbm,
    stat_ref, send_key_ref, keep_key_ref, send_ref, keep_ref,
    len_ref, exp_ref, index_ref, mant_ref, value_ref, query_ref, key_ref, sems,
):
    copies = [
        pltpu.make_async_copy(source, target, sems.at[i])
        for i, (source, target) in enumerate(
            (
                (exp_hbm, exp_ref),
                (mant_hbm, mant_ref),
                (query_hbm, query_ref),
                (len_hbm, len_ref),
                (index_hbm, index_ref),
                (value_hbm, value_ref),
            )
        )
    ]
    for copy in copies:
        copy.start()
    ctx = mant_ref.shape[0]
    me, core, bit = bits()
    for copy in copies:
        copy.wait()
    own_len = len_ref[me]
    for b in range(ctx // QB):
        exponent = exp_ref[b]
        factor = jnp.where(exponent > 0, 2.0, jnp.where(exponent < 0, 0.5, 1.0)).astype(f32)
        rows = pl.ds(b * QB, QB)
        key_ref[rows, :] = (mant_ref[rows, :].astype(f32) * factor).astype(bf16)
    half_m = M // 2
    position = lax.broadcasted_iota(jnp.int32, (SELECT_FROM, half_m), 0)
    for half, key_out, out in ((1 - core, send_key_ref, send_ref), (core, keep_key_ref, keep_ref)):
        wanted = index_ref[:, place(half, half_m)] - me * ctx
        chosen = jnp.where(position == wanted, 1.0, 0.0).astype(bf16)
        key_out[...] = mm(chosen, key_ref[:SELECT_FROM, :], TN).astype(bf16)
        prior = mm(value_ref[:SELECT_FROM, :], chosen, TN).astype(bf16)
        for piece in range(2):
            for part in range(2):
                begin = piece * CHUNK + part * QUARTER_M
                out[DH :, begin : begin + QUARTER_M] = prior[
                    part * (DH // 2) : (part + 1) * (DH // 2), piece * QUARTER_M : (piece + 1) * QUARTER_M
                ]
    dead = lax.broadcasted_iota(jnp.int32, (ctx, CHUNK), 0) >= own_len
    for half, out in ((1 - core, send_ref), (core, keep_ref)):
        for c in range(2):
            number = half * 2 + c
            scores = mm(key_ref[...], query_ref[place(number, CHUNK), :], NT)
            scores = jnp.where(dead, floor_value, scores)
            row_max = jnp.max(scores, axis=0, keepdims=True)
            attn = jnp.exp2((scores - row_max) * EXP2_SCALE)
            stat_ref[pl.ds(number, 1), :] = row_max
            stat_ref[pl.ds(CHUNKS + number, 1), :] = jnp.sum(attn, axis=0, keepdims=True)
            sums = mm(value_ref[...], attn.astype(bf16), TN)
            put_sums(out, pl.ds(c * CHUNK, CHUNK), sums)


def joined_stats(first_ref, second_ref, out_ref, scale_ref):
    max_first, max_second = first_ref[:CHUNKS, :], second_ref[:CHUNKS, :]
    joint = jnp.maximum(max_first, max_second)
    scale_first = jnp.exp2((max_first - joint) * EXP2_SCALE)
    scale_second = jnp.exp2((max_second - joint) * EXP2_SCALE)
    out_ref[:CHUNKS, :] = joint
    out_ref[CHUNKS:, :] = first_ref[CHUNKS:, :] * scale_first + second_ref[CHUNKS:, :] * scale_second
    scale_ref[...] = scale_first


def core_kernel(stat_a, stat_b, key_a, key_b, send_in, keep_in,
                stat_out, key_out, send_out, keep_out, scale_ref):
    me, core, bit = bits()
    joined_stats(stat_a, stat_b, stat_out, scale_ref)
    key_out[...] = key_a[...] + key_b[...]
    for half, source, out in ((1 - core, send_in, send_out), (core, keep_in, keep_out)):
        for c in range(2):
            columns = pl.ds(c * CHUNK, CHUNK)
            factor = scale_ref[pl.ds(half * 2 + c, 1), :]
            put_sums(out, columns, get_sums(source, columns) * factor)
        out[DH :, :] = source[DH :, :]


def halve_kernel(stat_a, stat_b, key_a, key_b, sum_a, sum_b,
                 stat_out, key_out, send_out, keep_out, scale_ref):
    me, core, bit = bits()
    joined_stats(stat_a, stat_b, stat_out, scale_ref)
    key_out[...] = key_a[...] + key_b[...]
    everything = pl.ds(0, CHUNK)
    for half, out in ((1 - bit, send_out), (bit, keep_out)):
        columns = place(half, CHUNK)
        factor = scale_ref[pl.ds(core * 2 + half, 1), :]
        put_sums(out, everything, (get_sums(sum_a, columns) + get_sums(sum_b, columns)) * factor)
        out[DH :, :] = sum_a[DH :, columns] + sum_b[DH :, columns]


def join_kernel(stat_a, stat_b, key_a, key_b, sum_a, sum_b, stat_out, key_out, sum_out, scale_ref):
    me, core, bit = bits()
    joined_stats(stat_a, stat_b, stat_out, scale_ref)
    key_out[...] = key_a[...] + key_b[...]
    everything = pl.ds(0, CHUNK)
    factor = scale_ref[pl.ds(core * 2 + bit, 1), :]
    put_sums(sum_out, everything, (get_sums(sum_a, everything) + get_sums(sum_b, everything)) * factor)
    sum_out[DH :, :] = sum_a[DH :, :] + sum_b[DH :, :]


def outputs_kernel(stat_ref, sum_a, sum_b, after_ref, out_ref):
    me, core, bit = bits()
    everything = pl.ds(0, CHUNK)
    row_mass = stat_ref[pl.ds(CHUNKS + core * 2 + bit, 1), :]
    put_sums(out_ref, everything, (get_sums(sum_a, everything) + get_sums(sum_b, everything)) / row_mass)
    out_ref[DH :, :] = sum_a[DH :, :] + sum_b[DH :, :]


def feature_kernel(
    len_ref, query_ref, stat_ref, own_key_ref, other_key_ref,
    gram_hi, gram_lo, linear_ref, norm_ref, scaled_hi, scaled_lo,
    key_ref, feat_hi, feat_lo,
):
    me, core, bit = bits()
    total = len_ref[0]
    for i in range(1, len_ref.shape[0]):
        total = total + len_ref[i]
    live_total = jnp.full((1, 1), total, jnp.int32).astype(f32)
    key_ref[place(core, M // 2), :] = own_key_ref[...]
    key_ref[place(1 - core, M // 2), :] = other_key_ref[...]
    frobenius = jnp.zeros((1, 1), f32)
    linear = jnp.zeros((16, M), f32)
    for c in range(CHUNKS):
        columns = pl.ds(c * CHUNK, CHUNK)
        row_max, row_mass = stat_ref[c : c + 1, :], stat_ref[CHUNKS + c : CHUNKS + c + 1, :]
        scores = mm(key_ref[...], query_ref[columns, :], NT)
        features = jnp.exp2((scores - row_max) * EXP2_SCALE)
        target = row_mass * (M / live_total)
        high, low = split(features)
        feat_hi[:, columns] = high
        feat_lo[:, columns] = low
        frobenius = frobenius + total_of(features * features)
        linear = linear + mm3(split(jnp.broadcast_to(target, (16, CHUNK))), (high, low), NT)
        high, low = split(features * (1.0 / target))
        scaled_hi[:, columns] = high
        scaled_lo[:, columns] = low
    feat = (feat_hi[...], feat_lo[...])
    high, low = split(mm3(feat, feat, NT))
    gram_hi[...] = high
    gram_lo[...] = low
    linear_ref[...] = linear
    norm_ref[...] = jnp.broadcast_to(frobenius, norm_ref.shape)


def weight_kernel(
    gram_hi, gram_lo, linear_ref, norm_ref, scaled_hi, scaled_lo,
    weight_out, factor_out, power_out, attend_ref,
):
    linear = linear_ref[...]
    frobenius = norm_ref[:1, :1]
    damping = nnls_ridge * (frobenius / M + 1e-6)
    stepsize = 1.0 / (frobenius + damping)
    weights = jnp.ones((16, M), f32)
    for number in range(NNLS_STEPS):
        gradient = mm3(split(weights), (gram_hi[...], gram_lo[...]), NN) - linear + damping * weights
        weights = jnp.maximum(weights - stepsize * gradient, 0.0)
        if number % 2 == 0 and number // 2 < CHUNKS:
            columns = pl.ds(number // 2 * CHUNK, CHUNK)
            scaled = (scaled_hi[:, columns], scaled_lo[:, columns])
            part = mm3(scaled, scaled, NT)
            attend_ref[...] = part if number == 0 else attend_ref[...] + part
    weight_row = weights[:1]
    weight_out[...] = weight_row
    weight_column = jnp.broadcast_to(weight_row, (DH, M)).T
    gram = attend_ref[...] * weight_row
    gram = gram * jnp.concatenate([weight_column] * (M // DH), axis=1)
    diagonal = lax.broadcasted_iota(jnp.int32, (M, M), 0) == lax.broadcasted_iota(
        jnp.int32, (M, M), 1
    )
    ridge = ridge_weight * (total_of(jnp.where(diagonal, gram, 0.0)) / M + 1e-6)
    system = gram + jnp.where(diagonal, ridge, 0.0)
    bound = jnp.max(jnp.sum(jnp.abs(system), axis=0, keepdims=True), axis=1, keepdims=True)
    row = lax.broadcasted_iota(jnp.int32, factor_out.shape, 0)
    factor_out[...] = jnp.where(row == 0, ridge, bound)
    power_out[...] = system * (1.0 / bound)


def forward_kernel(sum_ref, after_ref, out_ref):
    out_ref[...] = sum_ref[...]


def refit_kernel(
    power_in, weight_ref, factor_ref, scaled_hi, scaled_lo, part0, part1, part2, part3,
    value_out, both_ref, left_ref, right_ref, prior_ref,
):
    me, core, bit = bits()
    places = ((core, bit), (core, 1 - bit), (1 - core, bit), (1 - core, 1 - bit))
    product = jnp.zeros((DH, M), f32)
    for (hi_bit, lo_bit), part in zip(places, (part0, part1, part2, part3)):
        number = hi_bit * 2 + lo_bit
        columns = place(number, CHUNK)
        lanes = place(number, QUARTER_M)
        prior_ref[: DH // 2, lanes] = part[DH :, :QUARTER_M].astype(f32)
        prior_ref[DH // 2 :, lanes] = part[DH :, QUARTER_M:].astype(f32)
        product = product + (
            mm(part[:DH, :], scaled_hi[:, columns], NT) + mm(part[:DH, :], scaled_lo[:, columns], NT)
        )
    ridge, bound = factor_ref[0:1, :1], factor_ref[1:2, :1]
    both_ref[:M, :] = power_in[...]
    both_ref[M:, :] = (weight_ref[...] * product + ridge * prior_ref[...]) * (1.0 / bound)

    def newton_step(number, carry):
        both = both_ref[...]
        high, low = split(both)
        both_ref[...] = 2.0 * both - mm3((high, low), (high[:M], low[:M]), NN)
        return carry

    lax.fori_loop(0, NS_ITERS - 1, newton_step, 0)
    refit = both_ref[M:, :]
    refit = 2.0 * refit - mm3(split(refit), split(both_ref[:M, :]), NN)
    value_out[...] = refit.T


def shape(rows, columns, dtype):
    return jax.ShapeDtypeStruct((rows, columns), dtype)


def call(kernel, outs, arrays, scalars=0, scratch=(), in_specs=None, flops=None, limit=48):
    return pl.pallas_call(
        kernel,
        out_shape=tuple(outs),
        in_specs=in_specs
        or [pl.BlockSpec(memory_space=pltpu.SMEM)] * scalars
        + [pl.BlockSpec(memory_space=pltpu.VMEM)] * (len(arrays) - scalars),
        out_specs=tuple([pl.BlockSpec(memory_space=pltpu.VMEM)] * len(outs)),
        scratch_shapes=list(scratch),
        compiler_params=pltpu.CompilerParams(vmem_limit_bytes=int(limit * 1024 * 1024)),
        cost_estimate=None
        if flops is None
        else pl.CostEstimate(flops=flops, bytes_accessed=1024, transcendentals=0),
    )(*arrays)


def per_device(key_mant, scale_exp, values, queries, compact_index, shard_lengths):
    wide_count = lax.axis_size("wide")
    ctx = key_mant.shape[0]

    def exchanged(array, mask):
        return lax.ppermute(array, "wide", [(i, i ^ mask) for i in range(wide_count)])

    stat_shape = shape(2 * CHUNKS, CHUNK, f32)
    key_shape = shape(M // 2, DH, bf16)
    half_sum = shape(SUM_ROWS, 2 * CHUNK, bf16)
    quarter_sum = shape(SUM_ROWS, CHUNK, bf16)
    factors = [pltpu.VMEM((CHUNKS, CHUNK), f32)]

    stats, send_keys, keys, send, keep = call(
        attention_kernel,
        (stat_shape, key_shape, key_shape, half_sum, half_sum),
        [
            pltpu.with_memory_space_constraint(array, pltpu.HBM)
            for array in (
                shard_lengths, scale_exp, compact_index.reshape(1, M), key_mant, values, queries
            )
        ],
        in_specs=[pl.BlockSpec(memory_space=pltpu.HBM)] * 6,
        flops=10**9,
        scratch=[
            pltpu.SMEM(shard_lengths.shape, jnp.int32),
            pltpu.SMEM(scale_exp.shape, jnp.int32),
            pltpu.VMEM((1, M), jnp.int32),
            pltpu.VMEM((ctx, DH), bf16),
            pltpu.VMEM((ctx, DH), bf16),
            pltpu.VMEM((NQ, DH), bf16),
            pltpu.VMEM((ctx, DH), bf16),
            pltpu.SemaphoreType.DMA((6,)),
        ],
    )
    stats, keys, send, keep = call(
        core_kernel,
        (stat_shape, key_shape, half_sum, half_sum),
        (stats, exchanged(stats, 1), keys, exchanged(send_keys, 1), send, keep),
        scratch=factors,
    )
    stats, keys, send, keep = call(
        halve_kernel,
        (stat_shape, key_shape, quarter_sum, quarter_sum),
        (stats, exchanged(stats, 2), keys, exchanged(keys, 2), keep, exchanged(send, 1)),
        scratch=factors,
    )
    sums, got = keep, exchanged(send, 2)
    mask = 4
    while mask < wide_count:
        stats, keys, sums = call(
            join_kernel,
            (stat_shape, key_shape, quarter_sum),
            (stats, exchanged(stats, mask), keys, exchanged(keys, mask), sums, got),
            scratch=factors,
        )
        got = exchanged(sums, mask)
        mask *= 2
    gram_hi, gram_lo, linear, norm, scaled_hi, scaled_lo = call(
        feature_kernel,
        (shape(M, M, bf16),) * 2 + (shape(16, M, f32), shape(8, DH, f32)) + (shape(M, NQ, bf16),) * 2,
        (shard_lengths, queries, stats, keys, exchanged(keys, 1)),
        scalars=1,
        flops=4 * 10**9,
        scratch=[pltpu.VMEM((M, DH), bf16), pltpu.VMEM((M, NQ), bf16), pltpu.VMEM((M, NQ), bf16)],
    )
    (outputs,) = call(outputs_kernel, (quarter_sum,), (stats, sums, got, norm))
    side = exchanged(outputs, 2)
    core = exchanged(outputs, 1)
    weights, factor, power = call(
        weight_kernel,
        (shape(1, M, f32), shape(8, DH, f32), shape(M, M, f32)),
        (gram_hi, gram_lo, linear, norm, scaled_hi, scaled_lo),
        flops=5 * 10**9,
        scratch=[pltpu.VMEM((M, M), f32)],
    )
    (side,) = call(forward_kernel, (quarter_sum,), (side, factor))
    (compact_values,) = call(
        refit_kernel,
        (shape(M, DH, f32),),
        (power, weights, factor, scaled_hi, scaled_lo, outputs, side, core, exchanged(side, 1)),
        scratch=[
            pltpu.VMEM((M + DH, M), f32),
            pltpu.VMEM((M + DH, 3 * M), bf16),
            pltpu.VMEM((3 * M, M), bf16),
            pltpu.VMEM((DH, M), f32),
        ],
    )
    return weights.reshape(M), compact_values


def solution(mesh):
    placed = (
        P(("groups", "wide"), None),
        P(("groups", "wide")),
        P(("groups", "wide"), None),
        P("groups", None),
        P("groups"),
        P("groups"),
    )
    return jax.shard_map(
        per_device,
        mesh=mesh,
        in_specs=placed,
        out_specs=(P("groups"), P("groups", None)),
        check_vma=False,
    )
```

```python
import jax
import jax.numpy as jnp
from jax import lax
from jax.experimental import pallas as pl
from jax.experimental.pallas import tpu as pltpu
from jax.sharding import PartitionSpec as P

DH = 128
NQ = 1024
M = 512
QB = 32
SELECT_FROM = 256
NNLS_STEPS = 8
NS_ITERS = 9
SUM_FLOPS = 10**9
CHUNKS = 4
CHUNK = NQ // CHUNKS
QUARTER_M = M // CHUNKS
SUM_ROWS = DH + QUARTER_M // 2
PAIR_ROWS = SUM_ROWS + DH
HALF_M = M // 2

ridge_weight = 4.0
nnls_ridge = 0.1
floor_value = -1e30
EXP2_SCALE = DH ** (-0.5) * 1.4426950408889634

f32 = jnp.float32
bf16 = jnp.bfloat16
NN = (((1,), (0,)), ((), ()))
NT = (((1,), (1,)), ((), ()))
TN = (((0,), (0,)), ((), ()))


def mm(left, right, dims):
    return lax.dot_general(left, right, dims, preferred_element_type=f32)


def split(x):
    high = x.astype(bf16)
    return high, (x - high.astype(f32)).astype(bf16)


def mm3(left, right, dims):
    return mm(left[0], right[0], dims) + (mm(left[0], right[1], dims) + mm(left[1], right[0], dims))


def total_of(x):
    return jnp.sum(jnp.sum(x, axis=0, keepdims=True), axis=1, keepdims=True)


def place(number, size):
    return pl.ds(pl.multiple_of(number * size, size), size)


def bits():
    me = lax.axis_index("wide")
    return me, lax.rem(me, 2), lax.rem(lax.div(me, 2), 2)


PRIOR = SUM_ROWS - DH
PIECE_ROWS = SUM_ROWS // 2
EVERYTHING = slice(0, CHUNK)


def put_pair(out_ref, columns, prior, sums):
    high, low = split(sums)
    out_ref[:PRIOR, columns] = prior
    out_ref[PRIOR:SUM_ROWS, columns] = high
    out_ref[SUM_ROWS:, columns] = low


def get_pair(ref, columns):
    high = ref[PRIOR:SUM_ROWS, columns].astype(f32)
    return ref[:PRIOR, columns], high + ref[SUM_ROWS:, columns].astype(f32)


def put_pieces(first_ref, second_ref, prior, sums):
    sums = sums.astype(bf16)
    first_ref[:PRIOR, :] = prior
    first_ref[PRIOR:, :] = sums[: PIECE_ROWS - PRIOR]
    second_ref[...] = sums[PIECE_ROWS - PRIOR :]


def get_pieces(first_ref, second_ref):
    sums = jnp.concatenate([first_ref[PRIOR:, :], second_ref[...]], axis=0)
    return first_ref[:PRIOR, :], sums.astype(f32)


KEY_ROWS = HALF_M // 2
HEAD_ROWS = KEY_ROWS + 32


def put_keys(out_ref, keys):
    out_ref[:KEY_ROWS, :DH] = keys[:KEY_ROWS]
    out_ref[:KEY_ROWS, DH:] = keys[KEY_ROWS:]


def put_stats(out_ref, stats):
    high = stats.astype(bf16).astype(f32)
    middle = (stats - high).astype(bf16).astype(f32)
    low = stats - high - middle
    out_ref[KEY_ROWS:, :] = jnp.concatenate([high, middle, low, jnp.zeros_like(low)], axis=0).astype(bf16)


def get_stats(ref):
    parts = ref[KEY_ROWS:, :].astype(f32)
    return parts[:8] + parts[8:16] + parts[16:24]


def attention_kernel(
    len_hbm, exp_hbm, index_hbm, mant_hbm, value_hbm, query_hbm,
    send_head_ref, keep_head_ref, send_ref, keep_ref,
    stat_ref, len_ref, exp_ref, index_ref, mant_ref, value_ref, query_ref, key_ref, sems,
):
    copies = [
        pltpu.make_async_copy(source, target, sems.at[i])
        for i, (source, target) in enumerate(
            (
                (exp_hbm, exp_ref),
                (mant_hbm, mant_ref),
                (query_hbm, query_ref),
                (len_hbm, len_ref),
                (index_hbm, index_ref),
                (value_hbm, value_ref),
            )
        )
    ]
    for copy in copies:
        copy.start()
    ctx = mant_ref.shape[0]
    me, core, bit = bits()
    for copy in copies:
        copy.wait()
    for b in range(ctx // QB):
        exponent = exp_ref[b]
        factor = jnp.where(exponent > 0, 2.0, jnp.where(exponent < 0, 0.5, 1.0)).astype(f32)
        rows = pl.ds(b * QB, QB)
        key_ref[rows, :] = (mant_ref[rows, :].astype(f32) * factor).astype(bf16)
    half_m = M // 2
    position = lax.broadcasted_iota(jnp.int32, (SELECT_FROM, half_m), 0)
    for half, head_out, out in ((1 - core, send_head_ref, send_ref), (core, keep_head_ref, keep_ref)):
        wanted = index_ref[:, place(half, half_m)] - me * ctx
        chosen = jnp.where(position == wanted, 1.0, 0.0).astype(bf16)
        put_keys(head_out, mm(chosen, key_ref[:SELECT_FROM, :], TN).astype(bf16))
        prior = mm(value_ref[:SELECT_FROM, :], chosen, TN).astype(bf16)
        for piece in range(2):
            for part in range(2):
                begin = piece * CHUNK + part * QUARTER_M
                out[:PRIOR, begin : begin + QUARTER_M] = prior[
                    part * (DH // 2) : (part + 1) * (DH // 2), piece * QUARTER_M : (piece + 1) * QUARTER_M
                ]
    dead = lax.broadcasted_iota(jnp.int32, (ctx, CHUNK), 0) >= len_ref[me]
    for half, out in ((1 - core, send_ref), (core, keep_ref)):
        for c in range(2):
            number = half * 2 + c
            scores = mm(key_ref[...], query_ref[place(number, CHUNK), :], NT)
            scores = jnp.where(dead, floor_value, scores)
            row_max = jnp.max(scores, axis=0, keepdims=True)
            attn = jnp.exp2((scores - row_max) * EXP2_SCALE)
            stat_ref[pl.ds(number, 1), :] = row_max
            stat_ref[pl.ds(CHUNKS + number, 1), :] = jnp.sum(attn, axis=0, keepdims=True)
            sums = mm(value_ref[...], attn.astype(bf16), TN)
            high, low = split(sums)
            out[PRIOR:SUM_ROWS, c * CHUNK : (c + 1) * CHUNK] = high
            out[SUM_ROWS:, c * CHUNK : (c + 1) * CHUNK] = low
    put_stats(send_head_ref, stat_ref[...])
    put_stats(keep_head_ref, stat_ref[...])


def join_kernel(first_ref, second_ref, out_ref, scale_out):
    first, second = get_stats(first_ref), get_stats(second_ref)
    joint = jnp.maximum(first[:CHUNKS], second[:CHUNKS])
    scale_first = jnp.exp2((first[:CHUNKS] - joint) * EXP2_SCALE)
    scale_second = jnp.exp2((second[:CHUNKS] - joint) * EXP2_SCALE)
    mass = first[CHUNKS:] * scale_first + second[CHUNKS:] * scale_second
    put_stats(out_ref, jnp.concatenate([joint, mass], axis=0))
    out_ref[:KEY_ROWS, :] = first_ref[:KEY_ROWS, :] + second_ref[:KEY_ROWS, :]
    scale_out[...] = scale_first


def last_join_kernel(first_ref, second_ref, key_out, stat_out, scale_out):
    first, second = get_stats(first_ref), get_stats(second_ref)
    joint = jnp.maximum(first[:CHUNKS], second[:CHUNKS])
    scale_first = jnp.exp2((first[:CHUNKS] - joint) * EXP2_SCALE)
    scale_second = jnp.exp2((second[:CHUNKS] - joint) * EXP2_SCALE)
    stat_out[:CHUNKS, :] = joint
    stat_out[CHUNKS:, :] = first[CHUNKS:] * scale_first + second[CHUNKS:] * scale_second
    for c in range(2):
        columns = slice(c * DH, (c + 1) * DH)
        rows = slice(c * KEY_ROWS, (c + 1) * KEY_ROWS)
        key_out[rows, :] = first_ref[:KEY_ROWS, columns] + second_ref[:KEY_ROWS, columns]
    scale_out[...] = scale_first


def core_sum_kernel(scale_ref, send_in, keep_in, send_out, keep_out):
    me, core, bit = bits()
    for half, source, out in ((1 - core, send_in, send_out), (core, keep_in, keep_out)):
        for c in range(2):
            columns = pl.ds(c * CHUNK, CHUNK)
            prior, sums = get_pair(source, columns)
            put_pair(out, columns, prior, sums * scale_ref[pl.ds(half * 2 + c, 1), :])


def halve_sum_kernel(scale_ref, sum_a, sum_b, first_out, second_out, keep_out):
    me, core, bit = bits()

    def half_of(half):
        columns = place(half, CHUNK)
        prior_a, sums_a = get_pair(sum_a, columns)
        prior_b, sums_b = get_pair(sum_b, columns)
        return prior_a + prior_b, (sums_a + sums_b) * scale_ref[pl.ds(core * 2 + half, 1), :]

    put_pieces(first_out, second_out, *half_of(1 - bit))
    put_pair(keep_out, EVERYTHING, *half_of(bit))


def own_sums(refs):
    return get_pair(refs[0], EVERYTHING) if len(refs) == 1 else get_pieces(*refs)


def join_sum_kernel(scale_ref, *refs):
    me, core, bit = bits()
    prior_a, sums_a = own_sums(refs[:-4])
    prior_b, sums_b = get_pieces(*refs[-4:-2])
    factor = scale_ref[pl.ds(core * 2 + bit, 1), :]
    put_pieces(*refs[-2:], prior_a + prior_b, (sums_a + sums_b) * factor)


def outputs_kernel(stat_ref, first_a, second_a, first_b, second_b, after_ref, first_out, second_out):
    me, core, bit = bits()
    prior_a, sums_a = get_pieces(first_a, second_a)
    prior_b, sums_b = get_pieces(first_b, second_b)
    row_mass = stat_ref[pl.ds(CHUNKS + core * 2 + bit, 1), :]
    put_pieces(first_out, second_out, prior_a + prior_b, (sums_a + sums_b) / row_mass)


def gram3(high, low):
    top = mm3((high[:HALF_M], low[:HALF_M]), (high, low), NT)
    corner = mm3((high[HALF_M:], low[HALF_M:]), (high[HALF_M:], low[HALF_M:]), NT)
    return top, jnp.concatenate([top[:, HALF_M:].T, corner], axis=1)


def feature_kernel(
    len_ref, query_ref, stat_ref, own_key_ref, other_key_ref,
    gram_ref, linear_ref, norm_ref, scaled_hi, scaled_lo,
    key_ref, feat_hi, feat_lo,
):
    me, core, bit = bits()
    total = len_ref[0]
    for i in range(1, len_ref.shape[0]):
        total = total + len_ref[i]
    live_total = jnp.full((1, 1), total, jnp.int32).astype(f32)
    key_ref[place(core, M // 2), :] = own_key_ref[...]
    key_ref[place(1 - core, M // 2), :] = other_key_ref[...]
    frobenius = jnp.zeros((1, 1), f32)
    linear = jnp.zeros((M, DH), f32)
    for c in range(CHUNKS):
        columns = pl.ds(c * CHUNK, CHUNK)
        row_max, row_mass = stat_ref[c : c + 1, :], stat_ref[CHUNKS + c : CHUNKS + c + 1, :]
        scores = mm(key_ref[...], query_ref[columns, :], NT)
        features = jnp.exp2((scores - row_max) * EXP2_SCALE)
        target = row_mass * (M / live_total)
        high, low = split(features)
        feat_hi[:, columns] = high
        feat_lo[:, columns] = low
        frobenius = frobenius + total_of(features * features)
        weighted = features * target
        for tile in range(CHUNK // DH):
            linear = linear + weighted[:, tile * DH : (tile + 1) * DH]
        high, low = split(features * (1.0 / target))
        scaled_hi[:, columns] = high
        scaled_lo[:, columns] = low
    gram_ref[:HALF_M, :], gram_ref[HALF_M:, :] = gram3(feat_hi[...], feat_lo[...])
    linear_ref[...] = jnp.broadcast_to(jnp.sum(linear, axis=1, keepdims=True), (M, DH))
    norm_ref[...] = jnp.broadcast_to(frobenius, norm_ref.shape)


def weight_kernel(
    gram_ref, linear_ref, norm_ref, scaled_hi, scaled_lo,
    weight_out, factor_out, power_out, attend_ref,
):
    frobenius = norm_ref[:1, :1]
    damping = nnls_ridge * (frobenius / M + 1e-6)
    stepsize = 1.0 / (frobenius + damping)
    linear_column = linear_ref[...]
    linear_row = linear_column.T[:1]
    row = jnp.ones((1, M), f32)
    column = jnp.ones((M, DH), f32)
    tiles = [slice(t * DH, (t + 1) * DH) for t in range(M // DH)]

    def moved(weights, product, linear):
        gradient = product - linear + damping * weights
        return jnp.maximum(weights - stepsize * gradient, 0.0)

    for number in range(NNLS_STEPS):
        down = [jnp.sum(gram_ref[:, t] * column, axis=0, keepdims=True) for t in tiles]
        along = gram_ref[:, tiles[0]] * row[:, tiles[0]]
        for t in tiles[1:]:
            along = along + gram_ref[:, t] * row[:, t]
        along = jnp.broadcast_to(jnp.sum(along, axis=1, keepdims=True), (M, DH))
        row = moved(row, jnp.concatenate(down, axis=1), linear_row)
        column = moved(column, along, linear_column)
        if number % 2 == 0 and number // 2 < CHUNKS:
            columns = pl.ds(number // 2 * CHUNK, CHUNK)
            top, corner = gram3(scaled_hi[:, columns], scaled_lo[:, columns])
            attend_ref[:HALF_M, :] = top if number == 0 else attend_ref[:HALF_M, :] + top
            attend_ref[HALF_M:, :] = corner if number == 0 else attend_ref[HALF_M:, :] + corner
    weight_out[...] = row
    gram = attend_ref[...] * row
    gram = gram * jnp.concatenate([column] * (M // DH), axis=1)
    diagonal = lax.broadcasted_iota(jnp.int32, (M, M), 0) == lax.broadcasted_iota(
        jnp.int32, (M, M), 1
    )
    ridge = ridge_weight * (total_of(jnp.where(diagonal, gram, 0.0)) / M + 1e-6)
    system = gram + jnp.where(diagonal, ridge, 0.0)
    bound = jnp.max(jnp.sum(jnp.abs(system), axis=0, keepdims=True), axis=1, keepdims=True)
    row = lax.broadcasted_iota(jnp.int32, factor_out.shape, 0)
    factor_out[...] = jnp.where(row == 0, ridge, bound)
    power_out[...] = system * (1.0 / bound)


def forward_kernel(own_first, own_second, side_first, side_second, after_ref, out_ref):
    for i, ref in enumerate((own_first, own_second, side_first, side_second)):
        out_ref[i * PIECE_ROWS : (i + 1) * PIECE_ROWS, :] = ref[...]


def right_side(half_ref, half, bit, scaled_hi, scaled_lo, prior_ref):
    product = None
    for i, lo_bit in enumerate((bit, 1 - bit)):
        number = half * 2 + lo_bit
        begin = i * SUM_ROWS
        lanes = place(number, QUARTER_M)
        prior_ref[: DH // 2, lanes] = half_ref[begin : begin + PRIOR, :QUARTER_M].astype(f32)
        prior_ref[DH // 2 :, lanes] = half_ref[begin : begin + PRIOR, QUARTER_M:].astype(f32)
        outputs = half_ref[begin + PRIOR : begin + SUM_ROWS, :]
        columns = place(number, CHUNK)
        part = mm(outputs, scaled_hi[:, columns], NT) + mm(outputs, scaled_lo[:, columns], NT)
        product = part if product is None else product + part
    return product


def refit_kernel(
    power_in, weight_ref, factor_ref, scaled_hi, scaled_lo, own_ref, half_ref,
    value_out, both_ref, prior_ref,
):
    me, core, bit = bits()
    product = right_side(own_ref, core, bit, scaled_hi, scaled_lo, prior_ref)
    product = product + right_side(half_ref, 1 - core, bit, scaled_hi, scaled_lo, prior_ref)
    ridge, bound = factor_ref[0:1, :1], factor_ref[1:2, :1]
    both_ref[DH:, :] = power_in[...]
    both_ref[:DH, :] = (weight_ref[...] * product + ridge * prior_ref[...]) * (1.0 / bound)
    above = DH + HALF_M

    def newton_step(number, carry):
        high, low = split(both_ref[...])
        power = (high[DH:], low[DH:])
        top = 2.0 * both_ref[:above, :] - mm3((high[:above], low[:above]), power, NN)
        corner = mm3((high[above:], low[above:]), (power[0][:, HALF_M:], power[1][:, HALF_M:]), NN)
        both_ref[above:, HALF_M:] = 2.0 * both_ref[above:, HALF_M:] - corner
        both_ref[above:, :HALF_M] = top[DH:, HALF_M:].T
        both_ref[:above, :] = top
        return carry

    lax.fori_loop(0, NS_ITERS - 2, newton_step, 0)
    power = split(both_ref[DH:, :])
    refit = both_ref[:DH, :]
    refit = 2.0 * refit - mm3(split(refit), power, NN)
    once = mm3(split(refit), power, NN)
    refit = 2.0 * (refit - once) + mm3(split(once), power, NN)
    value_out[...] = refit.T


def shape(rows, columns, dtype):
    return jax.ShapeDtypeStruct((rows, columns), dtype)


def call(kernel, outs, arrays, scalars=0, scratch=(), in_specs=None, flops=None, limit=48):
    return pl.pallas_call(
        kernel,
        out_shape=tuple(outs),
        in_specs=in_specs
        or [pl.BlockSpec(memory_space=pltpu.SMEM)] * scalars
        + [pl.BlockSpec(memory_space=pltpu.VMEM)] * (len(arrays) - scalars),
        out_specs=tuple([pl.BlockSpec(memory_space=pltpu.VMEM)] * len(outs)),
        scratch_shapes=list(scratch),
        compiler_params=pltpu.CompilerParams(vmem_limit_bytes=int(limit * 1024 * 1024)),
        cost_estimate=None
        if flops is None
        else pl.CostEstimate(flops=flops, bytes_accessed=1024, transcendentals=0),
    )(*arrays)


def per_device(key_mant, scale_exp, values, queries, compact_index, shard_lengths):
    wide_count = lax.axis_size("wide")
    ctx = key_mant.shape[0]

    def exchanged(array, mask):
        return lax.ppermute(array, "wide", [(i, i ^ mask) for i in range(wide_count)])

    head_shape = shape(HEAD_ROWS, CHUNK, bf16)
    scale_shape = shape(CHUNKS, CHUNK, f32)
    half_sum = shape(PAIR_ROWS, 2 * CHUNK, bf16)
    pieces = (shape(PIECE_ROWS, CHUNK, bf16),) * 2

    send_head, head, send, keep = call(
        attention_kernel,
        (head_shape, head_shape, half_sum, half_sum),
        [
            pltpu.with_memory_space_constraint(array, pltpu.HBM)
            for array in (
                shard_lengths, scale_exp, compact_index.reshape(1, M), key_mant, values, queries
            )
        ],
        in_specs=[pl.BlockSpec(memory_space=pltpu.HBM)] * 6,
        flops=10**9,
        scratch=[
            pltpu.VMEM((2 * CHUNKS, CHUNK), f32),
            pltpu.SMEM(shard_lengths.shape, jnp.int32),
            pltpu.SMEM(scale_exp.shape, jnp.int32),
            pltpu.VMEM((1, M), jnp.int32),
            pltpu.VMEM((ctx, DH), bf16),
            pltpu.VMEM((ctx, DH), bf16),
            pltpu.VMEM((NQ, DH), bf16),
            pltpu.VMEM((ctx, DH), bf16),
            pltpu.SemaphoreType.DMA((6,)),
        ],
    )
    def both_exchanged(arrays, mask):
        return tuple(exchanged(array, mask) for array in arrays)

    head, scale = call(join_kernel, (head_shape, scale_shape), (head, exchanged(send_head, 1)))
    got_head = exchanged(head, 2)
    send, keep = call(core_sum_kernel, (half_sum, half_sum), (scale, send, keep), flops=SUM_FLOPS)
    got = exchanged(send, 1)
    masks = [4]
    while 2 * masks[-1] < wide_count:
        masks.append(2 * masks[-1])
    head, scale = call(join_kernel, (head_shape, scale_shape), (head, got_head))
    got_head = exchanged(head, masks[0])
    first, second, keep = call(
        halve_sum_kernel,
        pieces + (shape(PAIR_ROWS, CHUNK, bf16),),
        (scale, keep, got),
        flops=SUM_FLOPS,
    )
    sums, got = (keep,), both_exchanged((first, second), 2)
    for number, mask in enumerate(masks):
        if number + 1 < len(masks):
            head, scale = call(join_kernel, (head_shape, scale_shape), (head, got_head))
            got_head = exchanged(head, masks[number + 1])
        else:
            keys, stats, scale = call(
                last_join_kernel,
                (shape(HALF_M, DH, bf16), shape(2 * CHUNKS, CHUNK, f32), scale_shape),
                (head, got_head),
            )
            got_keys = exchanged(keys, 1)
        sums = call(join_sum_kernel, pieces, (scale,) + sums + got, flops=SUM_FLOPS)
        got = both_exchanged(sums, mask)
    gram, linear, norm, scaled_hi, scaled_lo = call(
        feature_kernel,
        (shape(M, M, f32), shape(M, DH, f32), shape(8, DH, f32)) + (shape(M, NQ, bf16),) * 2,
        (shard_lengths, queries, stats, keys, got_keys),
        scalars=1,
        flops=4 * 10**9,
        scratch=[pltpu.VMEM((M, DH), bf16), pltpu.VMEM((M, NQ), bf16), pltpu.VMEM((M, NQ), bf16)],
    )
    outputs = call(outputs_kernel, pieces, (stats,) + tuple(sums) + got + (norm,))
    side = both_exchanged(outputs, 2)
    weights, factor, power = call(
        weight_kernel,
        (shape(1, M, f32), shape(8, DH, f32), shape(M, M, f32)),
        (gram, linear, norm, scaled_hi, scaled_lo),
        flops=5 * 10**9,
        scratch=[pltpu.VMEM((M, M), f32)],
    )
    (half,) = call(
        forward_kernel,
        (shape(2 * SUM_ROWS, CHUNK, bf16),),
        tuple(outputs) + side + (factor,),
    )
    (compact_values,) = call(
        refit_kernel,
        (shape(M, DH, f32),),
        (power, weights, factor, scaled_hi, scaled_lo, half, exchanged(half, 1)),
        scratch=[
            pltpu.VMEM((M + DH, M), f32),
            pltpu.VMEM((DH, M), f32),
        ],
    )
    return weights.reshape(M), compact_values


def solution(mesh):
    placed = (
        P(("groups", "wide"), None),
        P(("groups", "wide")),
        P(("groups", "wide"), None),
        P("groups", None),
        P("groups"),
        P("groups"),
    )
    return jax.shard_map(
        per_device,
        mesh=mesh,
        in_specs=placed,
        out_specs=(P("groups"), P("groups", None)),
        check_vma=False,
    )
```

```python
import jax
import jax.numpy as jnp
from jax import lax
from jax.experimental import pallas as pl
from jax.experimental.pallas import tpu as pltpu
from jax.sharding import PartitionSpec as P

DH = 128
NQ = 1024
M = 512
QB = 32
SELECT_FROM = 256
NNLS_STEPS = 8
NS_ITERS = 9
SUM_FLOPS = 10**9
CHUNKS = 4
CHUNK = NQ // CHUNKS
QUARTER_M = M // CHUNKS
SUM_ROWS = DH + QUARTER_M // 2
PAIR_ROWS = SUM_ROWS + DH
HALF_M = M // 2

ridge_weight = 4.0
nnls_ridge = 0.1
floor_value = -1e30
EXP2_SCALE = DH ** (-0.5) * 1.4426950408889634

f32 = jnp.float32
bf16 = jnp.bfloat16
NN = (((1,), (0,)), ((), ()))
NT = (((1,), (1,)), ((), ()))
TN = (((0,), (0,)), ((), ()))


def mm(left, right, dims):
    return lax.dot_general(left, right, dims, preferred_element_type=f32)


def split(x):
    high = x.astype(bf16)
    return high, (x - high.astype(f32)).astype(bf16)


def mm3(left, right, dims):
    return mm(left[0], right[0], dims) + (mm(left[0], right[1], dims) + mm(left[1], right[0], dims))


def total_of(x):
    return jnp.sum(jnp.sum(x, axis=0, keepdims=True), axis=1, keepdims=True)


def place(number, size):
    return pl.ds(pl.multiple_of(number * size, size), size)


def bits():
    me = lax.axis_index("wide")
    return me, lax.rem(me, 2), lax.rem(lax.div(me, 2), 2)


PRIOR = SUM_ROWS - DH
PIECE_ROWS = SUM_ROWS // 2
EVERYTHING = slice(0, CHUNK)


def put_pair(out_ref, columns, prior, sums):
    high, low = split(sums)
    out_ref[:PRIOR, columns] = prior
    out_ref[PRIOR:SUM_ROWS, columns] = high
    out_ref[SUM_ROWS:, columns] = low


def get_pair(ref, columns):
    high = ref[PRIOR:SUM_ROWS, columns].astype(f32)
    return ref[:PRIOR, columns], high + ref[SUM_ROWS:, columns].astype(f32)


def put_pieces(first_ref, second_ref, prior, sums):
    sums = sums.astype(bf16)
    first_ref[:PRIOR, :] = prior
    first_ref[PRIOR:, :] = sums[: PIECE_ROWS - PRIOR]
    second_ref[...] = sums[PIECE_ROWS - PRIOR :]


def get_pieces(first_ref, second_ref):
    sums = jnp.concatenate([first_ref[PRIOR:, :], second_ref[...]], axis=0)
    return first_ref[:PRIOR, :], sums.astype(f32)


KEY_ROWS = HALF_M // 2
HEAD_ROWS = KEY_ROWS + 32


def put_keys(out_ref, keys):
    out_ref[:KEY_ROWS, :DH] = keys[:KEY_ROWS]
    out_ref[:KEY_ROWS, DH:] = keys[KEY_ROWS:]


def put_stats(out_ref, stats):
    high = stats.astype(bf16).astype(f32)
    middle = (stats - high).astype(bf16).astype(f32)
    low = stats - high - middle
    out_ref[KEY_ROWS:, :] = jnp.concatenate([high, middle, low, jnp.zeros_like(low)], axis=0).astype(bf16)


def get_stats(ref):
    parts = ref[KEY_ROWS:, :].astype(f32)
    return parts[:8] + parts[8:16] + parts[16:24]


def attention_kernel(
    len_hbm, exp_hbm, index_hbm, mant_hbm, value_hbm, query_hbm,
    send_head_ref, keep_head_ref, send_ref, keep_ref,
    stat_ref, len_ref, exp_ref, index_ref, mant_ref, value_ref, query_ref, key_ref, sems,
):
    copies = [
        pltpu.make_async_copy(source, target, sems.at[i])
        for i, (source, target) in enumerate(
            (
                (exp_hbm, exp_ref),
                (mant_hbm, mant_ref),
                (query_hbm, query_ref),
                (len_hbm, len_ref),
                (index_hbm, index_ref),
                (value_hbm, value_ref),
            )
        )
    ]
    for copy in copies:
        copy.start()
    ctx = mant_ref.shape[0]
    me, core, bit = bits()
    for copy in copies:
        copy.wait()
    for b in range(ctx // QB):
        exponent = exp_ref[b]
        factor = jnp.where(exponent > 0, 2.0, jnp.where(exponent < 0, 0.5, 1.0)).astype(f32)
        rows = pl.ds(b * QB, QB)
        key_ref[rows, :] = (mant_ref[rows, :].astype(f32) * factor).astype(bf16)
    half_m = M // 2
    position = lax.broadcasted_iota(jnp.int32, (SELECT_FROM, half_m), 0)
    for half, head_out, out in ((1 - core, send_head_ref, send_ref), (core, keep_head_ref, keep_ref)):
        wanted = index_ref[:, place(half, half_m)] - me * ctx
        chosen = jnp.where(position == wanted, 1.0, 0.0).astype(bf16)
        put_keys(head_out, mm(chosen, key_ref[:SELECT_FROM, :], TN).astype(bf16))
        prior = mm(value_ref[:SELECT_FROM, :], chosen, TN).astype(bf16)
        for piece in range(2):
            for part in range(2):
                begin = piece * CHUNK + part * QUARTER_M
                out[:PRIOR, begin : begin + QUARTER_M] = prior[
                    part * (DH // 2) : (part + 1) * (DH // 2), piece * QUARTER_M : (piece + 1) * QUARTER_M
                ]
    dead = lax.broadcasted_iota(jnp.int32, (ctx, CHUNK), 0) >= len_ref[me]
    for half, out in ((1 - core, send_ref), (core, keep_ref)):
        for c in range(2):
            number = half * 2 + c
            scores = mm(key_ref[...], query_ref[place(number, CHUNK), :], NT)
            scores = jnp.where(dead, floor_value, scores)
            row_max = jnp.max(scores, axis=0, keepdims=True)
            attn = jnp.exp2((scores - row_max) * EXP2_SCALE)
            stat_ref[pl.ds(number, 1), :] = row_max
            stat_ref[pl.ds(CHUNKS + number, 1), :] = jnp.sum(attn, axis=0, keepdims=True)
            sums = mm(value_ref[...], attn.astype(bf16), TN)
            high, low = split(sums)
            out[PRIOR:SUM_ROWS, c * CHUNK : (c + 1) * CHUNK] = high
            out[SUM_ROWS:, c * CHUNK : (c + 1) * CHUNK] = low
    put_stats(send_head_ref, stat_ref[...])
    put_stats(keep_head_ref, stat_ref[...])


def joined_stats(first_ref, second_ref, scale_first_out, scale_second_out):
    first, second = get_stats(first_ref), get_stats(second_ref)
    joint = jnp.maximum(first[:CHUNKS], second[:CHUNKS])
    scale_first = jnp.exp2((first[:CHUNKS] - joint) * EXP2_SCALE)
    scale_second = jnp.exp2((second[:CHUNKS] - joint) * EXP2_SCALE)
    scale_first_out[...] = scale_first
    scale_second_out[...] = scale_second
    mass = first[CHUNKS:] * scale_first + second[CHUNKS:] * scale_second
    return jnp.concatenate([joint, mass], axis=0)


def join_kernel(first_ref, second_ref, *refs):
    out_ref, scale_first_out, scale_second_out = refs[-3:]
    put_stats(out_ref, joined_stats(first_ref, second_ref, scale_first_out, scale_second_out))
    out_ref[:KEY_ROWS, :] = first_ref[:KEY_ROWS, :] + second_ref[:KEY_ROWS, :]


def last_join_kernel(first_ref, second_ref, after_ref, key_out, stat_out, scale_first_out, scale_second_out):
    stat_out[...] = joined_stats(first_ref, second_ref, scale_first_out, scale_second_out)
    for c in range(2):
        columns = slice(c * DH, (c + 1) * DH)
        rows = slice(c * KEY_ROWS, (c + 1) * KEY_ROWS)
        key_out[rows, :] = first_ref[:KEY_ROWS, columns] + second_ref[:KEY_ROWS, columns]


def halve_sum_kernel(scale_a, scale_b, sum_a, sum_b, first_out, second_out, keep_out):
    me, core, bit = bits()

    def half_of(half):
        columns = place(half, CHUNK)
        row = pl.ds(core * 2 + half, 1)
        prior_a, sums_a = get_pair(sum_a, columns)
        prior_b, sums_b = get_pair(sum_b, columns)
        return prior_a + prior_b, sums_a * scale_a[row, :] + sums_b * scale_b[row, :]

    put_pieces(first_out, second_out, *half_of(1 - bit))
    put_pair(keep_out, EVERYTHING, *half_of(bit))


def joined_sums(scale_a, scale_b, own, got):
    me, core, bit = bits()
    row = pl.ds(core * 2 + bit, 1)
    prior_a, sums_a = get_pair(own[0], EVERYTHING) if len(own) == 1 else get_pieces(*own)
    prior_b, sums_b = get_pieces(*got)
    return prior_a + prior_b, sums_a * scale_a[row, :] + sums_b * scale_b[row, :]


def join_sum_kernel(scale_a, scale_b, *refs):
    put_pieces(*refs[-2:], *joined_sums(scale_a, scale_b, refs[:-4], refs[-4:-2]))


def outputs_kernel(
    scale_a, scale_b, stat_ref, first_a, second_a, first_b, second_b, after_ref, first_out, second_out
):
    me, core, bit = bits()
    prior, sums = joined_sums(scale_a, scale_b, (first_a, second_a), (first_b, second_b))
    put_pieces(first_out, second_out, prior, sums / stat_ref[pl.ds(CHUNKS + core * 2 + bit, 1), :])


def gram3(high, low):
    top = mm3((high[:HALF_M], low[:HALF_M]), (high, low), NT)
    corner = mm3((high[HALF_M:], low[HALF_M:]), (high[HALF_M:], low[HALF_M:]), NT)
    return top, jnp.concatenate([top[:, HALF_M:].T, corner], axis=1)


def feature_kernel(
    len_ref, query_ref, stat_ref, own_key_ref, other_key_ref,
    gram_ref, linear_ref, norm_ref, scaled_hi, scaled_lo,
    key_ref, feat_hi, feat_lo,
):
    me, core, bit = bits()
    total = len_ref[0]
    for i in range(1, len_ref.shape[0]):
        total = total + len_ref[i]
    live_total = jnp.full((1, 1), total, jnp.int32).astype(f32)
    key_ref[place(core, M // 2), :] = own_key_ref[...]
    key_ref[place(1 - core, M // 2), :] = other_key_ref[...]
    frobenius = jnp.zeros((1, 1), f32)
    linear = jnp.zeros((M, DH), f32)
    for c in range(CHUNKS):
        columns = pl.ds(c * CHUNK, CHUNK)
        row_max, row_mass = stat_ref[c : c + 1, :], stat_ref[CHUNKS + c : CHUNKS + c + 1, :]
        scores = mm(key_ref[...], query_ref[columns, :], NT)
        features = jnp.exp2((scores - row_max) * EXP2_SCALE)
        target = row_mass * (M / live_total)
        high, low = split(features)
        feat_hi[:, columns] = high
        feat_lo[:, columns] = low
        frobenius = frobenius + total_of(features * features)
        weighted = features * target
        for tile in range(CHUNK // DH):
            linear = linear + weighted[:, tile * DH : (tile + 1) * DH]
        high, low = split(features * (1.0 / target))
        scaled_hi[:, columns] = high
        scaled_lo[:, columns] = low
    gram_ref[:HALF_M, :], gram_ref[HALF_M:, :] = gram3(feat_hi[...], feat_lo[...])
    linear_ref[...] = jnp.broadcast_to(jnp.sum(linear, axis=1, keepdims=True), (M, DH))
    norm_ref[...] = jnp.broadcast_to(frobenius, norm_ref.shape)


def weight_kernel(
    gram_ref, linear_ref, norm_ref, scaled_hi, scaled_lo,
    weight_out, factor_out, power_out, attend_ref,
):
    frobenius = norm_ref[:1, :1]
    damping = nnls_ridge * (frobenius / M + 1e-6)
    stepsize = 1.0 / (frobenius + damping)
    linear_column = linear_ref[...]
    linear_row = linear_column.T[:1]
    row = jnp.ones((1, M), f32)
    column = jnp.ones((M, DH), f32)
    tiles = [slice(t * DH, (t + 1) * DH) for t in range(M // DH)]

    def moved(weights, product, linear):
        gradient = product - linear + damping * weights
        return jnp.maximum(weights - stepsize * gradient, 0.0)

    for number in range(NNLS_STEPS):
        down = [jnp.sum(gram_ref[:, t] * column, axis=0, keepdims=True) for t in tiles]
        along = gram_ref[:, tiles[0]] * row[:, tiles[0]]
        for t in tiles[1:]:
            along = along + gram_ref[:, t] * row[:, t]
        along = jnp.broadcast_to(jnp.sum(along, axis=1, keepdims=True), (M, DH))
        row = moved(row, jnp.concatenate(down, axis=1), linear_row)
        column = moved(column, along, linear_column)
        if number % 2 == 0 and number // 2 < CHUNKS:
            columns = pl.ds(number // 2 * CHUNK, CHUNK)
            top, corner = gram3(scaled_hi[:, columns], scaled_lo[:, columns])
            attend_ref[:HALF_M, :] = top if number == 0 else attend_ref[:HALF_M, :] + top
            attend_ref[HALF_M:, :] = corner if number == 0 else attend_ref[HALF_M:, :] + corner
    weight_out[...] = row
    gram = attend_ref[...] * row
    gram = gram * jnp.concatenate([column] * (M // DH), axis=1)
    diagonal = lax.broadcasted_iota(jnp.int32, (M, M), 0) == lax.broadcasted_iota(
        jnp.int32, (M, M), 1
    )
    ridge = ridge_weight * (total_of(jnp.where(diagonal, gram, 0.0)) / M + 1e-6)
    system = gram + jnp.where(diagonal, ridge, 0.0)
    bound = jnp.max(jnp.sum(jnp.abs(system), axis=0, keepdims=True), axis=1, keepdims=True)
    row = lax.broadcasted_iota(jnp.int32, factor_out.shape, 0)
    factor_out[...] = jnp.where(row == 0, ridge, bound)
    power_out[...] = system * (1.0 / bound)


def forward_kernel(own_first, own_second, side_first, side_second, after_ref, out_ref):
    for i, ref in enumerate((own_first, own_second, side_first, side_second)):
        out_ref[i * PIECE_ROWS : (i + 1) * PIECE_ROWS, :] = ref[...]


def right_side(half_ref, half, bit, scaled_hi, scaled_lo, prior_ref):
    product = None
    for i, lo_bit in enumerate((bit, 1 - bit)):
        number = half * 2 + lo_bit
        begin = i * SUM_ROWS
        lanes = place(number, QUARTER_M)
        prior_ref[: DH // 2, lanes] = half_ref[begin : begin + PRIOR, :QUARTER_M].astype(f32)
        prior_ref[DH // 2 :, lanes] = half_ref[begin : begin + PRIOR, QUARTER_M:].astype(f32)
        outputs = half_ref[begin + PRIOR : begin + SUM_ROWS, :]
        columns = place(number, CHUNK)
        part = mm(outputs, scaled_hi[:, columns], NT) + mm(outputs, scaled_lo[:, columns], NT)
        product = part if product is None else product + part
    return product


def refit_kernel(
    power_in, weight_ref, factor_ref, scaled_hi, scaled_lo, own_ref, half_ref,
    value_out, both_ref, prior_ref,
):
    me, core, bit = bits()
    product = right_side(own_ref, core, bit, scaled_hi, scaled_lo, prior_ref)
    product = product + right_side(half_ref, 1 - core, bit, scaled_hi, scaled_lo, prior_ref)
    ridge, bound = factor_ref[0:1, :1], factor_ref[1:2, :1]
    both_ref[DH:, :] = power_in[...]
    both_ref[:DH, :] = (weight_ref[...] * product + ridge * prior_ref[...]) * (1.0 / bound)
    above = DH + HALF_M

    def newton_step(number, carry):
        high, low = split(both_ref[...])
        power = (high[DH:], low[DH:])
        top = 2.0 * both_ref[:above, :] - mm3((high[:above], low[:above]), power, NN)
        corner = mm3((high[above:], low[above:]), (power[0][:, HALF_M:], power[1][:, HALF_M:]), NN)
        both_ref[above:, HALF_M:] = 2.0 * both_ref[above:, HALF_M:] - corner
        both_ref[above:, :HALF_M] = top[DH:, HALF_M:].T
        both_ref[:above, :] = top
        return carry

    lax.fori_loop(0, NS_ITERS - 2, newton_step, 0)
    power = split(both_ref[DH:, :])
    refit = both_ref[:DH, :]
    refit = 2.0 * refit - mm3(split(refit), power, NN)
    once = mm3(split(refit), power, NN)
    refit = 2.0 * (refit - once) + mm3(split(once), power, NN)
    value_out[...] = refit.T


def shape(rows, columns, dtype):
    return jax.ShapeDtypeStruct((rows, columns), dtype)


def call(kernel, outs, arrays, scalars=0, scratch=(), in_specs=None, flops=None, limit=48):
    return pl.pallas_call(
        kernel,
        out_shape=tuple(outs),
        in_specs=in_specs
        or [pl.BlockSpec(memory_space=pltpu.SMEM)] * scalars
        + [pl.BlockSpec(memory_space=pltpu.VMEM)] * (len(arrays) - scalars),
        out_specs=tuple([pl.BlockSpec(memory_space=pltpu.VMEM)] * len(outs)),
        scratch_shapes=list(scratch),
        compiler_params=pltpu.CompilerParams(vmem_limit_bytes=int(limit * 1024 * 1024)),
        cost_estimate=None
        if flops is None
        else pl.CostEstimate(flops=flops, bytes_accessed=1024, transcendentals=0),
    )(*arrays)


def per_device(key_mant, scale_exp, values, queries, compact_index, shard_lengths):
    wide_count = lax.axis_size("wide")
    ctx = key_mant.shape[0]

    def exchanged(array, mask):
        return lax.ppermute(array, "wide", [(i, i ^ mask) for i in range(wide_count)])

    head_shape = shape(HEAD_ROWS, CHUNK, bf16)
    scale_shape = shape(CHUNKS, CHUNK, f32)
    half_sum = shape(PAIR_ROWS, 2 * CHUNK, bf16)
    pieces = (shape(PIECE_ROWS, CHUNK, bf16),) * 2

    send_head, head, send, keep = call(
        attention_kernel,
        (head_shape, head_shape, half_sum, half_sum),
        [
            pltpu.with_memory_space_constraint(array, pltpu.HBM)
            for array in (
                shard_lengths, scale_exp, compact_index.reshape(1, M), key_mant, values, queries
            )
        ],
        in_specs=[pl.BlockSpec(memory_space=pltpu.HBM)] * 6,
        flops=10**9,
        scratch=[
            pltpu.VMEM((2 * CHUNKS, CHUNK), f32),
            pltpu.SMEM(shard_lengths.shape, jnp.int32),
            pltpu.SMEM(scale_exp.shape, jnp.int32),
            pltpu.VMEM((1, M), jnp.int32),
            pltpu.VMEM((ctx, DH), bf16),
            pltpu.VMEM((ctx, DH), bf16),
            pltpu.VMEM((NQ, DH), bf16),
            pltpu.VMEM((ctx, DH), bf16),
            pltpu.SemaphoreType.DMA((6,)),
        ],
    )
    def both_exchanged(arrays, mask):
        return tuple(exchanged(array, mask) for array in arrays)

    def joined(*arrays):
        head, *scales = call(join_kernel, (head_shape, scale_shape, scale_shape), arrays)
        return head, tuple(scales)

    got = exchanged(send, 1)
    head, scales = joined(head, exchanged(send_head, 1))
    got_head = exchanged(head, 2)
    first, second, keep = call(
        halve_sum_kernel,
        pieces + (shape(PAIR_ROWS, CHUNK, bf16),),
        scales + (keep, got),
        flops=SUM_FLOPS,
    )
    sums, got = (keep,), both_exchanged((first, second), 2)
    mask = 4
    while mask < wide_count:
        head, scales = joined(head, got_head, first)
        got_head = exchanged(head, mask)
        sums = call(join_sum_kernel, pieces, scales + sums + got, flops=SUM_FLOPS)
        first = sums[0]
        got = both_exchanged(sums, mask)
        mask *= 2
    keys, stats, *scales = call(
        last_join_kernel,
        (shape(HALF_M, DH, bf16), shape(2 * CHUNKS, CHUNK, f32), scale_shape, scale_shape),
        (head, got_head, first),
    )
    got_keys = exchanged(keys, 1)
    gram, linear, norm, scaled_hi, scaled_lo = call(
        feature_kernel,
        (shape(M, M, f32), shape(M, DH, f32), shape(8, DH, f32)) + (shape(M, NQ, bf16),) * 2,
        (shard_lengths, queries, stats, keys, got_keys),
        scalars=1,
        flops=1000000000,
        scratch=[pltpu.VMEM((M, DH), bf16), pltpu.VMEM((M, NQ), bf16), pltpu.VMEM((M, NQ), bf16)],
    )
    outputs = call(outputs_kernel, pieces, (*scales, stats, *sums, *got, norm))
    side = both_exchanged(outputs, 2)
    weights, factor, power = call(
        weight_kernel,
        (shape(1, M, f32), shape(8, DH, f32), shape(M, M, f32)),
        (gram, linear, norm, scaled_hi, scaled_lo),
        flops=5 * 10**9,
        scratch=[pltpu.VMEM((M, M), f32)],
    )
    (half,) = call(
        forward_kernel,
        (shape(2 * SUM_ROWS, CHUNK, bf16),),
        tuple(outputs) + side + (factor,),
    )
    (compact_values,) = call(
        refit_kernel,
        (shape(M, DH, f32),),
        (power, weights, factor, scaled_hi, scaled_lo, half, exchanged(half, 1)),
        scratch=[
            pltpu.VMEM((M + DH, M), f32),
            pltpu.VMEM((DH, M), f32),
        ],
    )
    return weights.reshape(M), compact_values


def solution(mesh):
    placed = (
        P(("groups", "wide"), None),
        P(("groups", "wide")),
        P(("groups", "wide"), None),
        P("groups", None),
        P("groups"),
        P("groups"),
    )
    return jax.shard_map(
        per_device,
        mesh=mesh,
        in_specs=placed,
        out_specs=(P("groups"), P("groups", None)),
        check_vma=False,
    )
```

```python
import jax
import jax.numpy as jnp
from jax import lax
from jax.experimental import pallas as pl
from jax.experimental.pallas import tpu as pltpu
from jax.sharding import PartitionSpec as P

DH = 128
NQ = 1024
M = 512
QB = 32
SELECT_FROM = 256
NNLS_STEPS = 8
NS_ITERS = 9
EARLY_STEPS = 4
LATE_STEPS = 2
SUM_FLOPS = 10**9
CHUNKS = 4
CHUNK = NQ // CHUNKS
QUARTER_M = M // CHUNKS
SUM_ROWS = DH + QUARTER_M // 2
PAIR_ROWS = SUM_ROWS + DH
HALF_M = M // 2

ridge_weight = 4.0
nnls_ridge = 0.1
floor_value = -1e30
EXP2_SCALE = DH ** (-0.5) * 1.4426950408889634

f32 = jnp.float32
bf16 = jnp.bfloat16
NN = (((1,), (0,)), ((), ()))
NT = (((1,), (1,)), ((), ()))
TN = (((0,), (0,)), ((), ()))


def mm(left, right, dims):
    return lax.dot_general(left, right, dims, preferred_element_type=f32)


def split(x):
    high = x.astype(bf16)
    return high, (x - high.astype(f32)).astype(bf16)


def mm3(left, right, dims):
    return mm(left[0], right[0], dims) + (mm(left[0], right[1], dims) + mm(left[1], right[0], dims))


def total_of(x):
    return jnp.sum(jnp.sum(x, axis=0, keepdims=True), axis=1, keepdims=True)


def place(number, size):
    return pl.ds(pl.multiple_of(number * size, size), size)


def bits():
    me = lax.axis_index("wide")
    return me, lax.rem(me, 2), lax.rem(lax.div(me, 2), 2)


PRIOR = SUM_ROWS - DH
PIECE_ROWS = SUM_ROWS // 2
EVERYTHING = slice(0, CHUNK)


def put_pair(out_ref, columns, prior, sums):
    high, low = split(sums)
    out_ref[:PRIOR, columns] = prior
    out_ref[PRIOR:SUM_ROWS, columns] = high
    out_ref[SUM_ROWS:, columns] = low


def get_pair(ref, columns):
    high = ref[PRIOR:SUM_ROWS, columns].astype(f32)
    return ref[:PRIOR, columns], high + ref[SUM_ROWS:, columns].astype(f32)


def put_pieces(first_ref, second_ref, prior, sums):
    sums = sums.astype(bf16)
    first_ref[:PRIOR, :] = prior
    first_ref[PRIOR:, :] = sums[: PIECE_ROWS - PRIOR]
    second_ref[...] = sums[PIECE_ROWS - PRIOR :]


def get_pieces(first_ref, second_ref):
    sums = jnp.concatenate([first_ref[PRIOR:, :], second_ref[...]], axis=0)
    return first_ref[:PRIOR, :], sums.astype(f32)


KEY_ROWS = HALF_M // 2
HEAD_ROWS = KEY_ROWS + 32


def put_keys(out_ref, keys):
    out_ref[:KEY_ROWS, :DH] = keys[:KEY_ROWS]
    out_ref[:KEY_ROWS, DH:] = keys[KEY_ROWS:]


def put_stats(out_ref, stats):
    high = stats.astype(bf16).astype(f32)
    middle = (stats - high).astype(bf16).astype(f32)
    low = stats - high - middle
    out_ref[KEY_ROWS:, :] = jnp.concatenate([high, middle, low, jnp.zeros_like(low)], axis=0).astype(bf16)


def get_stats(ref):
    parts = ref[KEY_ROWS:, :].astype(f32)
    return parts[:8] + parts[8:16] + parts[16:24]


def attention_kernel(
    len_hbm, exp_hbm, index_hbm, mant_hbm, value_hbm, query_hbm,
    send_head_ref, keep_head_ref, send_ref, keep_ref,
    stat_ref, len_ref, exp_ref, index_ref, mant_ref, value_ref, query_ref, key_ref, attn_ref, sems,
):
    copies = [
        pltpu.make_async_copy(source, target, sems.at[i])
        for i, (source, target) in enumerate(
            (
                (exp_hbm, exp_ref),
                (mant_hbm, mant_ref),
                (query_hbm, query_ref),
                (len_hbm, len_ref),
                (index_hbm, index_ref),
                (value_hbm, value_ref),
            )
        )
    ]
    for copy in copies:
        copy.start()
    ctx = mant_ref.shape[0]
    me, core, bit = bits()
    for copy in copies:
        copy.wait()
    for b in range(ctx // QB):
        exponent = exp_ref[b]
        factor = jnp.where(exponent > 0, 2.0, jnp.where(exponent < 0, 0.5, 1.0)).astype(f32)
        rows = pl.ds(b * QB, QB)
        key_ref[rows, :] = (mant_ref[rows, :].astype(f32) * factor).astype(bf16)
    half_m = M // 2
    position = lax.broadcasted_iota(jnp.int32, (SELECT_FROM, half_m), 0)
    for half, head_out, out in ((1 - core, send_head_ref, send_ref), (core, keep_head_ref, keep_ref)):
        wanted = index_ref[:, place(half, half_m)] - me * ctx
        chosen = jnp.where(position == wanted, 1.0, 0.0).astype(bf16)
        put_keys(head_out, mm(chosen, key_ref[:SELECT_FROM, :], TN).astype(bf16))
        prior = mm(value_ref[:SELECT_FROM, :], chosen, TN).astype(bf16)
        for piece in range(2):
            for part in range(2):
                begin = piece * CHUNK + part * QUARTER_M
                out[:PRIOR, begin : begin + QUARTER_M] = prior[
                    part * (DH // 2) : (part + 1) * (DH // 2), piece * QUARTER_M : (piece + 1) * QUARTER_M
                ]
    dead = lax.broadcasted_iota(jnp.int32, (ctx, CHUNK), 0) >= len_ref[me]
    for half, out in ((1 - core, send_ref), (core, keep_ref)):
        for c in range(2):
            number = half * 2 + c
            scores = mm(key_ref[...], query_ref[place(number, CHUNK), :], NT)
            scores = jnp.where(dead, floor_value, scores)
            row_max = jnp.max(scores, axis=0, keepdims=True)
            attn = jnp.exp2((scores - row_max) * EXP2_SCALE)
            stat_ref[pl.ds(number, 1), :] = row_max
            stat_ref[pl.ds(CHUNKS + number, 1), :] = jnp.sum(attn, axis=0, keepdims=True)
            attn_ref[:, c * CHUNK : (c + 1) * CHUNK] = attn.astype(bf16)
        high, low = split(mm(value_ref[...], attn_ref[...], TN))
        out[PRIOR:SUM_ROWS, :] = high
        out[SUM_ROWS:, :] = low
    put_stats(send_head_ref, stat_ref[...])
    put_stats(keep_head_ref, stat_ref[...])


def joined_stats(first_ref, second_ref, scale_first_out, scale_second_out):
    first, second = get_stats(first_ref), get_stats(second_ref)
    joint = jnp.maximum(first[:CHUNKS], second[:CHUNKS])
    scale_first = jnp.exp2((first[:CHUNKS] - joint) * EXP2_SCALE)
    scale_second = jnp.exp2((second[:CHUNKS] - joint) * EXP2_SCALE)
    scale_first_out[...] = scale_first
    scale_second_out[...] = scale_second
    mass = first[CHUNKS:] * scale_first + second[CHUNKS:] * scale_second
    return jnp.concatenate([joint, mass], axis=0)


def join_kernel(first_ref, second_ref, *refs):
    out_ref, scale_first_out, scale_second_out = refs[-3:]
    put_stats(out_ref, joined_stats(first_ref, second_ref, scale_first_out, scale_second_out))
    out_ref[:KEY_ROWS, :] = first_ref[:KEY_ROWS, :] + second_ref[:KEY_ROWS, :]


def last_join_kernel(first_ref, second_ref, after_ref, key_out, stat_out, scale_first_out, scale_second_out):
    stat_out[...] = joined_stats(first_ref, second_ref, scale_first_out, scale_second_out)
    for c in range(2):
        columns = slice(c * DH, (c + 1) * DH)
        rows = slice(c * KEY_ROWS, (c + 1) * KEY_ROWS)
        key_out[rows, :] = first_ref[:KEY_ROWS, columns] + second_ref[:KEY_ROWS, columns]


def halve_sum_kernel(scale_a, scale_b, sum_a, sum_b, first_out, second_out, keep_out):
    me, core, bit = bits()

    def half_of(half):
        columns = place(half, CHUNK)
        row = pl.ds(core * 2 + half, 1)
        prior_a, sums_a = get_pair(sum_a, columns)
        prior_b, sums_b = get_pair(sum_b, columns)
        return prior_a + prior_b, sums_a * scale_a[row, :] + sums_b * scale_b[row, :]

    put_pieces(first_out, second_out, *half_of(1 - bit))
    put_pair(keep_out, EVERYTHING, *half_of(bit))


def joined_sums(scale_a, scale_b, own, got):
    me, core, bit = bits()
    row = pl.ds(core * 2 + bit, 1)
    prior_a, sums_a = get_pair(own[0], EVERYTHING) if len(own) == 1 else get_pieces(*own)
    prior_b, sums_b = get_pieces(*got)
    return prior_a + prior_b, sums_a * scale_a[row, :] + sums_b * scale_b[row, :]


def join_sum_kernel(scale_a, scale_b, *refs):
    put_pieces(*refs[-2:], *joined_sums(scale_a, scale_b, refs[:-4], refs[-4:-2]))


def outputs_kernel(
    scale_a, scale_b, stat_ref, first_a, second_a, first_b, second_b, after_ref, first_out, second_out
):
    me, core, bit = bits()
    prior, sums = joined_sums(scale_a, scale_b, (first_a, second_a), (first_b, second_b))
    put_pieces(first_out, second_out, prior, sums / stat_ref[pl.ds(CHUNKS + core * 2 + bit, 1), :])


def gram3(high, low):
    top = mm3((high[:HALF_M], low[:HALF_M]), (high, low), NT)
    corner = mm3((high[HALF_M:], low[HALF_M:]), (high[HALF_M:], low[HALF_M:]), NT)
    return top, jnp.concatenate([top[:, HALF_M:].T, corner], axis=1)


def feature_kernel(
    len_ref, query_ref, stat_ref, own_key_ref, other_key_ref,
    gram_ref, linear_ref, norm_ref, scaled_hi, scaled_lo,
    key_ref, feat_hi, feat_lo,
):
    me, core, bit = bits()
    total = len_ref[0]
    for i in range(1, len_ref.shape[0]):
        total = total + len_ref[i]
    live_total = jnp.full((1, 1), total, jnp.int32).astype(f32)
    key_ref[place(core, M // 2), :] = own_key_ref[...]
    key_ref[place(1 - core, M // 2), :] = other_key_ref[...]
    frobenius = jnp.zeros((1, 1), f32)
    linear = jnp.zeros((M, DH), f32)
    for c in range(CHUNKS):
        columns = pl.ds(c * CHUNK, CHUNK)
        row_max, row_mass = stat_ref[c : c + 1, :], stat_ref[CHUNKS + c : CHUNKS + c + 1, :]
        scores = mm(key_ref[...], query_ref[columns, :], NT)
        features = jnp.exp2((scores - row_max) * EXP2_SCALE)
        target = row_mass * (M / live_total)
        high, low = split(features)
        feat_hi[:, columns] = high
        feat_lo[:, columns] = low
        frobenius = frobenius + total_of(features * features)
        weighted = features * target
        for tile in range(CHUNK // DH):
            linear = linear + weighted[:, tile * DH : (tile + 1) * DH]
        high, low = split(features * (1.0 / target))
        scaled_hi[:, columns] = high
        scaled_lo[:, columns] = low
    gram_ref[:HALF_M, :], gram_ref[HALF_M:, :] = gram3(feat_hi[...], feat_lo[...])
    linear_ref[...] = jnp.broadcast_to(jnp.sum(linear, axis=1, keepdims=True), (M, DH))
    norm_ref[...] = jnp.broadcast_to(frobenius, norm_ref.shape)


def weight_kernel(
    gram_ref, linear_ref, norm_ref, scaled_hi, scaled_lo,
    weight_out, factor_out, power_out, attend_ref,
):
    frobenius = norm_ref[:1, :1]
    damping = nnls_ridge * (frobenius / M + 1e-6)
    stepsize = 1.0 / (frobenius + damping)
    linear_column = linear_ref[...]
    linear_row = linear_column.T[:1]
    row = jnp.ones((1, M), f32)
    column = jnp.ones((M, DH), f32)
    tiles = [slice(t * DH, (t + 1) * DH) for t in range(M // DH)]

    def moved(weights, product, linear):
        gradient = product - linear + damping * weights
        return jnp.maximum(weights - stepsize * gradient, 0.0)

    for number in range(NNLS_STEPS):
        down = [jnp.sum(gram_ref[:, t] * column, axis=0, keepdims=True) for t in tiles]
        along = gram_ref[:, tiles[0]] * row[:, tiles[0]]
        for t in tiles[1:]:
            along = along + gram_ref[:, t] * row[:, t]
        along = jnp.broadcast_to(jnp.sum(along, axis=1, keepdims=True), (M, DH))
        row = moved(row, jnp.concatenate(down, axis=1), linear_row)
        column = moved(column, along, linear_column)
        if number % 2 == 0 and number // 2 < CHUNKS:
            columns = pl.ds(number // 2 * CHUNK, CHUNK)
            top, corner = gram3(scaled_hi[:, columns], scaled_lo[:, columns])
            attend_ref[:HALF_M, :] = top if number == 0 else attend_ref[:HALF_M, :] + top
            attend_ref[HALF_M:, :] = corner if number == 0 else attend_ref[HALF_M:, :] + corner
    weight_out[...] = row
    gram = attend_ref[...] * row
    gram = gram * jnp.concatenate([column] * (M // DH), axis=1)
    diagonal = lax.broadcasted_iota(jnp.int32, (M, M), 0) == lax.broadcasted_iota(
        jnp.int32, (M, M), 1
    )
    ridge = ridge_weight * (total_of(jnp.where(diagonal, gram, 0.0)) / M + 1e-6)
    system = gram + jnp.where(diagonal, ridge, 0.0)
    bound = jnp.max(jnp.sum(jnp.abs(system), axis=0, keepdims=True), axis=1, keepdims=True)
    number = lax.broadcasted_iota(jnp.int32, factor_out.shape, 0)
    factor_out[...] = jnp.where(number == 0, ridge, jnp.where(number == 1, bound, row))
    power_out[...] = system * (1.0 / bound)


def forward_kernel(own_first, own_second, side_first, side_second, after_ref, out_ref):
    for i, ref in enumerate((own_first, own_second, side_first, side_second)):
        out_ref[i * PIECE_ROWS : (i + 1) * PIECE_ROWS, :] = ref[...]


def right_side(half_ref, half, bit, scaled_hi, scaled_lo, prior_ref):
    product = None
    for i, lo_bit in enumerate((bit, 1 - bit)):
        number = half * 2 + lo_bit
        begin = i * SUM_ROWS
        lanes = place(number, QUARTER_M)
        prior_ref[: DH // 2, lanes] = half_ref[begin : begin + PRIOR, :QUARTER_M].astype(f32)
        prior_ref[DH // 2 :, lanes] = half_ref[begin : begin + PRIOR, QUARTER_M:].astype(f32)
        outputs = half_ref[begin + PRIOR : begin + SUM_ROWS, :]
        columns = place(number, CHUNK)
        part = mm(outputs, scaled_hi[:, columns], NT) + mm(outputs, scaled_lo[:, columns], NT)
        product = part if product is None else product + part
    return product


def squared(power, pair):
    high, low = pair
    top = 2.0 * power[:HALF_M] - mm3((high[:HALF_M], low[:HALF_M]), pair, NN)
    corner = mm3((high[HALF_M:], low[HALF_M:]), (high[:, HALF_M:], low[:, HALF_M:]), NN)
    corner = 2.0 * power[HALF_M:, HALF_M:] - corner
    return top, jnp.concatenate([top[:, HALF_M:].T, corner], axis=1)


def times_power(refit, high, low):
    rows = refit.shape[0]
    pair = jnp.concatenate(split(refit), axis=0)
    by_high = mm(pair, high, NN)
    return by_high[:rows] + (by_high[rows:] + mm(pair[:rows], low, NN))


def power_kernel(power_in, after_ref, high_out, low_out, power_out):
    power_out[...] = power_in[...]

    def step(number, carry):
        pair = split(power_out[...])
        high_out[place(number, M), :], low_out[place(number, M), :] = pair
        power_out[:HALF_M, :], power_out[HALF_M:, :] = squared(power_out[...], pair)
        return carry

    lax.fori_loop(0, high_out.shape[0] // M, step, 0)


def refit_kernel(
    early_hi, early_lo, late_hi, late_lo, power_in, factor_ref, scaled_hi, scaled_lo, own_ref, half_ref,
    value_out, both_ref, prior_ref,
):
    me, core, bit = bits()
    product = right_side(own_ref, core, bit, scaled_hi, scaled_lo, prior_ref)
    product = product + right_side(half_ref, 1 - core, bit, scaled_hi, scaled_lo, prior_ref)
    ridge, bound, weights = factor_ref[0:1, :1], factor_ref[1:2, :1], factor_ref[2:3, :]
    refit = (weights * product + ridge * prior_ref[...]) * (1.0 / bound)
    for high, low in ((early_hi, early_lo), (late_hi, late_lo)):
        for begin in range(0, high.shape[0], M):
            rows = slice(begin, begin + M)
            refit = 2.0 * refit - times_power(refit, high[rows, :], low[rows, :])
    both_ref[DH:, :] = power_in[...]
    both_ref[:DH, :] = refit
    above = DH + HALF_M

    def newton_step(number, carry):
        high, low = split(both_ref[...])
        power = (high[DH:], low[DH:])
        top = 2.0 * both_ref[:above, :] - mm3((high[:above], low[:above]), power, NN)
        corner = mm3((high[above:], low[above:]), (power[0][:, HALF_M:], power[1][:, HALF_M:]), NN)
        both_ref[above:, HALF_M:] = 2.0 * both_ref[above:, HALF_M:] - corner
        both_ref[above:, :HALF_M] = top[DH:, HALF_M:].T
        both_ref[:above, :] = top
        return carry

    lax.fori_loop(EARLY_STEPS + LATE_STEPS, NS_ITERS - 2, newton_step, 0)
    power = split(both_ref[DH:, :])
    refit = both_ref[:DH, :]
    refit = 2.0 * refit - times_power(refit, *power)
    once = times_power(refit, *power)
    refit = 2.0 * (refit - once) + times_power(once, *power)
    value_out[...] = refit.T


def shape(rows, columns, dtype):
    return jax.ShapeDtypeStruct((rows, columns), dtype)


def call(kernel, outs, arrays, scalars=0, scratch=(), in_specs=None, flops=None, limit=38):
    return pl.pallas_call(
        kernel,
        out_shape=tuple(outs),
        in_specs=in_specs
        or [pl.BlockSpec(memory_space=pltpu.SMEM)] * scalars
        + [pl.BlockSpec(memory_space=pltpu.VMEM)] * (len(arrays) - scalars),
        out_specs=tuple([pl.BlockSpec(memory_space=pltpu.VMEM)] * len(outs)),
        scratch_shapes=list(scratch),
        compiler_params=pltpu.CompilerParams(vmem_limit_bytes=int(limit * 1024 * 1024)),
        cost_estimate=None
        if flops is None
        else pl.CostEstimate(flops=flops, bytes_accessed=1024, transcendentals=0),
    )(*arrays)


def per_device(key_mant, scale_exp, values, queries, compact_index, shard_lengths):
    wide_count = lax.axis_size("wide")
    ctx = key_mant.shape[0]

    def exchanged(array, mask):
        return lax.ppermute(array, "wide", [(i, i ^ mask) for i in range(wide_count)])

    head_shape = shape(HEAD_ROWS, CHUNK, bf16)
    scale_shape = shape(CHUNKS, CHUNK, f32)
    half_sum = shape(PAIR_ROWS, 2 * CHUNK, bf16)
    pieces = (shape(PIECE_ROWS, CHUNK, bf16),) * 2

    send_head, head, send, keep = call(
        attention_kernel,
        (head_shape, head_shape, half_sum, half_sum),
        [
            pltpu.with_memory_space_constraint(array, pltpu.HBM)
            for array in (
                shard_lengths, scale_exp, compact_index.reshape(1, M), key_mant, values, queries
            )
        ],
        in_specs=[pl.BlockSpec(memory_space=pltpu.HBM)] * 6,
        flops=10**9,
        scratch=[
            pltpu.VMEM((2 * CHUNKS, CHUNK), f32),
            pltpu.SMEM(shard_lengths.shape, jnp.int32),
            pltpu.SMEM(scale_exp.shape, jnp.int32),
            pltpu.VMEM((1, M), jnp.int32),
            pltpu.VMEM((ctx, DH), bf16),
            pltpu.VMEM((ctx, DH), bf16),
            pltpu.VMEM((NQ, DH), bf16),
            pltpu.VMEM((ctx, DH), bf16),
            pltpu.VMEM((ctx, 2 * CHUNK), bf16),
            pltpu.SemaphoreType.DMA((6,)),
        ],
    )
    def both_exchanged(arrays, mask):
        return tuple(exchanged(array, mask) for array in arrays)

    def joined(*arrays):
        head, *scales = call(join_kernel, (head_shape, scale_shape, scale_shape), arrays)
        return head, tuple(scales)

    got = exchanged(send, 1)
    head, scales = joined(head, exchanged(send_head, 1))
    got_head = exchanged(head, 2)
    first, second, keep = call(
        halve_sum_kernel,
        pieces + (shape(PAIR_ROWS, CHUNK, bf16),),
        scales + (keep, got),
        flops=SUM_FLOPS,
    )
    sums, got = (keep,), both_exchanged((first, second), 2)
    mask = 4
    while mask < wide_count:
        head, scales = joined(head, got_head, first)
        got_head = exchanged(head, mask)
        sums = call(join_sum_kernel, pieces, scales + sums + got, flops=SUM_FLOPS)
        first = sums[0]
        got = both_exchanged(sums, mask)
        mask *= 2
    keys, stats, *scales = call(
        last_join_kernel,
        (shape(HALF_M, DH, bf16), shape(2 * CHUNKS, CHUNK, f32), scale_shape, scale_shape),
        (head, got_head, first),
    )
    got_keys = exchanged(keys, 1)
    gram, linear, norm, scaled_hi, scaled_lo = call(
        feature_kernel,
        (shape(M, M, f32), shape(M, DH, f32), shape(8, DH, f32)) + (shape(M, NQ, bf16),) * 2,
        (shard_lengths, queries, stats, keys, got_keys),
        scalars=1,
        flops=1000000000,
        scratch=[pltpu.VMEM((M, DH), bf16), pltpu.VMEM((M, NQ), bf16), pltpu.VMEM((M, NQ), bf16)],
    )
    weights, factor, power = call(
        weight_kernel,
        (shape(1, M, f32), shape(8, M, f32), shape(M, M, f32)),
        (gram, linear, norm, scaled_hi, scaled_lo),
        flops=5 * 10**9,
        scratch=[pltpu.VMEM((M, M), f32)],
    )
    outputs = call(outputs_kernel, pieces, (*scales, stats, *sums, *got, factor))
    side = both_exchanged(outputs, 2)

    def powers(power, after, steps):
        pairs = (shape(steps * M, M, bf16),) * 2
        return call(power_kernel, pairs + (shape(M, M, f32),), (power, after), flops=steps * 10**9)

    early_hi, early_lo, power = powers(power, outputs[0], EARLY_STEPS)
    (half,) = call(
        forward_kernel,
        (shape(2 * SUM_ROWS, CHUNK, bf16),),
        tuple(outputs) + side + (power,),
    )
    other = exchanged(half, 1)
    late_hi, late_lo, power = powers(power, half, LATE_STEPS)
    (compact_values,) = call(
        refit_kernel,
        (shape(M, DH, f32),),
        (early_hi, early_lo, late_hi, late_lo, power, factor, scaled_hi, scaled_lo, half, other),
        scratch=[pltpu.VMEM((M + DH, M), f32), pltpu.VMEM((DH, M), f32)],
    )
    return weights.reshape(M), compact_values


def solution(mesh):
    placed = (
        P(("groups", "wide"), None),
        P(("groups", "wide")),
        P(("groups", "wide"), None),
        P("groups", None),
        P("groups"),
        P("groups"),
    )
    return jax.shard_map(
        per_device,
        mesh=mesh,
        in_specs=placed,
        out_specs=(P("groups"), P("groups", None)),
        check_vma=False,
    )
```

```python
import jax
import jax.numpy as jnp
from jax import lax
from jax.experimental import pallas as pl
from jax.experimental.pallas import tpu as pltpu
from jax.sharding import PartitionSpec as P

DH = 128
NQ = 1024
M = 512
QB = 32
SELECT_FROM = 256
NNLS_STEPS = 8
NS_ITERS = 9
EARLY_STEPS = 4
LATE_STEPS = 2
SUM_FLOPS = 10**9
CHUNKS = 4
CHUNK = NQ // CHUNKS
QUARTER_M = M // CHUNKS
SUM_ROWS = DH + QUARTER_M // 2
PAIR_ROWS = SUM_ROWS + DH
HALF_M = M // 2

ridge_weight = 4.0
nnls_ridge = 0.1
floor_value = -1e30
EXP2_SCALE = DH ** (-0.5) * 1.4426950408889634

f32 = jnp.float32
bf16 = jnp.bfloat16
NN = (((1,), (0,)), ((), ()))
NT = (((1,), (1,)), ((), ()))
TN = (((0,), (0,)), ((), ()))


def mm(left, right, dims):
    return lax.dot_general(left, right, dims, preferred_element_type=f32)


def split(x):
    high = x.astype(bf16)
    return high, (x - high.astype(f32)).astype(bf16)


def mm3(left, right, dims):
    return mm(left[0], right[0], dims) + (mm(left[0], right[1], dims) + mm(left[1], right[0], dims))


def total_of(x):
    return jnp.sum(jnp.sum(x, axis=0, keepdims=True), axis=1, keepdims=True)


def place(number, size):
    return pl.ds(pl.multiple_of(number * size, size), size)


def bits():
    me = lax.axis_index("wide")
    return me, lax.rem(me, 2), lax.rem(lax.div(me, 2), 2)


PRIOR = SUM_ROWS - DH
PIECE_ROWS = SUM_ROWS // 2
EVERYTHING = slice(0, CHUNK)


def put_pair(out_ref, columns, prior, sums):
    high, low = split(sums)
    out_ref[:PRIOR, columns] = prior
    out_ref[PRIOR:SUM_ROWS, columns] = high
    out_ref[SUM_ROWS:, columns] = low


def get_pair(ref, columns):
    high = ref[PRIOR:SUM_ROWS, columns].astype(f32)
    return ref[:PRIOR, columns], high + ref[SUM_ROWS:, columns].astype(f32)


def put_pieces(first_ref, second_ref, prior, sums):
    sums = sums.astype(bf16)
    first_ref[:PRIOR, :] = prior
    first_ref[PRIOR:, :] = sums[: PIECE_ROWS - PRIOR]
    second_ref[...] = sums[PIECE_ROWS - PRIOR :]


def get_pieces(first_ref, second_ref):
    sums = jnp.concatenate([first_ref[PRIOR:, :], second_ref[...]], axis=0)
    return first_ref[:PRIOR, :], sums.astype(f32)


KEY_ROWS = HALF_M // 2
HEAD_ROWS = KEY_ROWS + 32


def put_keys(out_ref, keys):
    out_ref[:KEY_ROWS, :DH] = keys[:KEY_ROWS]
    out_ref[:KEY_ROWS, DH:] = keys[KEY_ROWS:]


def put_stats(out_ref, stats):
    high = stats.astype(bf16).astype(f32)
    middle = (stats - high).astype(bf16).astype(f32)
    low = stats - high - middle
    out_ref[KEY_ROWS:, :] = jnp.concatenate([high, middle, low, jnp.zeros_like(low)], axis=0).astype(bf16)


def get_stats(ref):
    parts = ref[KEY_ROWS:, :].astype(f32)
    return parts[:8] + parts[8:16] + parts[16:24]


def attention_kernel(
    len_hbm, exp_hbm, index_hbm, mant_hbm, value_hbm, query_hbm,
    send_head_ref, keep_head_ref, send_ref, keep_ref,
    stat_ref, len_ref, exp_ref, index_ref, mant_ref, value_ref, query_ref, key_ref, attn_ref, sems,
):
    copies = [
        pltpu.make_async_copy(source, target, sems.at[i])
        for i, (source, target) in enumerate(
            (
                (exp_hbm, exp_ref),
                (mant_hbm, mant_ref),
                (query_hbm, query_ref),
                (len_hbm, len_ref),
                (index_hbm, index_ref),
                (value_hbm, value_ref),
            )
        )
    ]
    for copy in copies:
        copy.start()
    ctx = mant_ref.shape[0]
    me, core, bit = bits()
    for copy in copies:
        copy.wait()
    for b in range(ctx // QB):
        exponent = exp_ref[b]
        factor = jnp.where(exponent > 0, 2.0, jnp.where(exponent < 0, 0.5, 1.0)).astype(f32)
        rows = pl.ds(b * QB, QB)
        key_ref[rows, :] = (mant_ref[rows, :].astype(f32) * factor).astype(bf16)
    half_m = M // 2
    position = lax.broadcasted_iota(jnp.int32, (SELECT_FROM, half_m), 0)
    for half, head_out, out in ((1 - core, send_head_ref, send_ref), (core, keep_head_ref, keep_ref)):
        wanted = index_ref[:, place(half, half_m)] - me * ctx
        chosen = jnp.where(position == wanted, 1.0, 0.0).astype(bf16)
        put_keys(head_out, mm(chosen, key_ref[:SELECT_FROM, :], TN).astype(bf16))
        prior = mm(value_ref[:SELECT_FROM, :], chosen, TN).astype(bf16)
        for piece in range(2):
            for part in range(2):
                begin = piece * CHUNK + part * QUARTER_M
                out[:PRIOR, begin : begin + QUARTER_M] = prior[
                    part * (DH // 2) : (part + 1) * (DH // 2), piece * QUARTER_M : (piece + 1) * QUARTER_M
                ]
    dead = lax.broadcasted_iota(jnp.int32, (ctx, CHUNK), 0) >= len_ref[me]
    for half, out in ((1 - core, send_ref), (core, keep_ref)):
        for c in range(2):
            number = half * 2 + c
            scores = mm(key_ref[...], query_ref[place(number, CHUNK), :], NT)
            scores = jnp.where(dead, floor_value, scores)
            row_max = jnp.max(scores, axis=0, keepdims=True)
            attn = jnp.exp2((scores - row_max) * EXP2_SCALE)
            stat_ref[pl.ds(number, 1), :] = row_max
            stat_ref[pl.ds(CHUNKS + number, 1), :] = jnp.sum(attn, axis=0, keepdims=True)
            attn_ref[:, c * CHUNK : (c + 1) * CHUNK] = attn.astype(bf16)
        high, low = split(mm(value_ref[...], attn_ref[...], TN))
        out[PRIOR:SUM_ROWS, :] = high
        out[SUM_ROWS:, :] = low
    put_stats(send_head_ref, stat_ref[...])
    put_stats(keep_head_ref, stat_ref[...])


def joined_stats(first_ref, second_ref, scale_first_out, scale_second_out):
    first, second = get_stats(first_ref), get_stats(second_ref)
    joint = jnp.maximum(first[:CHUNKS], second[:CHUNKS])
    scale_first = jnp.exp2((first[:CHUNKS] - joint) * EXP2_SCALE)
    scale_second = jnp.exp2((second[:CHUNKS] - joint) * EXP2_SCALE)
    scale_first_out[...] = scale_first
    scale_second_out[...] = scale_second
    mass = first[CHUNKS:] * scale_first + second[CHUNKS:] * scale_second
    return jnp.concatenate([joint, mass], axis=0)


def join_kernel(first_ref, second_ref, *refs):
    out_ref, scale_first_out, scale_second_out = refs[-3:]
    put_stats(out_ref, joined_stats(first_ref, second_ref, scale_first_out, scale_second_out))
    out_ref[:KEY_ROWS, :] = first_ref[:KEY_ROWS, :] + second_ref[:KEY_ROWS, :]


def last_join_kernel(first_ref, second_ref, after_ref, key_out, stat_out, scale_first_out, scale_second_out):
    stat_out[...] = joined_stats(first_ref, second_ref, scale_first_out, scale_second_out)
    for c in range(2):
        columns = slice(c * DH, (c + 1) * DH)
        rows = slice(c * KEY_ROWS, (c + 1) * KEY_ROWS)
        key_out[rows, :] = first_ref[:KEY_ROWS, columns] + second_ref[:KEY_ROWS, columns]


def halve_sum_kernel(scale_a, scale_b, sum_a, sum_b, first_out, second_out, keep_out):
    me, core, bit = bits()

    def half_of(half):
        columns = place(half, CHUNK)
        row = pl.ds(core * 2 + half, 1)
        prior_a, sums_a = get_pair(sum_a, columns)
        prior_b, sums_b = get_pair(sum_b, columns)
        return prior_a + prior_b, sums_a * scale_a[row, :] + sums_b * scale_b[row, :]

    put_pieces(first_out, second_out, *half_of(1 - bit))
    put_pair(keep_out, EVERYTHING, *half_of(bit))


def joined_sums(scale_a, scale_b, own, got):
    me, core, bit = bits()
    row = pl.ds(core * 2 + bit, 1)
    prior_a, sums_a = get_pair(own[0], EVERYTHING) if len(own) == 1 else get_pieces(*own)
    prior_b, sums_b = get_pieces(*got)
    return prior_a + prior_b, sums_a * scale_a[row, :] + sums_b * scale_b[row, :]


def join_sum_kernel(scale_a, scale_b, *refs):
    put_pieces(*refs[-2:], *joined_sums(scale_a, scale_b, refs[:-4], refs[-4:-2]))


def last_join_sum_kernel(scale_a, scale_b, *refs):
    out_ref = refs[-1]
    prior, sums = joined_sums(scale_a, scale_b, refs[:-3], refs[-3:-1])
    out_ref[:PRIOR, :] = prior
    out_ref[PRIOR:, :] = sums.astype(bf16)


def outputs_kernel(scale_a, scale_b, stat_ref, sum_a, sum_b, after_ref, out_ref):
    me, core, bit = bits()
    row = pl.ds(core * 2 + bit, 1)
    sums = sum_a[PRIOR:, :].astype(f32) * scale_a[row, :] + sum_b[PRIOR:, :].astype(f32) * scale_b[row, :]
    out_ref[:PRIOR, :] = sum_a[:PRIOR, :] + sum_b[:PRIOR, :]
    out_ref[PRIOR:, :] = (sums / stat_ref[pl.ds(CHUNKS + core * 2 + bit, 1), :]).astype(bf16)


def gram3(high, low):
    top = mm3((high[:HALF_M], low[:HALF_M]), (high, low), NT)
    corner = mm3((high[HALF_M:], low[HALF_M:]), (high[HALF_M:], low[HALF_M:]), NT)
    return top, jnp.concatenate([top[:, HALF_M:].T, corner], axis=1)


def feature_kernel(
    len_ref, query_ref, stat_ref, own_key_ref, other_key_ref,
    gram_ref, linear_ref, norm_ref, scaled_hi, scaled_lo,
    key_ref, feat_hi, feat_lo,
):
    me, core, bit = bits()
    total = len_ref[0]
    for i in range(1, len_ref.shape[0]):
        total = total + len_ref[i]
    live_total = jnp.full((1, 1), total, jnp.int32).astype(f32)
    key_ref[place(core, M // 2), :] = own_key_ref[...]
    key_ref[place(1 - core, M // 2), :] = other_key_ref[...]
    frobenius = jnp.zeros((1, 1), f32)
    linear = jnp.zeros((M, DH), f32)
    for c in range(CHUNKS):
        columns = pl.ds(c * CHUNK, CHUNK)
        row_max, row_mass = stat_ref[c : c + 1, :], stat_ref[CHUNKS + c : CHUNKS + c + 1, :]
        scores = mm(key_ref[...], query_ref[columns, :], NT)
        features = jnp.exp2((scores - row_max) * EXP2_SCALE)
        target = row_mass * (M / live_total)
        top, corner = gram3(*split(features))
        gram_ref[:HALF_M, :] = top if c == 0 else gram_ref[:HALF_M, :] + top
        gram_ref[HALF_M:, :] = corner if c == 0 else gram_ref[HALF_M:, :] + corner
        frobenius = frobenius + total_of(features * features)
        weighted = features * target
        for tile in range(CHUNK // DH):
            linear = linear + weighted[:, tile * DH : (tile + 1) * DH]
        high, low = split(features * (1.0 / target))
        scaled_hi[:, columns] = high
        scaled_lo[:, columns] = low
    linear_ref[...] = jnp.broadcast_to(jnp.sum(linear, axis=1, keepdims=True), (M, DH))
    norm_ref[...] = jnp.broadcast_to(frobenius, norm_ref.shape)


def weight_kernel(
    gram_ref, linear_ref, norm_ref, scaled_hi, scaled_lo,
    weight_out, factor_out, power_out, attend_ref,
):
    frobenius = norm_ref[:1, :1]
    damping = nnls_ridge * (frobenius / M + 1e-6)
    stepsize = 1.0 / (frobenius + damping)
    linear_column = linear_ref[...]
    linear_row = linear_column.T[:1]
    row = jnp.ones((1, M), f32)
    column = jnp.ones((M, DH), f32)
    tiles = [slice(t * DH, (t + 1) * DH) for t in range(M // DH)]

    def moved(weights, product, linear):
        gradient = product - linear + damping * weights
        return jnp.maximum(weights - stepsize * gradient, 0.0)

    for number in range(NNLS_STEPS):
        down = [jnp.sum(gram_ref[:, t] * column, axis=0, keepdims=True) for t in tiles]
        along = gram_ref[:, tiles[0]] * row[:, tiles[0]]
        for t in tiles[1:]:
            along = along + gram_ref[:, t] * row[:, t]
        along = jnp.broadcast_to(jnp.sum(along, axis=1, keepdims=True), (M, DH))
        row = moved(row, jnp.concatenate(down, axis=1), linear_row)
        column = moved(column, along, linear_column)
        if number % 2 == 0 and number // 2 < CHUNKS:
            columns = pl.ds(number // 2 * CHUNK, CHUNK)
            top, corner = gram3(scaled_hi[:, columns], scaled_lo[:, columns])
            attend_ref[:HALF_M, :] = top if number == 0 else attend_ref[:HALF_M, :] + top
            attend_ref[HALF_M:, :] = corner if number == 0 else attend_ref[HALF_M:, :] + corner
    weight_out[...] = row
    gram = attend_ref[...] * row
    gram = gram * jnp.concatenate([column] * (M // DH), axis=1)
    diagonal = lax.broadcasted_iota(jnp.int32, (M, M), 0) == lax.broadcasted_iota(
        jnp.int32, (M, M), 1
    )
    ridge = ridge_weight * (total_of(jnp.where(diagonal, gram, 0.0)) / M + 1e-6)
    system = gram + jnp.where(diagonal, ridge, 0.0)
    bound = jnp.max(jnp.sum(jnp.abs(system), axis=0, keepdims=True), axis=1, keepdims=True)
    number = lax.broadcasted_iota(jnp.int32, factor_out.shape, 0)
    factor_out[...] = jnp.where(number == 0, ridge, jnp.where(number == 1, bound, row))
    power_out[...] = system * (1.0 / bound)


def forward_kernel(own_ref, side_ref, after_ref, out_ref):
    out_ref[:SUM_ROWS, :] = own_ref[...]
    out_ref[SUM_ROWS:, :] = side_ref[...]


def right_side(half_ref, half, bit, scaled_hi, scaled_lo, prior_ref):
    product = None
    for i, lo_bit in enumerate((bit, 1 - bit)):
        number = half * 2 + lo_bit
        begin = i * SUM_ROWS
        lanes = place(number, QUARTER_M)
        prior_ref[: DH // 2, lanes] = half_ref[begin : begin + PRIOR, :QUARTER_M].astype(f32)
        prior_ref[DH // 2 :, lanes] = half_ref[begin : begin + PRIOR, QUARTER_M:].astype(f32)
        outputs = half_ref[begin + PRIOR : begin + SUM_ROWS, :]
        columns = place(number, CHUNK)
        part = mm(outputs, scaled_hi[:, columns], NT) + mm(outputs, scaled_lo[:, columns], NT)
        product = part if product is None else product + part
    return product


def squared(power, pair):
    high, low = pair
    top = 2.0 * power[:HALF_M] - mm3((high[:HALF_M], low[:HALF_M]), pair, NN)
    corner = mm3((high[HALF_M:], low[HALF_M:]), (high[:, HALF_M:], low[:, HALF_M:]), NN)
    corner = 2.0 * power[HALF_M:, HALF_M:] - corner
    return top, jnp.concatenate([top[:, HALF_M:].T, corner], axis=1)


def times_power(refit, high, low):
    rows = refit.shape[0]
    pair = jnp.concatenate(split(refit), axis=0)
    by_high = mm(pair, high, NN)
    return by_high[:rows] + (by_high[rows:] + mm(pair[:rows], low, NN))


def power_kernel(power_in, after_ref, high_out, low_out, power_out):
    power_out[...] = power_in[...]

    def step(number, carry):
        pair = split(power_out[...])
        high_out[place(number, M), :], low_out[place(number, M), :] = pair
        power_out[:HALF_M, :], power_out[HALF_M:, :] = squared(power_out[...], pair)
        return carry

    lax.fori_loop(0, high_out.shape[0] // M, step, 0)


def refit_kernel(
    early_hi, early_lo, late_hi, late_lo, power_in, factor_ref, scaled_hi, scaled_lo, own_ref, half_ref,
    value_out, both_ref, prior_ref,
):
    me, core, bit = bits()
    product = right_side(own_ref, core, bit, scaled_hi, scaled_lo, prior_ref)
    product = product + right_side(half_ref, 1 - core, bit, scaled_hi, scaled_lo, prior_ref)
    ridge, bound, weights = factor_ref[0:1, :1], factor_ref[1:2, :1], factor_ref[2:3, :]
    refit = (weights * product + ridge * prior_ref[...]) * (1.0 / bound)
    for high, low in ((early_hi, early_lo), (late_hi, late_lo)):
        for begin in range(0, high.shape[0], M):
            rows = slice(begin, begin + M)
            refit = 2.0 * refit - times_power(refit, high[rows, :], low[rows, :])
    both_ref[DH:, :] = power_in[...]
    both_ref[:DH, :] = refit
    above = DH + HALF_M

    def newton_step(number, carry):
        high, low = split(both_ref[...])
        power = (high[DH:], low[DH:])
        top = 2.0 * both_ref[:above, :] - mm3((high[:above], low[:above]), power, NN)
        corner = mm3((high[above:], low[above:]), (power[0][:, HALF_M:], power[1][:, HALF_M:]), NN)
        both_ref[above:, HALF_M:] = 2.0 * both_ref[above:, HALF_M:] - corner
        both_ref[above:, :HALF_M] = top[DH:, HALF_M:].T
        both_ref[:above, :] = top
        return carry

    lax.fori_loop(EARLY_STEPS + LATE_STEPS, NS_ITERS - 2, newton_step, 0)
    power = split(both_ref[DH:, :])
    refit = both_ref[:DH, :]
    refit = 2.0 * refit - times_power(refit, *power)
    once = times_power(refit, *power)
    refit = 2.0 * (refit - once) + times_power(once, *power)
    value_out[...] = refit.T


def shape(rows, columns, dtype):
    return jax.ShapeDtypeStruct((rows, columns), dtype)


def call(kernel, outs, arrays, scalars=0, scratch=(), in_specs=None, flops=None, limit=38):
    return pl.pallas_call(
        kernel,
        out_shape=tuple(outs),
        in_specs=in_specs
        or [pl.BlockSpec(memory_space=pltpu.SMEM)] * scalars
        + [pl.BlockSpec(memory_space=pltpu.VMEM)] * (len(arrays) - scalars),
        out_specs=tuple([pl.BlockSpec(memory_space=pltpu.VMEM)] * len(outs)),
        scratch_shapes=list(scratch),
        compiler_params=pltpu.CompilerParams(vmem_limit_bytes=int(limit * 1024 * 1024)),
        cost_estimate=None
        if flops is None
        else pl.CostEstimate(flops=flops, bytes_accessed=1024, transcendentals=0),
    )(*arrays)


def per_device(key_mant, scale_exp, values, queries, compact_index, shard_lengths):
    wide_count = lax.axis_size("wide")
    ctx = key_mant.shape[0]

    def exchanged(array, mask):
        return lax.ppermute(array, "wide", [(i, i ^ mask) for i in range(wide_count)])

    head_shape = shape(HEAD_ROWS, CHUNK, bf16)
    scale_shape = shape(CHUNKS, CHUNK, f32)
    half_sum = shape(PAIR_ROWS, 2 * CHUNK, bf16)
    pieces = (shape(PIECE_ROWS, CHUNK, bf16),) * 2

    send_head, head, send, keep = call(
        attention_kernel,
        (head_shape, head_shape, half_sum, half_sum),
        [
            pltpu.with_memory_space_constraint(array, pltpu.HBM)
            for array in (
                shard_lengths, scale_exp, compact_index.reshape(1, M), key_mant, values, queries
            )
        ],
        in_specs=[pl.BlockSpec(memory_space=pltpu.HBM)] * 6,
        flops=10**9,
        scratch=[
            pltpu.VMEM((2 * CHUNKS, CHUNK), f32),
            pltpu.SMEM(shard_lengths.shape, jnp.int32),
            pltpu.SMEM(scale_exp.shape, jnp.int32),
            pltpu.VMEM((1, M), jnp.int32),
            pltpu.VMEM((ctx, DH), bf16),
            pltpu.VMEM((ctx, DH), bf16),
            pltpu.VMEM((NQ, DH), bf16),
            pltpu.VMEM((ctx, DH), bf16),
            pltpu.VMEM((ctx, 2 * CHUNK), bf16),
            pltpu.SemaphoreType.DMA((6,)),
        ],
    )
    def both_exchanged(arrays, mask):
        return tuple(exchanged(array, mask) for array in arrays)

    def joined(*arrays):
        head, *scales = call(join_kernel, (head_shape, scale_shape, scale_shape), arrays)
        return head, tuple(scales)

    got = exchanged(send, 1)
    head, scales = joined(head, exchanged(send_head, 1))
    got_head = exchanged(head, 2)
    first, second, keep = call(
        halve_sum_kernel,
        pieces + (shape(PAIR_ROWS, CHUNK, bf16),),
        scales + (keep, got),
        flops=SUM_FLOPS,
    )
    sums, got = (keep,), both_exchanged((first, second), 2)
    mask = 4
    while mask < wide_count:
        head, scales = joined(head, got_head, first)
        got_head = exchanged(head, mask)
        last = 2 * mask >= wide_count
        sums = call(
            last_join_sum_kernel if last else join_sum_kernel,
            (shape(SUM_ROWS, CHUNK, bf16),) if last else pieces,
            (*scales, *sums, *got),
            flops=SUM_FLOPS,
        )
        first = sums[0]
        got = both_exchanged(sums, mask)
        mask *= 2
    keys, stats, *scales = call(
        last_join_kernel,
        (shape(HALF_M, DH, bf16), shape(2 * CHUNKS, CHUNK, f32), scale_shape, scale_shape),
        (head, got_head, first),
    )
    got_keys = exchanged(keys, 1)
    gram, linear, norm, scaled_hi, scaled_lo = call(
        feature_kernel,
        (shape(M, M, f32), shape(M, DH, f32), shape(8, DH, f32)) + (shape(M, NQ, bf16),) * 2,
        (shard_lengths, queries, stats, keys, got_keys),
        scalars=1,
        flops=1000000000,
        scratch=[pltpu.VMEM((M, DH), bf16), pltpu.VMEM((M, NQ), bf16), pltpu.VMEM((M, NQ), bf16)],
    )
    weights, factor, power = call(
        weight_kernel,
        (shape(1, M, f32), shape(8, M, f32), shape(M, M, f32)),
        (gram, linear, norm, scaled_hi, scaled_lo),
        flops=5 * 10**9,
        scratch=[pltpu.VMEM((M, M), f32)],
    )
    (outputs,) = call(
        outputs_kernel,
        (shape(SUM_ROWS, CHUNK, bf16),),
        (*scales, stats, *sums, *got, factor),
    )
    side = exchanged(outputs, 2)

    def powers(power, after, steps):
        pairs = (shape(steps * M, M, bf16),) * 2
        return call(power_kernel, pairs + (shape(M, M, f32),), (power, after), flops=steps * 10**9)

    early_hi, early_lo, power = powers(power, outputs, EARLY_STEPS)
    (half,) = call(
        forward_kernel,
        (shape(2 * SUM_ROWS, CHUNK, bf16),),
        (outputs, side, power),
    )
    other = exchanged(half, 1)
    late_hi, late_lo, power = powers(power, half, LATE_STEPS)
    (compact_values,) = call(
        refit_kernel,
        (shape(M, DH, f32),),
        (early_hi, early_lo, late_hi, late_lo, power, factor, scaled_hi, scaled_lo, half, other),
        scratch=[pltpu.VMEM((M + DH, M), f32), pltpu.VMEM((DH, M), f32)],
    )
    return weights.reshape(M), compact_values


def solution(mesh):
    placed = (
        P(("groups", "wide"), None),
        P(("groups", "wide")),
        P(("groups", "wide"), None),
        P("groups", None),
        P("groups"),
        P("groups"),
    )
    return jax.shard_map(
        per_device,
        mesh=mesh,
        in_specs=placed,
        out_specs=(P("groups"), P("groups", None)),
        check_vma=False,
    )
```

```python
import jax
import jax.numpy as jnp
from jax import lax
from jax.experimental import pallas as pl
from jax.experimental.pallas import tpu as pltpu
from jax.sharding import PartitionSpec as P

DH = 128
NQ = 1024
M = 512
QB = 32
SELECT_FROM = 256
NNLS_STEPS = 8
NS_ITERS = 9
EARLY_STEPS = 4
LATE_STEPS = 2
SUM_FLOPS = 10**9
CHUNKS = 4
CHUNK = NQ // CHUNKS
QUARTER_M = M // CHUNKS
SUM_ROWS = DH + QUARTER_M // 2
PAIR_ROWS = SUM_ROWS + DH
HALF_M = M // 2

ridge_weight = 4.0
nnls_ridge = 0.1
floor_value = -1e30
EXP2_SCALE = DH ** (-0.5) * 1.4426950408889634

f32 = jnp.float32
bf16 = jnp.bfloat16
NN = (((1,), (0,)), ((), ()))
NT = (((1,), (1,)), ((), ()))
TN = (((0,), (0,)), ((), ()))


def mm(left, right, dims):
    return lax.dot_general(left, right, dims, preferred_element_type=f32)


def split(x):
    high = x.astype(bf16)
    return high, (x - high.astype(f32)).astype(bf16)


def mm3(left, right, dims):
    return mm(left[0], right[0], dims) + (mm(left[0], right[1], dims) + mm(left[1], right[0], dims))


def total_of(x):
    return jnp.sum(jnp.sum(x, axis=0, keepdims=True), axis=1, keepdims=True)


def place(number, size):
    return pl.ds(pl.multiple_of(number * size, size), size)


def bits():
    me = lax.axis_index("wide")
    return me, lax.rem(me, 2), lax.rem(lax.div(me, 2), 2)


PRIOR = SUM_ROWS - DH
PIECE_ROWS = SUM_ROWS // 2
EVERYTHING = slice(0, CHUNK)


def put_pair(out_ref, columns, prior, sums):
    high, low = split(sums)
    out_ref[:PRIOR, columns] = prior
    out_ref[PRIOR:SUM_ROWS, columns] = high
    out_ref[SUM_ROWS:, columns] = low


def get_pair(ref, columns):
    high = ref[PRIOR:SUM_ROWS, columns].astype(f32)
    return ref[:PRIOR, columns], high + ref[SUM_ROWS:, columns].astype(f32)


def put_pieces(first_ref, second_ref, prior, sums):
    sums = sums.astype(bf16)
    first_ref[:PRIOR, :] = prior
    first_ref[PRIOR:, :] = sums[: PIECE_ROWS - PRIOR]
    second_ref[...] = sums[PIECE_ROWS - PRIOR :]


def get_pieces(first_ref, second_ref):
    sums = jnp.concatenate([first_ref[PRIOR:, :], second_ref[...]], axis=0)
    return first_ref[:PRIOR, :], sums.astype(f32)


KEY_ROWS = HALF_M // 2
HEAD_ROWS = KEY_ROWS + 32


def put_keys(out_ref, keys):
    out_ref[:KEY_ROWS, :DH] = keys[:KEY_ROWS]
    out_ref[:KEY_ROWS, DH:] = keys[KEY_ROWS:]


def put_stats(out_ref, stats):
    high = stats.astype(bf16).astype(f32)
    middle = (stats - high).astype(bf16).astype(f32)
    low = stats - high - middle
    out_ref[KEY_ROWS:, :] = jnp.concatenate([high, middle, low, jnp.zeros_like(low)], axis=0).astype(bf16)


def get_stats(ref):
    parts = ref[KEY_ROWS:, :].astype(f32)
    return parts[:8] + parts[8:16] + parts[16:24]


def attention_kernel(
    len_hbm, exp_hbm, index_hbm, mant_hbm, value_hbm, query_hbm,
    send_head_ref, keep_head_ref, send_ref, keep_ref,
    stat_ref, len_ref, exp_ref, index_ref, mant_ref, value_ref, query_ref, key_ref, attn_ref, sems,
):
    copies = [
        pltpu.make_async_copy(source, target, sems.at[i])
        for i, (source, target) in enumerate(
            (
                (exp_hbm, exp_ref),
                (mant_hbm, mant_ref),
                (query_hbm, query_ref),
                (len_hbm, len_ref),
                (index_hbm, index_ref),
                (value_hbm, value_ref),
            )
        )
    ]
    for copy in copies:
        copy.start()
    ctx = mant_ref.shape[0]
    me, core, bit = bits()
    for copy in copies:
        copy.wait()
    for b in range(ctx // QB):
        exponent = exp_ref[b]
        factor = jnp.where(exponent > 0, 2.0, jnp.where(exponent < 0, 0.5, 1.0)).astype(f32)
        rows = pl.ds(b * QB, QB)
        key_ref[rows, :] = (mant_ref[rows, :].astype(f32) * factor).astype(bf16)
    half_m = M // 2
    position = lax.broadcasted_iota(jnp.int32, (SELECT_FROM, half_m), 0)
    for half, head_out, out in ((1 - core, send_head_ref, send_ref), (core, keep_head_ref, keep_ref)):
        wanted = index_ref[:, place(half, half_m)] - me * ctx
        chosen = jnp.where(position == wanted, 1.0, 0.0).astype(bf16)
        put_keys(head_out, mm(chosen, key_ref[:SELECT_FROM, :], TN).astype(bf16))
        prior = mm(value_ref[:SELECT_FROM, :], chosen, TN).astype(bf16)
        for piece in range(2):
            for part in range(2):
                begin = piece * CHUNK + part * QUARTER_M
                out[:PRIOR, begin : begin + QUARTER_M] = prior[
                    part * (DH // 2) : (part + 1) * (DH // 2), piece * QUARTER_M : (piece + 1) * QUARTER_M
                ]
    dead = lax.broadcasted_iota(jnp.int32, (ctx, CHUNK), 0) >= len_ref[me]
    for half, out in ((1 - core, send_ref), (core, keep_ref)):
        for c in range(2):
            number = half * 2 + c
            scores = mm(key_ref[...], query_ref[place(number, CHUNK), :], NT)
            scores = jnp.where(dead, floor_value, scores)
            row_max = jnp.max(scores, axis=0, keepdims=True)
            attn = jnp.exp2((scores - row_max) * EXP2_SCALE)
            stat_ref[pl.ds(number, 1), :] = row_max
            stat_ref[pl.ds(CHUNKS + number, 1), :] = jnp.sum(attn, axis=0, keepdims=True)
            attn_ref[:, c * CHUNK : (c + 1) * CHUNK] = attn.astype(bf16)
        high, low = split(mm(value_ref[...], attn_ref[...], TN))
        out[PRIOR:SUM_ROWS, :] = high
        out[SUM_ROWS:, :] = low
    put_stats(send_head_ref, stat_ref[...])
    put_stats(keep_head_ref, stat_ref[...])


def joined_stats(first_ref, second_ref, scale_first_out, scale_second_out):
    first, second = get_stats(first_ref), get_stats(second_ref)
    joint = jnp.maximum(first[:CHUNKS], second[:CHUNKS])
    scale_first = jnp.exp2((first[:CHUNKS] - joint) * EXP2_SCALE)
    scale_second = jnp.exp2((second[:CHUNKS] - joint) * EXP2_SCALE)
    scale_first_out[...] = scale_first
    scale_second_out[...] = scale_second
    mass = first[CHUNKS:] * scale_first + second[CHUNKS:] * scale_second
    return jnp.concatenate([joint, mass], axis=0)


def join_kernel(first_ref, second_ref, *refs):
    out_ref, scale_first_out, scale_second_out = refs[-3:]
    put_stats(out_ref, joined_stats(first_ref, second_ref, scale_first_out, scale_second_out))
    out_ref[:KEY_ROWS, :] = first_ref[:KEY_ROWS, :] + second_ref[:KEY_ROWS, :]


def last_join_kernel(first_ref, second_ref, after_ref, key_out, stat_out, scale_first_out, scale_second_out):
    stat_out[...] = joined_stats(first_ref, second_ref, scale_first_out, scale_second_out)
    for c in range(2):
        columns = slice(c * DH, (c + 1) * DH)
        rows = slice(c * KEY_ROWS, (c + 1) * KEY_ROWS)
        key_out[rows, :] = first_ref[:KEY_ROWS, columns] + second_ref[:KEY_ROWS, columns]


def copy_kernel(sum_ref, after_ref, out_ref):
    out_ref[...] = sum_ref[...]


def halve_sum_kernel(scale_a, scale_b, sum_a, sum_b, first_out, second_out, keep_out):
    me, core, bit = bits()

    def half_of(half):
        columns = place(half, CHUNK)
        row = pl.ds(core * 2 + half, 1)
        prior_a, sums_a = get_pair(sum_a, columns)
        prior_b, sums_b = get_pair(sum_b, columns)
        return prior_a + prior_b, sums_a * scale_a[row, :] + sums_b * scale_b[row, :]

    put_pieces(first_out, second_out, *half_of(1 - bit))
    put_pair(keep_out, EVERYTHING, *half_of(bit))


def joined_sums(scale_a, scale_b, own, got):
    me, core, bit = bits()
    row = pl.ds(core * 2 + bit, 1)
    prior_a, sums_a = get_pair(own[0], EVERYTHING) if len(own) == 1 else get_pieces(*own)
    prior_b, sums_b = get_pieces(*got)
    return prior_a + prior_b, sums_a * scale_a[row, :] + sums_b * scale_b[row, :]


def join_sum_kernel(scale_a, scale_b, *refs):
    put_pieces(*refs[-2:], *joined_sums(scale_a, scale_b, refs[:-4], refs[-4:-2]))


def last_join_sum_kernel(scale_a, scale_b, *refs):
    out_ref = refs[-1]
    prior, sums = joined_sums(scale_a, scale_b, refs[:-3], refs[-3:-1])
    out_ref[:PRIOR, :] = prior
    out_ref[PRIOR:, :] = sums.astype(bf16)


def outputs_kernel(scale_a, scale_b, stat_ref, sum_a, sum_b, after_ref, out_ref):
    me, core, bit = bits()
    row = pl.ds(core * 2 + bit, 1)
    sums = sum_a[PRIOR:, :].astype(f32) * scale_a[row, :] + sum_b[PRIOR:, :].astype(f32) * scale_b[row, :]
    out_ref[:PRIOR, :] = sum_a[:PRIOR, :] + sum_b[:PRIOR, :]
    out_ref[PRIOR:, :] = (sums / stat_ref[pl.ds(CHUNKS + core * 2 + bit, 1), :]).astype(bf16)


def gram3(high, low):
    top = mm3((high[:HALF_M], low[:HALF_M]), (high, low), NT)
    corner = mm3((high[HALF_M:], low[HALF_M:]), (high[HALF_M:], low[HALF_M:]), NT)
    return top, jnp.concatenate([top[:, HALF_M:].T, corner], axis=1)


def feature_kernel(
    len_ref, query_ref, stat_ref, own_key_ref, other_key_ref,
    gram_ref, linear_ref, norm_ref, scaled_hi, scaled_lo,
    key_ref, feat_hi, feat_lo,
):
    me, core, bit = bits()
    total = len_ref[0]
    for i in range(1, len_ref.shape[0]):
        total = total + len_ref[i]
    live_total = jnp.full((1, 1), total, jnp.int32).astype(f32)
    key_ref[place(core, M // 2), :] = own_key_ref[...]
    key_ref[place(1 - core, M // 2), :] = other_key_ref[...]
    frobenius = jnp.zeros((1, 1), f32)
    linear = jnp.zeros((M, DH), f32)
    for c in range(CHUNKS):
        columns = pl.ds(c * CHUNK, CHUNK)
        row_max, row_mass = stat_ref[c : c + 1, :], stat_ref[CHUNKS + c : CHUNKS + c + 1, :]
        scores = mm(key_ref[...], query_ref[columns, :], NT)
        features = jnp.exp2((scores - row_max) * EXP2_SCALE)
        target = row_mass * (M / live_total)
        top, corner = gram3(*split(features))
        gram_ref[:HALF_M, :] = top if c == 0 else gram_ref[:HALF_M, :] + top
        gram_ref[HALF_M:, :] = corner if c == 0 else gram_ref[HALF_M:, :] + corner
        frobenius = frobenius + total_of(features * features)
        weighted = features * target
        for tile in range(CHUNK // DH):
            linear = linear + weighted[:, tile * DH : (tile + 1) * DH]
        high, low = split(features * (1.0 / target))
        scaled_hi[:, columns] = high
        scaled_lo[:, columns] = low
    linear_ref[...] = jnp.broadcast_to(jnp.sum(linear, axis=1, keepdims=True), (M, DH))
    norm_ref[...] = jnp.broadcast_to(frobenius, norm_ref.shape)


def weight_kernel(
    gram_ref, linear_ref, norm_ref, scaled_hi, scaled_lo,
    weight_out, factor_out, power_out, attend_ref,
):
    frobenius = norm_ref[:1, :1]
    damping = nnls_ridge * (frobenius / M + 1e-6)
    stepsize = 1.0 / (frobenius + damping)
    linear_column = linear_ref[...]
    linear_row = linear_column.T[:1]
    row = jnp.ones((1, M), f32)
    column = jnp.ones((M, DH), f32)
    tiles = [slice(t * DH, (t + 1) * DH) for t in range(M // DH)]

    def moved(weights, product, linear):
        gradient = product - linear + damping * weights
        return jnp.maximum(weights - stepsize * gradient, 0.0)

    for number in range(NNLS_STEPS):
        down = [jnp.sum(gram_ref[:, t] * column, axis=0, keepdims=True) for t in tiles]
        along = gram_ref[:, tiles[0]] * row[:, tiles[0]]
        for t in tiles[1:]:
            along = along + gram_ref[:, t] * row[:, t]
        along = jnp.broadcast_to(jnp.sum(along, axis=1, keepdims=True), (M, DH))
        row = moved(row, jnp.concatenate(down, axis=1), linear_row)
        column = moved(column, along, linear_column)
        if number % 2 == 0 and number // 2 < CHUNKS:
            columns = pl.ds(number // 2 * CHUNK, CHUNK)
            top, corner = gram3(scaled_hi[:, columns], scaled_lo[:, columns])
            attend_ref[:HALF_M, :] = top if number == 0 else attend_ref[:HALF_M, :] + top
            attend_ref[HALF_M:, :] = corner if number == 0 else attend_ref[HALF_M:, :] + corner
    weight_out[...] = row
    gram = attend_ref[...] * row
    gram = gram * jnp.concatenate([column] * (M // DH), axis=1)
    diagonal = lax.broadcasted_iota(jnp.int32, (M, M), 0) == lax.broadcasted_iota(
        jnp.int32, (M, M), 1
    )
    ridge = ridge_weight * (total_of(jnp.where(diagonal, gram, 0.0)) / M + 1e-6)
    system = gram + jnp.where(diagonal, ridge, 0.0)
    bound = jnp.max(jnp.sum(jnp.abs(system), axis=0, keepdims=True), axis=1, keepdims=True)
    number = lax.broadcasted_iota(jnp.int32, factor_out.shape, 0)
    factor_out[...] = jnp.where(number == 0, ridge, jnp.where(number == 1, bound, row))
    power_out[...] = system * (1.0 / bound)


def forward_kernel(own_ref, side_ref, after_ref, out_ref):
    out_ref[:SUM_ROWS, :] = own_ref[...]
    out_ref[SUM_ROWS:, :] = side_ref[...]


def right_side(half_ref, half, bit, scaled_hi, scaled_lo, prior_ref):
    product = None
    for i, lo_bit in enumerate((bit, 1 - bit)):
        number = half * 2 + lo_bit
        begin = i * SUM_ROWS
        lanes = place(number, QUARTER_M)
        prior_ref[: DH // 2, lanes] = half_ref[begin : begin + PRIOR, :QUARTER_M].astype(f32)
        prior_ref[DH // 2 :, lanes] = half_ref[begin : begin + PRIOR, QUARTER_M:].astype(f32)
        outputs = half_ref[begin + PRIOR : begin + SUM_ROWS, :]
        columns = place(number, CHUNK)
        part = mm(outputs, scaled_hi[:, columns], NT) + mm(outputs, scaled_lo[:, columns], NT)
        product = part if product is None else product + part
    return product


def squared(power, pair):
    high, low = pair
    top = 2.0 * power[:HALF_M] - mm3((high[:HALF_M], low[:HALF_M]), pair, NN)
    corner = mm3((high[HALF_M:], low[HALF_M:]), (high[:, HALF_M:], low[:, HALF_M:]), NN)
    corner = 2.0 * power[HALF_M:, HALF_M:] - corner
    return top, jnp.concatenate([top[:, HALF_M:].T, corner], axis=1)


def times_power(refit, high, low):
    rows = refit.shape[0]
    pair = jnp.concatenate(split(refit), axis=0)
    by_high = mm(pair, high, NN)
    return by_high[:rows] + (by_high[rows:] + mm(pair[:rows], low, NN))


def power_kernel(power_in, after_ref, high_out, low_out, power_out):
    power_out[...] = power_in[...]

    def step(number, carry):
        pair = split(power_out[...])
        high_out[place(number, M), :], low_out[place(number, M), :] = pair
        power_out[:HALF_M, :], power_out[HALF_M:, :] = squared(power_out[...], pair)
        return carry

    lax.fori_loop(0, high_out.shape[0] // M, step, 0)


def refit_kernel(
    early_hi, early_lo, late_hi, late_lo, power_in, factor_ref, scaled_hi, scaled_lo, own_ref, half_ref,
    value_out, both_ref, prior_ref,
):
    me, core, bit = bits()
    product = right_side(own_ref, core, bit, scaled_hi, scaled_lo, prior_ref)
    product = product + right_side(half_ref, 1 - core, bit, scaled_hi, scaled_lo, prior_ref)
    ridge, bound, weights = factor_ref[0:1, :1], factor_ref[1:2, :1], factor_ref[2:3, :]
    refit = (weights * product + ridge * prior_ref[...]) * (1.0 / bound)
    for high, low in ((early_hi, early_lo), (late_hi, late_lo)):
        for begin in range(0, high.shape[0], M):
            rows = slice(begin, begin + M)
            refit = 2.0 * refit - times_power(refit, high[rows, :], low[rows, :])
    both_ref[DH:, :] = power_in[...]
    both_ref[:DH, :] = refit
    above = DH + HALF_M

    def newton_step(number, carry):
        high, low = split(both_ref[...])
        power = (high[DH:], low[DH:])
        top = 2.0 * both_ref[:above, :] - mm3((high[:above], low[:above]), power, NN)
        corner = mm3((high[above:], low[above:]), (power[0][:, HALF_M:], power[1][:, HALF_M:]), NN)
        both_ref[above:, HALF_M:] = 2.0 * both_ref[above:, HALF_M:] - corner
        both_ref[above:, :HALF_M] = top[DH:, HALF_M:].T
        both_ref[:above, :] = top
        return carry

    lax.fori_loop(EARLY_STEPS + LATE_STEPS, NS_ITERS - 2, newton_step, 0)
    power = split(both_ref[DH:, :])
    refit = both_ref[:DH, :]
    refit = 2.0 * refit - times_power(refit, *power)
    once = times_power(refit, *power)
    refit = 2.0 * (refit - once) + times_power(once, *power)
    value_out[...] = refit.T


def shape(rows, columns, dtype):
    return jax.ShapeDtypeStruct((rows, columns), dtype)


def call(kernel, outs, arrays, scalars=0, scratch=(), in_specs=None, flops=None, limit=38):
    return pl.pallas_call(
        kernel,
        out_shape=tuple(outs),
        in_specs=in_specs
        or [pl.BlockSpec(memory_space=pltpu.SMEM)] * scalars
        + [pl.BlockSpec(memory_space=pltpu.VMEM)] * (len(arrays) - scalars),
        out_specs=tuple([pl.BlockSpec(memory_space=pltpu.VMEM)] * len(outs)),
        scratch_shapes=list(scratch),
        compiler_params=pltpu.CompilerParams(vmem_limit_bytes=int(limit * 1024 * 1024)),
        cost_estimate=None
        if flops is None
        else pl.CostEstimate(flops=flops, bytes_accessed=1024, transcendentals=0),
    )(*arrays)


def per_device(key_mant, scale_exp, values, queries, compact_index, shard_lengths):
    wide_count = lax.axis_size("wide")
    ctx = key_mant.shape[0]

    def exchanged(array, mask):
        return lax.ppermute(array, "wide", [(i, i ^ mask) for i in range(wide_count)])

    head_shape = shape(HEAD_ROWS, CHUNK, bf16)
    scale_shape = shape(CHUNKS, CHUNK, f32)
    half_sum = shape(PAIR_ROWS, 2 * CHUNK, bf16)
    pieces = (shape(PIECE_ROWS, CHUNK, bf16),) * 2

    send_head, head, send, keep = call(
        attention_kernel,
        (head_shape, head_shape, half_sum, half_sum),
        [
            pltpu.with_memory_space_constraint(array, pltpu.HBM)
            for array in (
                shard_lengths, scale_exp, compact_index.reshape(1, M), key_mant, values, queries
            )
        ],
        in_specs=[pl.BlockSpec(memory_space=pltpu.HBM)] * 6,
        flops=10**9,
        scratch=[
            pltpu.VMEM((2 * CHUNKS, CHUNK), f32),
            pltpu.SMEM(shard_lengths.shape, jnp.int32),
            pltpu.SMEM(scale_exp.shape, jnp.int32),
            pltpu.VMEM((1, M), jnp.int32),
            pltpu.VMEM((ctx, DH), bf16),
            pltpu.VMEM((ctx, DH), bf16),
            pltpu.VMEM((NQ, DH), bf16),
            pltpu.VMEM((ctx, DH), bf16),
            pltpu.VMEM((ctx, 2 * CHUNK), bf16),
            pltpu.SemaphoreType.DMA((6,)),
        ],
    )
    def both_exchanged(arrays, mask):
        return tuple(exchanged(array, mask) for array in arrays)

    def joined(*arrays):
        head, *scales = call(join_kernel, (head_shape, scale_shape, scale_shape), arrays)
        return head, tuple(scales)

    head, scales = joined(head, exchanged(send_head, 1))
    got_head = exchanged(head, 2)
    (send,) = call(copy_kernel, (half_sum,), (send, head))
    got = exchanged(send, 1)
    first, second, keep = call(
        halve_sum_kernel,
        pieces + (shape(PAIR_ROWS, CHUNK, bf16),),
        scales + (keep, got),
        flops=SUM_FLOPS,
    )
    sums, got = (keep,), both_exchanged((first, second), 2)
    mask = 4
    while mask < wide_count:
        head, scales = joined(head, got_head, first)
        got_head = exchanged(head, mask)
        last = 2 * mask >= wide_count
        sums = call(
            last_join_sum_kernel if last else join_sum_kernel,
            (shape(SUM_ROWS, CHUNK, bf16),) if last else pieces,
            (*scales, *sums, *got),
            flops=SUM_FLOPS,
        )
        first = sums[0]
        got = both_exchanged(sums, mask)
        mask *= 2
    keys, stats, *scales = call(
        last_join_kernel,
        (shape(HALF_M, DH, bf16), shape(2 * CHUNKS, CHUNK, f32), scale_shape, scale_shape),
        (head, got_head, first),
    )
    got_keys = exchanged(keys, 1)
    gram, linear, norm, scaled_hi, scaled_lo = call(
        feature_kernel,
        (shape(M, M, f32), shape(M, DH, f32), shape(8, DH, f32)) + (shape(M, NQ, bf16),) * 2,
        (shard_lengths, queries, stats, keys, got_keys),
        scalars=1,
        flops=1000000000,
        scratch=[pltpu.VMEM((M, DH), bf16), pltpu.VMEM((M, NQ), bf16), pltpu.VMEM((M, NQ), bf16)],
    )
    weights, factor, power = call(
        weight_kernel,
        (shape(1, M, f32), shape(8, M, f32), shape(M, M, f32)),
        (gram, linear, norm, scaled_hi, scaled_lo),
        flops=5 * 10**9,
        scratch=[pltpu.VMEM((M, M), f32)],
    )
    (outputs,) = call(
        outputs_kernel,
        (shape(SUM_ROWS, CHUNK, bf16),),
        (*scales, stats, *sums, *got, factor),
    )
    side = exchanged(outputs, 2)

    def powers(power, after, steps):
        pairs = (shape(steps * M, M, bf16),) * 2
        return call(power_kernel, pairs + (shape(M, M, f32),), (power, after), flops=steps * 10**9)

    early_hi, early_lo, power = powers(power, outputs, EARLY_STEPS)
    (half,) = call(
        forward_kernel,
        (shape(2 * SUM_ROWS, CHUNK, bf16),),
        (outputs, side, power),
    )
    other = exchanged(half, 1)
    late_hi, late_lo, power = powers(power, half, LATE_STEPS)
    (compact_values,) = call(
        refit_kernel,
        (shape(M, DH, f32),),
        (early_hi, early_lo, late_hi, late_lo, power, factor, scaled_hi, scaled_lo, half, other),
        scratch=[pltpu.VMEM((M + DH, M), f32), pltpu.VMEM((DH, M), f32)],
    )
    return weights.reshape(M), compact_values


def solution(mesh):
    placed = (
        P(("groups", "wide"), None),
        P(("groups", "wide")),
        P(("groups", "wide"), None),
        P("groups", None),
        P("groups"),
        P("groups"),
    )
    return jax.shard_map(
        per_device,
        mesh=mesh,
        in_specs=placed,
        out_specs=(P("groups"), P("groups", None)),
        check_vma=False,
    )
```

```python
import jax
import jax.numpy as jnp
from jax import lax
from jax.experimental import pallas as pl
from jax.experimental.pallas import tpu as pltpu
from jax.sharding import PartitionSpec as P

DH = 128
NQ = 1024
M = 512
QB = 32
SELECT_FROM = 256
NNLS_STEPS = 8
NS_ITERS = 9
EARLY_STEPS = 4
LATE_STEPS = 2
SUM_FLOPS = 10**9
CHUNKS = 4
CHUNK = NQ // CHUNKS
QUARTER_M = M // CHUNKS
SUM_ROWS = DH + QUARTER_M // 2
PAIR_ROWS = SUM_ROWS + DH
HALF_M = M // 2

ridge_weight = 4.0
nnls_ridge = 0.1
floor_value = -1e30
EXP2_SCALE = DH ** (-0.5) * 1.4426950408889634

f32 = jnp.float32
bf16 = jnp.bfloat16
NN = (((1,), (0,)), ((), ()))
NT = (((1,), (1,)), ((), ()))
TN = (((0,), (0,)), ((), ()))


def mm(left, right, dims):
    return lax.dot_general(left, right, dims, preferred_element_type=f32)


def split(x):
    high = x.astype(bf16)
    return high, (x - high.astype(f32)).astype(bf16)


def mm3(left, right, dims):
    return mm(left[0], right[0], dims) + (mm(left[0], right[1], dims) + mm(left[1], right[0], dims))


def total_of(x):
    return jnp.sum(jnp.sum(x, axis=0, keepdims=True), axis=1, keepdims=True)


def place(number, size):
    return pl.ds(pl.multiple_of(number * size, size), size)


def bits():
    me = lax.axis_index("wide")
    return me, lax.rem(me, 2), lax.rem(lax.div(me, 2), 2)


PRIOR = SUM_ROWS - DH
PIECE_ROWS = SUM_ROWS // 2
EVERYTHING = slice(0, CHUNK)


def put_pair(out_ref, columns, prior, sums):
    high, low = split(sums)
    out_ref[:PRIOR, columns] = prior
    out_ref[PRIOR:SUM_ROWS, columns] = high
    out_ref[SUM_ROWS:, columns] = low


def get_pair(ref, columns):
    high = ref[PRIOR:SUM_ROWS, columns].astype(f32)
    return ref[:PRIOR, columns], high + ref[SUM_ROWS:, columns].astype(f32)


def put_pieces(first_ref, second_ref, prior, sums):
    sums = sums.astype(bf16)
    first_ref[:PRIOR, :] = prior
    first_ref[PRIOR:, :] = sums[: PIECE_ROWS - PRIOR]
    second_ref[...] = sums[PIECE_ROWS - PRIOR :]


def get_pieces(first_ref, second_ref):
    sums = jnp.concatenate([first_ref[PRIOR:, :], second_ref[...]], axis=0)
    return first_ref[:PRIOR, :], sums.astype(f32)


KEY_ROWS = HALF_M // 2
HEAD_ROWS = KEY_ROWS + 32


def put_keys(out_ref, keys):
    out_ref[:KEY_ROWS, :DH] = keys[:KEY_ROWS]
    out_ref[:KEY_ROWS, DH:] = keys[KEY_ROWS:]


def put_stats(out_ref, stats):
    high = stats.astype(bf16).astype(f32)
    middle = (stats - high).astype(bf16).astype(f32)
    low = stats - high - middle
    out_ref[KEY_ROWS:, :] = jnp.concatenate([high, middle, low, jnp.zeros_like(low)], axis=0).astype(bf16)


def get_stats(ref):
    parts = ref[KEY_ROWS:, :].astype(f32)
    return parts[:8] + parts[8:16] + parts[16:24]


def attention_kernel(
    len_hbm, exp_hbm, index_hbm, mant_hbm, value_hbm, query_hbm,
    send_head_ref, keep_head_ref, send_ref, keep_ref,
    stat_ref, len_ref, exp_ref, index_ref, mant_ref, value_ref, query_ref, key_ref, attn_ref, sems,
):
    copies = [
        pltpu.make_async_copy(source, target, sems.at[i])
        for i, (source, target) in enumerate(
            (
                (exp_hbm, exp_ref),
                (mant_hbm, mant_ref),
                (query_hbm, query_ref),
                (len_hbm, len_ref),
                (index_hbm, index_ref),
                (value_hbm, value_ref),
            )
        )
    ]
    for copy in copies:
        copy.start()
    ctx = mant_ref.shape[0]
    me, core, bit = bits()
    for copy in copies:
        copy.wait()
    for b in range(ctx // QB):
        exponent = exp_ref[b]
        factor = jnp.where(exponent > 0, 2.0, jnp.where(exponent < 0, 0.5, 1.0)).astype(f32)
        rows = pl.ds(b * QB, QB)
        key_ref[rows, :] = (mant_ref[rows, :].astype(f32) * factor).astype(bf16)
    half_m = M // 2
    position = lax.broadcasted_iota(jnp.int32, (SELECT_FROM, half_m), 0)
    for half, head_out, out in ((1 - core, send_head_ref, send_ref), (core, keep_head_ref, keep_ref)):
        wanted = index_ref[:, place(half, half_m)] - me * ctx
        chosen = jnp.where(position == wanted, 1.0, 0.0).astype(bf16)
        put_keys(head_out, mm(chosen, key_ref[:SELECT_FROM, :], TN).astype(bf16))
        prior = mm(value_ref[:SELECT_FROM, :], chosen, TN).astype(bf16)
        for piece in range(2):
            for part in range(2):
                begin = piece * CHUNK + part * QUARTER_M
                out[:PRIOR, begin : begin + QUARTER_M] = prior[
                    part * (DH // 2) : (part + 1) * (DH // 2), piece * QUARTER_M : (piece + 1) * QUARTER_M
                ]
    dead = lax.broadcasted_iota(jnp.int32, (ctx, CHUNK), 0) >= len_ref[me]
    for half, out in ((1 - core, send_ref), (core, keep_ref)):
        for c in range(2):
            number = half * 2 + c
            scores = mm(key_ref[...], query_ref[place(number, CHUNK), :], NT)
            scores = jnp.where(dead, floor_value, scores)
            row_max = jnp.max(scores, axis=0, keepdims=True)
            attn = jnp.exp2((scores - row_max) * EXP2_SCALE)
            stat_ref[pl.ds(number, 1), :] = row_max
            stat_ref[pl.ds(CHUNKS + number, 1), :] = jnp.sum(attn, axis=0, keepdims=True)
            begin = (0 if out is send_ref else 2 * CHUNK) + c * CHUNK
            attn_ref[:, begin : begin + CHUNK] = attn.astype(bf16)
    sums = mm(value_ref[...], attn_ref[...], TN)
    for i, out in enumerate((send_ref, keep_ref)):
        high, low = split(sums[:, i * 2 * CHUNK : (i + 1) * 2 * CHUNK])
        out[PRIOR:SUM_ROWS, :] = high
        out[SUM_ROWS:, :] = low
    put_stats(send_head_ref, stat_ref[...])
    put_stats(keep_head_ref, stat_ref[...])


def joined_stats(first_ref, second_ref, scale_first_out, scale_second_out):
    first, second = get_stats(first_ref), get_stats(second_ref)
    joint = jnp.maximum(first[:CHUNKS], second[:CHUNKS])
    scale_first = jnp.exp2((first[:CHUNKS] - joint) * EXP2_SCALE)
    scale_second = jnp.exp2((second[:CHUNKS] - joint) * EXP2_SCALE)
    scale_first_out[...] = scale_first
    scale_second_out[...] = scale_second
    mass = first[CHUNKS:] * scale_first + second[CHUNKS:] * scale_second
    return jnp.concatenate([joint, mass], axis=0)


def join_kernel(first_ref, second_ref, *refs):
    out_ref, scale_first_out, scale_second_out = refs[-3:]
    put_stats(out_ref, joined_stats(first_ref, second_ref, scale_first_out, scale_second_out))
    out_ref[:KEY_ROWS, :] = first_ref[:KEY_ROWS, :] + second_ref[:KEY_ROWS, :]


def last_join_kernel(first_ref, second_ref, after_ref, key_out, stat_out, scale_first_out, scale_second_out):
    stat_out[...] = joined_stats(first_ref, second_ref, scale_first_out, scale_second_out)
    for c in range(2):
        columns = slice(c * DH, (c + 1) * DH)
        rows = slice(c * KEY_ROWS, (c + 1) * KEY_ROWS)
        key_out[rows, :] = first_ref[:KEY_ROWS, columns] + second_ref[:KEY_ROWS, columns]


def copy_kernel(sum_ref, after_ref, out_ref):
    out_ref[...] = sum_ref[...]


def halve_sum_kernel(scale_a, scale_b, sum_a, sum_b, first_out, second_out, keep_out):
    me, core, bit = bits()

    def half_of(half):
        columns = place(half, CHUNK)
        row = pl.ds(core * 2 + half, 1)
        prior_a, sums_a = get_pair(sum_a, columns)
        prior_b, sums_b = get_pair(sum_b, columns)
        return prior_a + prior_b, sums_a * scale_a[row, :] + sums_b * scale_b[row, :]

    put_pieces(first_out, second_out, *half_of(1 - bit))
    put_pair(keep_out, EVERYTHING, *half_of(bit))


def joined_sums(scale_a, scale_b, own, got):
    me, core, bit = bits()
    row = pl.ds(core * 2 + bit, 1)
    prior_a, sums_a = get_pair(own[0], EVERYTHING) if len(own) == 1 else get_pieces(*own)
    prior_b, sums_b = get_pieces(*got)
    return prior_a + prior_b, sums_a * scale_a[row, :] + sums_b * scale_b[row, :]


def join_sum_kernel(scale_a, scale_b, *refs):
    put_pieces(*refs[-2:], *joined_sums(scale_a, scale_b, refs[:-4], refs[-4:-2]))


def last_join_sum_kernel(scale_a, scale_b, *refs):
    out_ref = refs[-1]
    prior, sums = joined_sums(scale_a, scale_b, refs[:-3], refs[-3:-1])
    out_ref[:PRIOR, :] = prior
    out_ref[PRIOR:, :] = sums.astype(bf16)


def outputs_kernel(scale_a, scale_b, stat_ref, sum_a, sum_b, after_ref, out_ref):
    me, core, bit = bits()
    row = pl.ds(core * 2 + bit, 1)
    sums = sum_a[PRIOR:, :].astype(f32) * scale_a[row, :] + sum_b[PRIOR:, :].astype(f32) * scale_b[row, :]
    out_ref[:PRIOR, :] = sum_a[:PRIOR, :] + sum_b[:PRIOR, :]
    out_ref[PRIOR:, :] = (sums / stat_ref[pl.ds(CHUNKS + core * 2 + bit, 1), :]).astype(bf16)


def gram3(high, low):
    top = mm3((high[:HALF_M], low[:HALF_M]), (high, low), NT)
    corner = mm3((high[HALF_M:], low[HALF_M:]), (high[HALF_M:], low[HALF_M:]), NT)
    return top, jnp.concatenate([top[:, HALF_M:].T, corner], axis=1)


def feature_kernel(
    len_ref, query_ref, stat_ref, own_key_ref, other_key_ref,
    gram_ref, linear_ref, norm_ref, scaled_hi, scaled_lo,
    key_ref, feat_hi, feat_lo,
):
    me, core, bit = bits()
    total = len_ref[0]
    for i in range(1, len_ref.shape[0]):
        total = total + len_ref[i]
    live_total = jnp.full((1, 1), total, jnp.int32).astype(f32)
    key_ref[place(core, M // 2), :] = own_key_ref[...]
    key_ref[place(1 - core, M // 2), :] = other_key_ref[...]
    frobenius = jnp.zeros((1, 1), f32)
    linear = jnp.zeros((M, DH), f32)
    for c in range(CHUNKS):
        columns = pl.ds(c * CHUNK, CHUNK)
        row_max, row_mass = stat_ref[c : c + 1, :], stat_ref[CHUNKS + c : CHUNKS + c + 1, :]
        scores = mm(key_ref[...], query_ref[columns, :], NT)
        features = jnp.exp2((scores - row_max) * EXP2_SCALE)
        target = row_mass * (M / live_total)
        top, corner = gram3(*split(features))
        gram_ref[:HALF_M, :] = top if c == 0 else gram_ref[:HALF_M, :] + top
        gram_ref[HALF_M:, :] = corner if c == 0 else gram_ref[HALF_M:, :] + corner
        frobenius = frobenius + total_of(features * features)
        weighted = features * target
        for tile in range(CHUNK // DH):
            linear = linear + weighted[:, tile * DH : (tile + 1) * DH]
        high, low = split(features * (1.0 / target))
        scaled_hi[:, columns] = high
        scaled_lo[:, columns] = low
    linear_ref[...] = jnp.broadcast_to(jnp.sum(linear, axis=1, keepdims=True), (M, DH))
    norm_ref[...] = jnp.broadcast_to(frobenius, norm_ref.shape)


def weight_kernel(
    gram_ref, linear_ref, norm_ref, scaled_hi, scaled_lo,
    weight_out, factor_out, power_out, attend_ref,
):
    frobenius = norm_ref[:1, :1]
    damping = nnls_ridge * (frobenius / M + 1e-6)
    stepsize = 1.0 / (frobenius + damping)
    linear_column = linear_ref[...]
    linear_row = linear_column.T[:1]
    row = jnp.ones((1, M), f32)
    column = jnp.ones((M, DH), f32)
    tiles = [slice(t * DH, (t + 1) * DH) for t in range(M // DH)]

    def moved(weights, product, linear):
        gradient = product - linear + damping * weights
        return jnp.maximum(weights - stepsize * gradient, 0.0)

    for number in range(NNLS_STEPS):
        down = [jnp.sum(gram_ref[:, t] * column, axis=0, keepdims=True) for t in tiles]
        along = gram_ref[:, tiles[0]] * row[:, tiles[0]]
        for t in tiles[1:]:
            along = along + gram_ref[:, t] * row[:, t]
        along = jnp.broadcast_to(jnp.sum(along, axis=1, keepdims=True), (M, DH))
        row = moved(row, jnp.concatenate(down, axis=1), linear_row)
        column = moved(column, along, linear_column)
        if number % 2 == 0 and number // 2 < CHUNKS:
            columns = pl.ds(number // 2 * CHUNK, CHUNK)
            top, corner = gram3(scaled_hi[:, columns], scaled_lo[:, columns])
            attend_ref[:HALF_M, :] = top if number == 0 else attend_ref[:HALF_M, :] + top
            attend_ref[HALF_M:, :] = corner if number == 0 else attend_ref[HALF_M:, :] + corner
    weight_out[...] = row
    gram = attend_ref[...] * row
    gram = gram * jnp.concatenate([column] * (M // DH), axis=1)
    diagonal = lax.broadcasted_iota(jnp.int32, (M, M), 0) == lax.broadcasted_iota(
        jnp.int32, (M, M), 1
    )
    ridge = ridge_weight * (total_of(jnp.where(diagonal, gram, 0.0)) / M + 1e-6)
    system = gram + jnp.where(diagonal, ridge, 0.0)
    bound = jnp.max(jnp.sum(jnp.abs(system), axis=0, keepdims=True), axis=1, keepdims=True)
    number = lax.broadcasted_iota(jnp.int32, factor_out.shape, 0)
    factor_out[...] = jnp.where(number == 0, ridge, jnp.where(number == 1, bound, row))
    power_out[...] = system * (1.0 / bound)


def forward_kernel(own_ref, side_ref, after_ref, out_ref):
    out_ref[:SUM_ROWS, :] = own_ref[...]
    out_ref[SUM_ROWS:, :] = side_ref[...]


def right_side(half_ref, half, bit, scaled_hi, scaled_lo, prior_ref):
    product = None
    for i, lo_bit in enumerate((bit, 1 - bit)):
        number = half * 2 + lo_bit
        begin = i * SUM_ROWS
        lanes = place(number, QUARTER_M)
        prior_ref[: DH // 2, lanes] = half_ref[begin : begin + PRIOR, :QUARTER_M].astype(f32)
        prior_ref[DH // 2 :, lanes] = half_ref[begin : begin + PRIOR, QUARTER_M:].astype(f32)
        outputs = half_ref[begin + PRIOR : begin + SUM_ROWS, :]
        columns = place(number, CHUNK)
        part = mm(outputs, scaled_hi[:, columns], NT) + mm(outputs, scaled_lo[:, columns], NT)
        product = part if product is None else product + part
    return product


def squared(power, pair):
    high, low = pair
    top = 2.0 * power[:HALF_M] - mm3((high[:HALF_M], low[:HALF_M]), pair, NN)
    corner = mm3((high[HALF_M:], low[HALF_M:]), (high[:, HALF_M:], low[:, HALF_M:]), NN)
    corner = 2.0 * power[HALF_M:, HALF_M:] - corner
    return top, jnp.concatenate([top[:, HALF_M:].T, corner], axis=1)


def times_power(refit, high, low):
    rows = refit.shape[0]
    pair = jnp.concatenate(split(refit), axis=0)
    by_high = mm(pair, high, NN)
    return by_high[:rows] + (by_high[rows:] + mm(pair[:rows], low, NN))


def power_kernel(power_in, after_ref, high_out, low_out, power_out):
    power_out[...] = power_in[...]

    def step(number, carry):
        pair = split(power_out[...])
        high_out[place(number, M), :], low_out[place(number, M), :] = pair
        power_out[:HALF_M, :], power_out[HALF_M:, :] = squared(power_out[...], pair)
        return carry

    lax.fori_loop(0, high_out.shape[0] // M, step, 0)


def refit_kernel(
    early_hi, early_lo, late_hi, late_lo, power_in, factor_ref, scaled_hi, scaled_lo, own_ref, half_ref,
    value_out, both_ref, prior_ref,
):
    me, core, bit = bits()
    product = right_side(own_ref, core, bit, scaled_hi, scaled_lo, prior_ref)
    product = product + right_side(half_ref, 1 - core, bit, scaled_hi, scaled_lo, prior_ref)
    ridge, bound, weights = factor_ref[0:1, :1], factor_ref[1:2, :1], factor_ref[2:3, :]
    refit = (weights * product + ridge * prior_ref[...]) * (1.0 / bound)
    for high, low in ((early_hi, early_lo), (late_hi, late_lo)):
        for begin in range(0, high.shape[0], M):
            rows = slice(begin, begin + M)
            refit = 2.0 * refit - times_power(refit, high[rows, :], low[rows, :])
    both_ref[DH:, :] = power_in[...]
    both_ref[:DH, :] = refit
    above = DH + HALF_M

    def newton_step(number, carry):
        high, low = split(both_ref[...])
        power = (high[DH:], low[DH:])
        top = 2.0 * both_ref[:above, :] - mm3((high[:above], low[:above]), power, NN)
        corner = mm3((high[above:], low[above:]), (power[0][:, HALF_M:], power[1][:, HALF_M:]), NN)
        both_ref[above:, HALF_M:] = 2.0 * both_ref[above:, HALF_M:] - corner
        both_ref[above:, :HALF_M] = top[DH:, HALF_M:].T
        both_ref[:above, :] = top
        return carry

    lax.fori_loop(EARLY_STEPS + LATE_STEPS, NS_ITERS - 2, newton_step, 0)
    power = split(both_ref[DH:, :])
    refit = both_ref[:DH, :]
    refit = 2.0 * refit - times_power(refit, *power)
    once = times_power(refit, *power)
    refit = 2.0 * (refit - once) + times_power(once, *power)
    value_out[...] = refit.T


def shape(rows, columns, dtype):
    return jax.ShapeDtypeStruct((rows, columns), dtype)


def call(kernel, outs, arrays, scalars=0, scratch=(), in_specs=None, flops=None, limit=38):
    return pl.pallas_call(
        kernel,
        out_shape=tuple(outs),
        in_specs=in_specs
        or [pl.BlockSpec(memory_space=pltpu.SMEM)] * scalars
        + [pl.BlockSpec(memory_space=pltpu.VMEM)] * (len(arrays) - scalars),
        out_specs=tuple([pl.BlockSpec(memory_space=pltpu.VMEM)] * len(outs)),
        scratch_shapes=list(scratch),
        compiler_params=pltpu.CompilerParams(vmem_limit_bytes=int(limit * 1024 * 1024)),
        cost_estimate=None
        if flops is None
        else pl.CostEstimate(flops=flops, bytes_accessed=1024, transcendentals=0),
    )(*arrays)


def per_device(key_mant, scale_exp, values, queries, compact_index, shard_lengths):
    wide_count = lax.axis_size("wide")
    ctx = key_mant.shape[0]

    def exchanged(array, mask):
        return lax.ppermute(array, "wide", [(i, i ^ mask) for i in range(wide_count)])

    head_shape = shape(HEAD_ROWS, CHUNK, bf16)
    scale_shape = shape(CHUNKS, CHUNK, f32)
    half_sum = shape(PAIR_ROWS, 2 * CHUNK, bf16)
    pieces = (shape(PIECE_ROWS, CHUNK, bf16),) * 2

    send_head, head, send, keep = call(
        attention_kernel,
        (head_shape, head_shape, half_sum, half_sum),
        [
            pltpu.with_memory_space_constraint(array, pltpu.HBM)
            for array in (
                shard_lengths, scale_exp, compact_index.reshape(1, M), key_mant, values, queries
            )
        ],
        in_specs=[pl.BlockSpec(memory_space=pltpu.HBM)] * 6,
        flops=10**9,
        scratch=[
            pltpu.VMEM((2 * CHUNKS, CHUNK), f32),
            pltpu.SMEM(shard_lengths.shape, jnp.int32),
            pltpu.SMEM(scale_exp.shape, jnp.int32),
            pltpu.VMEM((1, M), jnp.int32),
            pltpu.VMEM((ctx, DH), bf16),
            pltpu.VMEM((ctx, DH), bf16),
            pltpu.VMEM((NQ, DH), bf16),
            pltpu.VMEM((ctx, DH), bf16),
            pltpu.VMEM((ctx, NQ), bf16),
            pltpu.SemaphoreType.DMA((6,)),
        ],
    )
    def both_exchanged(arrays, mask):
        return tuple(exchanged(array, mask) for array in arrays)

    def joined(*arrays):
        head, *scales = call(join_kernel, (head_shape, scale_shape, scale_shape), arrays)
        return head, tuple(scales)

    head, scales = joined(head, exchanged(send_head, 1))
    got_head = exchanged(head, 2)
    (send,) = call(copy_kernel, (half_sum,), (send, head))
    got = exchanged(send, 1)
    first, second, keep = call(
        halve_sum_kernel,
        pieces + (shape(PAIR_ROWS, CHUNK, bf16),),
        scales + (keep, got),
        flops=SUM_FLOPS,
    )
    sums, got = (keep,), both_exchanged((first, second), 2)
    mask = 4
    while mask < wide_count:
        head, scales = joined(head, got_head, first)
        got_head = exchanged(head, mask)
        last = 2 * mask >= wide_count
        sums = call(
            last_join_sum_kernel if last else join_sum_kernel,
            (shape(SUM_ROWS, CHUNK, bf16),) if last else pieces,
            (*scales, *sums, *got),
            flops=SUM_FLOPS,
        )
        first = sums[0]
        got = both_exchanged(sums, mask)
        mask *= 2
    keys, stats, *scales = call(
        last_join_kernel,
        (shape(HALF_M, DH, bf16), shape(2 * CHUNKS, CHUNK, f32), scale_shape, scale_shape),
        (head, got_head, first),
    )
    got_keys = exchanged(keys, 1)
    gram, linear, norm, scaled_hi, scaled_lo = call(
        feature_kernel,
        (shape(M, M, f32), shape(M, DH, f32), shape(8, DH, f32)) + (shape(M, NQ, bf16),) * 2,
        (shard_lengths, queries, stats, keys, got_keys),
        scalars=1,
        flops=1000000000,
        scratch=[pltpu.VMEM((M, DH), bf16), pltpu.VMEM((M, NQ), bf16), pltpu.VMEM((M, NQ), bf16)],
    )
    weights, factor, power = call(
        weight_kernel,
        (shape(1, M, f32), shape(8, M, f32), shape(M, M, f32)),
        (gram, linear, norm, scaled_hi, scaled_lo),
        flops=5 * 10**9,
        scratch=[pltpu.VMEM((M, M), f32)],
    )
    (outputs,) = call(
        outputs_kernel,
        (shape(SUM_ROWS, CHUNK, bf16),),
        (*scales, stats, *sums, *got, factor),
    )
    side = exchanged(outputs, 2)

    def powers(power, after, steps):
        pairs = (shape(steps * M, M, bf16),) * 2
        return call(power_kernel, pairs + (shape(M, M, f32),), (power, after), flops=steps * 10**9)

    early_hi, early_lo, power = powers(power, outputs, EARLY_STEPS)
    (half,) = call(
        forward_kernel,
        (shape(2 * SUM_ROWS, CHUNK, bf16),),
        (outputs, side, power),
    )
    other = exchanged(half, 1)
    late_hi, late_lo, power = powers(power, half, LATE_STEPS)
    (compact_values,) = call(
        refit_kernel,
        (shape(M, DH, f32),),
        (early_hi, early_lo, late_hi, late_lo, power, factor, scaled_hi, scaled_lo, half, other),
        scratch=[pltpu.VMEM((M + DH, M), f32), pltpu.VMEM((DH, M), f32)],
    )
    return weights.reshape(M), compact_values


def solution(mesh):
    placed = (
        P(("groups", "wide"), None),
        P(("groups", "wide")),
        P(("groups", "wide"), None),
        P("groups", None),
        P("groups"),
        P("groups"),
    )
    return jax.shard_map(
        per_device,
        mesh=mesh,
        in_specs=placed,
        out_specs=(P("groups"), P("groups", None)),
        check_vma=False,
    )
```
